32 devices in a mesh: seq: 4 (over z), dp: 8 (over y, x, core).
Axes of the slice: x: 2, y: 2, z: 4, core: 2. Of those that a mesh axis runs over, the one named last changes fastest.
Arguments:
- hidden_states: bfloat16 [8, 3072, 768], P('dp', 'seq'), may hold values from -6 to 6
- output_cotangent: bfloat16 [8, 3072, 768], P('dp', 'seq'), may hold values from -6 to 6
- document_lengths: int32 [8, 5], P('dp'), may hold values from 1 to 3068, as said below
- bucket_index: int32 [8, 24, 3072], P('dp', 'seq'), may hold values from 0 to 31
- norm_gains: float32 [2, 768], replicated, may hold values from 0.2 to 5.4
- bias_table: float32 [32, 12], replicated, may hold values from -4 to 4
- project_weight: float32 [768, 2304], P(('seq', 'dp')), may hold values from -0.21875 to 0.21875
- output_weight: float32 [768, 768], P(('seq', 'dp')), may hold values from -0.875 to 0.875
- expand_weight: float32 [768, 3072], P(('seq', 'dp')), may hold values from -0.21875 to 0.21875
- reduce_weight: float32 [3072, 768], P(('seq', 'dp')), may hold values from -0.109375 to 0.109375
- project_rows: float32 [768], P(('seq', 'dp')), may hold values from 0.1 to 3
- project_columns: float32 [2304], replicated, may hold values from 0.1 to 3
- output_rows: float32 [768], P(('seq', 'dp')), may hold values from 0.1 to 3
- output_columns: float32 [768], replicated, may hold values from 0.1 to 3
- expand_rows: float32 [768], P(('seq', 'dp')), may hold values from 0.1 to 3
- expand_columns: float32 [3072], replicated, may hold values from 0.1 to 3
- reduce_rows: float32 [3072], P(('seq', 'dp')), may hold values from 0.1 to 3
- reduce_columns: float32 [768], replicated, may hold values from 0.1 to 3
- gains_moment: float32 [2, 768], replicated, may hold values from 0.1 to 3
- table_moment: float32 [32, 12], replicated, may hold values from 0.1 to 3
Outputs:
- layer_output: bfloat16 [8, 3072, 768], P('dp', 'seq')
- input_gradient: bfloat16 [8, 3072, 768], P('dp', 'seq')
- gains_gradient: float32 [2, 768], replicated
- table_gradient: float32 [32, 12], replicated
- project_gradient: float32 [768, 2304], P(('seq', 'dp'))
- output_gradient: float32 [768, 768], P(('seq', 'dp'))
- expand_gradient: float32 [768, 3072], P(('seq', 'dp'))
- reduce_gradient: float32 [3072, 768], P(('seq', 'dp'))
- gains_updated: float32 [2, 768], replicated
- table_updated: float32 [32, 12], replicated
- project_updated: float32 [768, 2304], P(('seq', 'dp'))
- output_updated: float32 [768, 768], P(('seq', 'dp'))
- expand_updated: float32 [768, 3072], P(('seq', 'dp'))
- reduce_updated: float32 [3072, 768], P(('seq', 'dp'))
- project_rows_new: float32 [768], P(('seq', 'dp'))
- project_columns_new: float32 [2304], replicated
- output_rows_new: float32 [768], P(('seq', 'dp'))
- output_columns_new: float32 [768], replicated
- expand_rows_new: float32 [768], P(('seq', 'dp'))
- expand_columns_new: float32 [3072], replicated
- reduce_rows_new: float32 [3072], P(('seq', 'dp'))
- reduce_columns_new: float32 [768], replicated
- gains_moment_new: float32 [2, 768], replicated
- table_moment_new: float32 [32, 12], replicated
The draws below stay inside these ranges and needn't reach their ends.
Inputs may be any that keep to these rules, and one draw needn't show every extreme that they name: `document_lengths`: each row's 5 lengths sum to 3072.
All inputs are finite; a program needn't handle non-finite values.
Results may differ from the reference program's by a relative error of at most 0.018.
The reference program's roundings to bfloat16 on the way count: a program that leaves them out, or rounds other values in their place, can miss the bound.
Values may be sent and summed in bfloat16 or wider, within the bound.
A program may use at most 192 MiB of HBM per device.

```python
import math
import jax
import jax.numpy as jnp
from jax import lax

D = 768
HEADS = 12
HEAD = 64
FF = 3072
NBUCK = 32
BLK = 128
TOK_DEV = 768
ROW_LEN = 3072
ROWS = 8
TOKENS = 24576


def draw_document_lengths(key, part):
    key = jax.random.fold_in(key, 11)
    key_parts = jax.random.split(key, 4)
    leading = jax.random.randint(key_parts[0], (ROWS,), 2, TOK_DEV).at[0].set(2)
    trailing = jax.random.randint(key_parts[1], (ROWS,), 2, TOK_DEV).at[0].set(2)
    first_doc = jax.random.randint(key_parts[2], (ROWS,), 1, leading)
    last_doc = jax.random.randint(key_parts[3], (ROWS,), 1, trailing)
    middle_doc = ROW_LEN - leading - trailing
    return jnp.stack([first_doc, leading - first_doc, middle_doc, last_doc, trailing - last_doc], axis=1).astype(jnp.int32)


def draw_norm_gains(key, part):
    key = jax.random.fold_in(key, 23)
    ramp = jnp.arange(D, dtype=jnp.float32) / (D - 1)
    noise = jax.random.uniform(key, (2, D), jnp.float32, 0.7, 1.3)
    return 0.6 * jnp.exp(ramp * math.log(3.0)) * noise


def touch_ends(entries, stream_key, least, high):
    shape = entries.shape
    spot = [jax.random.randint(jax.random.fold_in(stream_key, axis), (), 0, shape[axis]) for axis in range(len(shape))]
    entries = entries.at[tuple(spot)].set(least)
    longest = shape.index(max(shape))
    spot[longest] = (spot[longest] + 1) % shape[longest]
    return entries.at[tuple(spot)].set(high)


def block_scale(key, extent, cuts, smallest, top_value):
    gain, own = 1.0, jax.random.fold_in(key, 6)
    for axis_at, blocks in cuts:
        steps = jnp.exp(jax.random.uniform(jax.random.fold_in(own, axis_at), (blocks,), jnp.float32, smallest / len(cuts), top_value / len(cuts)))
        gain = gain * jnp.repeat(steps, extent[axis_at] // blocks).reshape([-1 if axis == axis_at else 1 for axis in range(len(extent))])
    return gain


def gaussian(rng, dims, spread, most, cuts=(), kind=jnp.bfloat16):
    values = jax.random.normal(rng, dims, jnp.float32) * spread
    if len(cuts) > 0:
        values = block_scale(rng, dims, cuts, -0.22, 0.18) * values
    return jnp.clip(values, min=-most, max=most).astype(kind)


def setup_inputs(seed: int = 0) -> dict:
    seeds = jax.random.split(jax.random.key(seed), 21)
    hidden_states = gaussian(seeds[0], (ROWS, ROW_LEN, D), 1.0, 6.0, ((0, 8), (1, 4)))
    output_cotangent = gaussian(seeds[1], (ROWS, ROW_LEN, D), 1.0, 6.0, ((0, 8), (1, 4)))
    document_lengths = draw_document_lengths(jax.random.fold_in(seeds[20], 71), 0)
    bucket_index = touch_ends(jax.random.randint(seeds[3], (ROWS, ROW_LEN // BLK, ROW_LEN), 0, NBUCK), jax.random.fold_in(seeds[3], 1), 0, NBUCK - 1).astype(jnp.int32)
    norm_gains = draw_norm_gains(jax.random.fold_in(seeds[20], 71), 0)
    bias_table = gaussian(seeds[5], (NBUCK, HEADS), 1.0, 4.0, (), jnp.float32)
    project_weight = gaussian(seeds[6], (D, 3 * D), D ** -0.5, 0.21875, ((0, 32),), jnp.float32)
    output_weight = gaussian(seeds[7], (D, D), (D // 16) ** -0.5, 0.875, ((0, 32),), jnp.float32)
    expand_weight = gaussian(seeds[8], (D, FF), D ** -0.5, 0.21875, ((0, 32),), jnp.float32)
    reduce_weight = gaussian(seeds[9], (FF, D), FF ** -0.5, 0.109375, ((0, 32),), jnp.float32)
    project_rows = jnp.clip(jnp.exp(math.log(3.0) - 3.4011974 * jax.random.uniform(seeds[10], (D,), jnp.float32) ** block_scale(seeds[10], (D,), ((0, 32),), -0.2, 0.2)), 0.1, 3.0)
    project_columns = jnp.clip(jnp.exp(jax.random.uniform(seeds[11], (3 * D,), jnp.float32, math.log(0.1), math.log(3.0))), 0.1, 3.0)
    output_rows = jnp.clip(jnp.exp(math.log(3.0) - 3.4011974 * jax.random.uniform(seeds[12], (D,), jnp.float32) ** block_scale(seeds[12], (D,), ((0, 32),), -0.2, 0.2)), 0.1, 3.0)
    output_columns = jnp.clip(jnp.exp(jax.random.uniform(seeds[13], (D,), jnp.float32, math.log(0.1), math.log(3.0))), 0.1, 3.0)
    expand_rows = jnp.clip(jnp.exp(math.log(3.0) - 3.4011974 * jax.random.uniform(seeds[14], (D,), jnp.float32) ** block_scale(seeds[14], (D,), ((0, 32),), -0.2, 0.2)), 0.1, 3.0)
    expand_columns = jnp.clip(jnp.exp(jax.random.uniform(seeds[15], (FF,), jnp.float32, math.log(0.1), math.log(3.0))), 0.1, 3.0)
    reduce_rows = jnp.clip(jnp.exp(math.log(3.0) - 3.4011974 * jax.random.uniform(seeds[16], (FF,), jnp.float32) ** block_scale(seeds[16], (FF,), ((0, 32),), -0.2, 0.2)), 0.1, 3.0)
    reduce_columns = jnp.clip(jnp.exp(jax.random.uniform(seeds[17], (D,), jnp.float32, math.log(0.1), math.log(3.0))), 0.1, 3.0)
    gains_moment = jnp.clip(jnp.exp(jax.random.uniform(seeds[18], (2, D), jnp.float32, math.log(0.1), math.log(3.0))), 0.1, 3.0)
    table_moment = jnp.clip(jnp.exp(jax.random.uniform(seeds[19], (NBUCK, HEADS), jnp.float32, math.log(0.1), math.log(3.0))), 0.1, 3.0)
    return {"hidden_states": hidden_states, "output_cotangent": output_cotangent, "document_lengths": document_lengths, "bucket_index": bucket_index, "norm_gains": norm_gains, "bias_table": bias_table, "project_weight": project_weight, "output_weight": output_weight, "expand_weight": expand_weight, "reduce_weight": reduce_weight, "project_rows": project_rows, "project_columns": project_columns, "output_rows": output_rows, "output_columns": output_columns, "expand_rows": expand_rows, "expand_columns": expand_columns, "reduce_rows": reduce_rows, "reduce_columns": reduce_columns, "gains_moment": gains_moment, "table_moment": table_moment}


@jax.custom_vjp
def low(v):
    return lax.optimization_barrier(v.astype(jnp.bfloat16)).astype(jnp.float32)

@jax.custom_vjp
def low_back(v):
    return v

def low_keep(v):
    return (low(v), None)

def low_pass(kept, grad):
    return (grad,)

def back_keep(v):
    return (v, None)

def back_low(kept, grad):
    return (low(grad),)
low.defvjp(low_keep, low_pass)
low_back.defvjp(back_keep, back_low)
score_scale = 0.125
masked_score = -1e+30
norm_epsilon = 1e-06
tiny_term = 1e-30
learn_rate = 0.3
decay_rate = 1.0 - 2.0 ** (-0.8)
highest = lax.Precision.HIGHEST

def product(former, latter):
    return jnp.dot(former, latter, precision=highest, preferred_element_type=jnp.float32)

def rms_norm(values, gain_vector):
    return values * lax.rsqrt(lax.optimization_barrier(jnp.mean(values * values, axis=-1, keepdims=True)) + norm_epsilon) * gain_vector

def gelu_tanh(values):
    return 0.5 * values * (1.0 + jnp.tanh(0.7978845608028654 * (values + 0.044715 * values * values * values)))

def documents(lengths, row_length):
    doc_ends = jnp.cumsum(lengths)
    position = jnp.arange(row_length, dtype=jnp.int32)
    return lax.optimization_barrier(jnp.sum((position[:, None] >= doc_ends[None, :]).astype(jnp.int32), axis=1)).astype(jnp.int32)

def row_forward(inputs, norm_gains, bias_table, project_weight, output_weight, expand_weight, reduce_weight, doc_row, bucket_row):
    row_length = inputs.shape[0]
    normed_one = low(rms_norm(inputs, norm_gains[0]))
    projected = low(low_back(product(normed_one, low(project_weight))))
    queries = projected[:, :D].reshape(row_length, HEADS, HEAD)
    key_rows = projected[:, D:2 * D].reshape(row_length, HEADS, HEAD)
    value_rows = projected[:, 2 * D:].reshape(row_length, HEADS, HEAD)
    block_size = math.gcd(512, row_length)
    block_count = row_length // block_size
    query_blocks = queries.reshape(block_count, block_size, HEADS, HEAD)
    bucket_blocks = bucket_row.reshape(block_count, block_size // BLK, row_length)
    doc_blocks = doc_row.reshape(block_count, block_size)

    def attend(block_parts):
        query_block, bucket_block, doc_block = block_parts
        raw_scores = low_back(jnp.einsum('qhe,khe->hqk', query_block, key_rows, precision=highest))
        picked = jnp.transpose(bias_table[bucket_block], (2, 0, 1))
        bias_block = jnp.repeat(picked, BLK, axis=1)
        scores = raw_scores * score_scale + bias_block
        same_doc = doc_block[:, None] == doc_row[None, :]
        scores = jnp.where(same_doc[None], scores, masked_score)
        top_score = lax.optimization_barrier(jnp.max(scores, axis=-1, keepdims=True))
        unscaled = jnp.exp(scores - top_score)
        attention = low(unscaled / lax.optimization_barrier(jnp.sum(unscaled, axis=-1, keepdims=True)))
        return jnp.einsum('hqk,khe->qhe', attention, value_rows, precision=highest)
    context = lax.map(jax.checkpoint(attend), (query_blocks, bucket_blocks, doc_blocks))
    context = low(low_back(context.reshape(row_length, D)))
    residual = inputs + low_back(product(context, low(output_weight)))
    normed_two = low(rms_norm(residual, norm_gains[1]))
    expanded = low_back(product(normed_two, low(expand_weight)))
    activated = low(gelu_tanh(expanded))
    return residual + low_back(product(activated, low(reduce_weight)))

def factored(weight, gradient, row_previous, column_previous):
    squares = gradient * gradient + tiny_term
    row_stat = decay_rate * row_previous + (1.0 - decay_rate) * lax.optimization_barrier(jnp.mean(squares, axis=1))
    column_stat = decay_rate * column_previous + (1.0 - decay_rate) * lax.optimization_barrier(jnp.mean(squares, axis=0))
    denominator = row_stat[:, None] * column_stat[None, :] / jnp.mean(row_stat)
    return (weight - learn_rate * gradient * lax.rsqrt(denominator), row_stat, column_stat)

def unfactored(weight, gradient, previous):
    moment = decay_rate * previous + (1.0 - decay_rate) * (gradient * gradient + tiny_term)
    return (weight - learn_rate * gradient * lax.rsqrt(moment), moment)

def reference(hidden_states, output_cotangent, document_lengths, bucket_index, norm_gains, bias_table, project_weight, output_weight, expand_weight, reduce_weight, project_rows, project_columns, output_rows, output_columns, expand_rows, expand_columns, reduce_rows, reduce_columns, gains_moment, table_moment):
    parameters = (norm_gains, bias_table, project_weight, output_weight, expand_weight, reduce_weight)
    row_length = hidden_states.shape[1]

    def one_row(totals, row_parts):
        input_row, cotangent_row, length_row, bucket_row = row_parts
        doc_row = documents(length_row, row_length)

        def forward(inputs, gains_value, table_value, project_value, output_value, expand_value, reduce_value):
            return row_forward(inputs, gains_value, table_value, project_value, output_value, expand_value, reduce_value, doc_row, bucket_row)
        outputs, pullback = jax.vjp(forward, input_row.astype(jnp.float32), *parameters)
        gradient_parts = pullback(cotangent_row.astype(jnp.float32))
        totals = tuple((total_part + new_part for total_part, new_part in zip(totals, gradient_parts[1:])))
        return (totals, (outputs.astype(jnp.bfloat16), gradient_parts[0].astype(jnp.bfloat16)))
    zero_sums = tuple((jnp.zeros(parameter.shape, jnp.float32) for parameter in parameters))
    totals, (layer_output, input_gradient) = lax.scan(one_row, zero_sums, (hidden_states, output_cotangent, document_lengths, bucket_index))
    gradient_scale = 1.0 / math.sqrt(TOKENS)
    gains_gradient, table_gradient, project_gradient, output_gradient, expand_gradient, reduce_gradient = tuple((total_part * gradient_scale for total_part in totals))
    project_updated, project_rows_new, project_columns_new = factored(project_weight, project_gradient, project_rows, project_columns)
    output_updated, output_rows_new, output_columns_new = factored(output_weight, output_gradient, output_rows, output_columns)
    expand_updated, expand_rows_new, expand_columns_new = factored(expand_weight, expand_gradient, expand_rows, expand_columns)
    reduce_updated, reduce_rows_new, reduce_columns_new = factored(reduce_weight, reduce_gradient, reduce_rows, reduce_columns)
    gains_updated, gains_moment_new = unfactored(norm_gains, gains_gradient, gains_moment)
    table_updated, table_moment_new = unfactored(bias_table, table_gradient, table_moment)
    return (layer_output, input_gradient, gains_gradient, table_gradient, project_gradient, output_gradient, expand_gradient, reduce_gradient, gains_updated, table_updated, project_updated, output_updated, expand_updated, reduce_updated, project_rows_new, project_columns_new, output_rows_new, output_columns_new, expand_rows_new, expand_columns_new, reduce_rows_new, reduce_columns_new, gains_moment_new, table_moment_new)
```

```python
import math

import jax
import jax.numpy as jnp
from jax import lax
from jax.experimental import pallas as pl
from jax.experimental.pallas import tpu as pltpu
from jax.sharding import PartitionSpec as P

D = 768
HEADS = 12
HEAD = 64
BLK = 128
PAIR = 2 * HEAD
PAIRS = HEADS // 2
DOCS = 5
TERMS = 3

score_scale = 0.125
masked_score = -1e30
norm_epsilon = 1e-06
tiny_term = 1e-30
learn_rate = 0.3
decay_rate = 1.0 - 2.0 ** (-0.8)
back_step = 768
vmem_bytes = 56 * 2**20

low_type = jnp.bfloat16
f32 = jnp.float32


def dot(former, latter, former_axis, latter_axis):
    return lax.dot_general(
        former,
        latter,
        (((former_axis,), (latter_axis,)), ((), ())),
        preferred_element_type=f32,
    )


def rms_norm(values, gain_vector):
    return (
        values
        * lax.rsqrt(jnp.mean(values * values, axis=-1, keepdims=True) + norm_epsilon)
        * gain_vector
    )


def gelu_tanh(values):
    return (
        0.5
        * values
        * (1.0 + jnp.tanh(0.7978845608028654 * (values + 0.044715 * values * values * values)))
    )


def documents(lengths, row_length):
    doc_ends = jnp.cumsum(lengths)
    position = jnp.arange(row_length, dtype=jnp.int32)
    return jnp.sum((position[:, None] >= doc_ends[None, :]).astype(jnp.int32), axis=1)


def split_terms(values):
    terms = []
    rest = values
    for _ in range(TERMS):
        term = lax.reduce_precision(rest, 8, 7)
        terms.append(term)
        rest = rest - term
    return terms


def extra_columns(blocks):
    return TERMS * blocks, TERMS * blocks + DOCS


def query_extra(doc_query, blocks):
    count = doc_query.shape[0]
    doc_start, one_start = extra_columns(blocks)
    lane = lax.broadcasted_iota(jnp.int32, (count, 128), 1)
    block = lax.broadcasted_iota(jnp.int32, (count, 128), 0) // BLK
    is_block = (lane < doc_start) & (lane % blocks == block)
    is_doc = (lane >= doc_start) & (lane < one_start) & (lane - doc_start == doc_query[:, None])
    return (is_block | is_doc).astype(low_type)


def with_row_terms(extra, values, blocks):
    _, one_start = extra_columns(blocks)
    lane = lax.broadcasted_iota(jnp.int32, (1, 1, 128), 2)
    result = jnp.broadcast_to(extra.astype(f32)[None], (HEADS,) + extra.shape)
    for place, term in enumerate(split_terms(values)):
        result = jnp.where(lane == one_start + place, term[:, :, None], result)
    return result.astype(low_type)


def key_picks(bucket_rows, doc_all, buckets):
    blocks, row_length = bucket_rows.shape
    one_hot = (
        bucket_rows.T[:, :, None] == jnp.arange(buckets, dtype=jnp.int32)[None, None, :]
    ).reshape(row_length, blocks * buckets)
    other_doc = doc_all[:, None] != jnp.arange(DOCS, dtype=jnp.int32)[None, :]
    ones = jnp.ones((row_length, 1), jnp.bool_)
    return jnp.concatenate([one_hot, other_doc, ones], axis=1).astype(low_type)


def key_extra(picks, bias_table, blocks):
    buckets = bias_table.shape[0]
    doc_start, one_start = extra_columns(blocks)
    terms = jnp.stack(split_terms(bias_table), axis=0)
    lane = jnp.arange(128, dtype=jnp.int32)
    place = jnp.clip(lane // blocks, 0, TERMS - 1)
    spread = jnp.transpose(terms[place], (1, 2, 0))
    at_block = (lane[None, :] % blocks == jnp.arange(blocks, dtype=jnp.int32)[:, None]) & (
        lane[None, :] < doc_start
    )
    bias_part = jnp.where(at_block[:, None, None, :], spread[None], 0.0).reshape(
        blocks * buckets, HEADS, 128
    )
    doc_part = jnp.where(
        lane[None, :] - doc_start == jnp.arange(DOCS, dtype=jnp.int32)[:, None], masked_score, 0.0
    )
    one_part = ((lane >= one_start) & (lane < one_start + TERMS)).astype(f32)[None]
    rest = jnp.concatenate([doc_part, one_part], axis=0)
    rest = jnp.broadcast_to(rest[:, None, :], (DOCS + 1, HEADS, 128))
    whole = jnp.concatenate([bias_part, rest], axis=0).reshape(-1, HEADS * 128).astype(low_type)
    return dot(picks, whole, 1, 0).astype(low_type)


def forward_kernel(queries, extra, keys, values_t, keys_extra, context_t, log_total):
    count = queries.shape[0]
    lane = lax.broadcasted_iota(jnp.int32, (count, PAIR), 1)
    query_pair = queries[...]
    for head in range(2):
        mine = (lane < HEAD) if head == 0 else (lane >= HEAD)
        query_side = jnp.concatenate(
            [jnp.where(mine, query_pair, jnp.zeros_like(query_pair)), extra[...]], axis=1
        )
        key_side = jnp.concatenate([keys[...], keys_extra[:, 128 * head : 128 * head + 128]], axis=1)
        scores = dot(key_side, query_side, 1, 1)
        top = jnp.max(scores, axis=0, keepdims=True)
        unscaled = jnp.exp(scores - top).astype(low_type)
        value_side = jnp.concatenate(
            [
                values_t[HEAD * head : HEAD * head + HEAD, :],
                jnp.ones((16, unscaled.shape[0]), low_type),
            ],
            axis=0,
        )
        weighted = dot(value_side, unscaled, 1, 0)
        total = weighted[HEAD : HEAD + 1]
        context_t[pl.ds(HEAD * head, HEAD), :] = weighted[:HEAD] / total
        log_total[pl.ds(8 * head, 8), :] = jnp.broadcast_to(top + jnp.log(total), (8, count))


def attend(queries, extra, keys, values_t, keys_extra):
    count, row_length = queries.shape[0], keys.shape[0]
    return pl.pallas_call(
        forward_kernel,
        grid=(PAIRS,),
        out_shape=[
            jax.ShapeDtypeStruct((D, count), f32),
            jax.ShapeDtypeStruct((HEADS * 8, count), f32),
        ],
        in_specs=[
            pl.BlockSpec((count, PAIR), lambda pair: (0, pair)),
            pl.BlockSpec((count, 128), lambda pair: (0, 0)),
            pl.BlockSpec((row_length, PAIR), lambda pair: (0, pair)),
            pl.BlockSpec((PAIR, row_length), lambda pair: (pair, 0)),
            pl.BlockSpec((row_length, 256), lambda pair: (0, pair)),
        ],
        out_specs=[
            pl.BlockSpec((PAIR, count), lambda pair: (pair, 0)),
            pl.BlockSpec((16, count), lambda pair: (pair, 0)),
        ],
        compiler_params=pltpu.CompilerParams(vmem_limit_bytes=vmem_bytes),
        cost_estimate=pl.CostEstimate(
            flops=4 * HEADS * count * row_length * 256,
            bytes_accessed=HEADS * row_length * 1024,
            transcendentals=HEADS * count * row_length,
        ),
        name="attention_forward",
    )(queries, extra, keys, values_t, keys_extra)


def backward_kernel(
    queries,
    query_rows,
    delta_rows,
    context_grad,
    queries_t,
    context_grad_t,
    keys,
    values_t,
    keys_extra,
    query_grad,
    key_grad_t,
    value_grad_t,
    folded,
):
    step = pl.program_id(1)
    count, amount = queries.shape[0], keys.shape[0]
    lane = lax.broadcasted_iota(jnp.int32, (count, PAIR), 1)
    query_pair, grad_pair = queries[...], context_grad[...]
    zeros = jnp.zeros_like(query_pair)

    @pl.when(step == 0)
    def _():
        query_grad[...] = jnp.zeros_like(query_grad)

    query_grads = []
    for head in range(2):
        mine = (lane < HEAD) if head == 0 else (lane >= HEAD)
        rows = pl.ds(HEAD * head, HEAD)
        more = keys_extra[:, 128 * head : 128 * head + 128]
        query_side = jnp.concatenate([jnp.where(mine, query_pair, zeros), query_rows[head]], axis=1)
        grad_side = jnp.concatenate([jnp.where(mine, grad_pair, zeros), delta_rows[head]], axis=1)
        key_side = jnp.concatenate([keys[...], more], axis=1)
        value_side = jnp.concatenate(
            [values_t[...], jnp.ones((128, amount), low_type)], axis=0
        )
        attention = jnp.exp(dot(query_side, key_side, 1, 1))
        score_grad = attention * dot(grad_side, value_side, 1, 0)
        attention_low = attention.astype(low_type)
        score_low = score_grad.astype(low_type)
        for block in range(count // BLK):
            folded[head, pl.ds(block, 1), :] = jnp.sum(
                score_grad[BLK * block : BLK * block + BLK], axis=0, keepdims=True
            )
        query_grads.append(dot(score_low, keys[...], 1, 0))
        value_grad_t[rows, :] = dot(context_grad_t[rows, :], attention_low, 1, 0).astype(low_type)
        key_grad_t[rows, :] = dot(queries_t[rows, :], score_low, 1, 0).astype(low_type)
    query_grad[...] += jnp.where(lane < HEAD, query_grads[0], query_grads[1])


def attend_back(
    queries, query_rows, delta_rows, context_grad, queries_t, context_grad_t, keys, values_t, keys_extra
):
    count, row_length = queries.shape[0], keys.shape[0]
    blocks = count // BLK
    of_pair = pl.BlockSpec((count, PAIR), lambda pair, step: (0, pair))
    of_pair_t = pl.BlockSpec((PAIR, count), lambda pair, step: (pair, 0))
    of_heads = pl.BlockSpec((2, count, 128), lambda pair, step: (pair, 0, 0))
    key_t = pl.BlockSpec((PAIR, back_step), lambda pair, step: (pair, step))
    return pl.pallas_call(
        backward_kernel,
        grid=(PAIRS, row_length // back_step),
        out_shape=[
            jax.ShapeDtypeStruct((count, D), f32),
            jax.ShapeDtypeStruct((D, row_length), low_type),
            jax.ShapeDtypeStruct((D, row_length), low_type),
            jax.ShapeDtypeStruct((HEADS, blocks, row_length), f32),
        ],
        in_specs=[
            of_pair,
            of_heads,
            of_heads,
            of_pair,
            of_pair_t,
            of_pair_t,
            pl.BlockSpec((back_step, PAIR), lambda pair, step: (step, pair)),
            key_t,
            pl.BlockSpec((back_step, 256), lambda pair, step: (step, pair)),
        ],
        out_specs=[
            of_pair,
            key_t,
            key_t,
            pl.BlockSpec((2, blocks, back_step), lambda pair, step: (pair, 0, step)),
        ],
        compiler_params=pltpu.CompilerParams(vmem_limit_bytes=vmem_bytes),
        cost_estimate=pl.CostEstimate(
            flops=10 * HEADS * count * row_length * 200,
            bytes_accessed=HEADS * row_length * 2048,
            transcendentals=HEADS * count * row_length,
        ),
        name="attention_backward",
    )(
        queries,
        query_rows,
        delta_rows,
        context_grad,
        queries_t,
        context_grad_t,
        keys,
        values_t,
        keys_extra,
    )


def body(
    hidden_states,
    output_cotangent,
    document_lengths,
    bucket_index,
    norm_gains,
    bias_table,
    project_weight,
    output_weight,
    expand_weight,
    reduce_weight,
    project_rows,
    project_columns,
    output_rows,
    output_columns,
    expand_rows,
    expand_columns,
    reduce_rows,
    reduce_columns,
    gains_moment,
    table_moment,
):
    every = ("seq", "dp")
    local_rows = hidden_states.shape[1]
    row_length = local_rows * lax.axis_size("seq")
    gradient_scale = 1.0 / math.sqrt(row_length * lax.axis_size("dp"))
    place = lax.axis_index("seq")
    blocks = local_rows // BLK

    project_full = lax.all_gather(project_weight.astype(low_type), every, axis=0, tiled=True)
    row_states = lax.all_gather(hidden_states[0], "seq", axis=0, tiled=True)
    mixed = jnp.concatenate([output_weight, expand_weight], axis=1).astype(low_type)
    mixed_full = lax.all_gather(mixed, every, axis=0, tiled=True)
    reduce_full = lax.all_gather(reduce_weight.astype(low_type), every, axis=0, tiled=True)
    output_full, expand_full = mixed_full[:, :D], mixed_full[:, D:]

    doc_all = documents(document_lengths[0], row_length)
    doc_query = lax.dynamic_slice_in_dim(doc_all, place * local_rows, local_rows)
    picks = key_picks(bucket_index[0], doc_all, bias_table.shape[0])
    keys_extra = key_extra(picks, bias_table, blocks)
    extra = query_extra(doc_query, blocks)

    inputs = hidden_states[0].astype(f32)
    normed_one, pullback_one = jax.vjp(rms_norm, inputs, norm_gains[0])
    normed_low = normed_one.astype(low_type)
    normed_all = rms_norm(row_states.astype(f32), norm_gains[0]).astype(low_type)
    query_weight, key_weight, value_weight = (
        project_full[:, :D],
        project_full[:, D : 2 * D],
        project_full[:, 2 * D :],
    )
    queries = (dot(normed_low, query_weight, 1, 0).astype(low_type).astype(f32) * score_scale).astype(
        low_type
    )
    queries_t = (
        dot(query_weight, normed_low, 0, 1).astype(low_type).astype(f32) * score_scale
    ).astype(low_type)
    keys = dot(normed_all, key_weight, 1, 0).astype(low_type)
    values_t = dot(value_weight, normed_all, 0, 1).astype(low_type)

    context_t, log_total = attend(queries, extra, keys, values_t, keys_extra)
    log_total = log_total.reshape(HEADS, 8, local_rows)[:, 0]
    context_low_t = context_t.astype(low_type)
    residual = inputs + dot(context_low_t, output_full, 0, 0)
    normed_two, pullback_two = jax.vjp(rms_norm, residual, norm_gains[1])
    normed_two_low = normed_two.astype(low_type)
    expanded = dot(normed_two_low, expand_full, 1, 0)
    activated, pullback_gelu = jax.vjp(gelu_tanh, expanded)
    activated_low = activated.astype(low_type)
    layer_output = (residual + dot(activated_low, reduce_full, 1, 0)).astype(low_type)[None]

    upstream_low = output_cotangent[0].astype(low_type)
    upstream = upstream_low.astype(f32)
    reduce_term = dot(activated_low, upstream_low, 0, 0)
    (expanded_grad,) = pullback_gelu(dot(upstream_low, reduce_full, 1, 1))
    expanded_low = expanded_grad.astype(low_type)
    expand_term = dot(normed_two_low, expanded_low, 0, 0)
    residual_part, gain_two_grad = pullback_two(dot(expanded_low, expand_full, 1, 1))
    residual_grad = upstream + residual_part
    residual_low = residual_grad.astype(low_type)
    output_term = dot(context_low_t, residual_low, 1, 0)
    context_grad = dot(residual_low, output_full, 1, 1).astype(low_type)
    context_grad_t = dot(output_full, residual_low, 1, 1).astype(low_type)
    delta = jnp.sum(
        (context_grad_t.astype(f32) * context_t).reshape(HEADS, HEAD, local_rows), axis=1
    )

    query_grad, key_grad_t, value_grad_t, folded = attend_back(
        queries,
        with_row_terms(extra, -log_total, blocks),
        with_row_terms(jnp.zeros_like(extra), -delta, blocks),
        context_grad,
        queries_t,
        context_grad_t,
        keys,
        values_t,
        keys_extra,
    )
    buckets = bias_table.shape[0]
    picked = jnp.dot(
        folded.reshape(HEADS * blocks, row_length),
        picks[:, : blocks * buckets].astype(f32),
        precision=lax.Precision.HIGHEST,
    )
    table_grad = jnp.einsum("hkkb->bh", picked.reshape(HEADS, blocks, blocks, buckets))

    query_grad_low = (query_grad * score_scale).astype(low_type)
    project_term = jnp.concatenate(
        [
            dot(normed_low, query_grad_low, 0, 0),
            dot(normed_all, key_grad_t, 0, 1),
            dot(normed_all, value_grad_t, 0, 1),
        ],
        axis=1,
    )
    key_part = dot(key_grad_t, key_weight, 0, 1) + dot(value_grad_t, value_weight, 0, 1)
    key_part = lax.psum_scatter(
        key_part.astype(low_type), "seq", scatter_dimension=0, tiled=True
    ).astype(f32)
    input_part, gain_one_grad = pullback_one(dot(query_grad_low, query_weight, 1, 1) + key_part)
    input_gradient = (residual_grad + input_part).astype(low_type)[None]

    mixed_term = jnp.concatenate([output_term, expand_term], axis=1).astype(low_type)
    scatter = lambda term: lax.psum_scatter(
        term.astype(low_type), every, scatter_dimension=0, tiled=True
    ).astype(f32)
    mixed_share = scatter(mixed_term)
    reduce_share = scatter(reduce_term)
    project_share = scatter(project_term)
    shares = (project_share, mixed_share[:, :D], mixed_share[:, D:], reduce_share)

    gradients = tuple((share * gradient_scale for share in shares))
    row_before = (project_rows, output_rows, expand_rows, reduce_rows)
    row_after = []
    column_parts = []
    row_sums = []
    for gradient, previous in zip(gradients, row_before):
        squares = gradient * gradient + tiny_term
        updated_rows = decay_rate * previous + (1.0 - decay_rate) * jnp.mean(squares, axis=1)
        row_after.append(updated_rows)
        column_parts.append(jnp.sum(squares, axis=0))
        row_sums.append(jnp.sum(updated_rows))
    summed = lax.psum(
        (
            column_parts[0],
            column_parts[1],
            column_parts[2],
            column_parts[3],
            jnp.stack(row_sums),
            jnp.stack([gain_one_grad, gain_two_grad]),
            table_grad,
        ),
        every,
    )
    column_before = (project_columns, output_columns, expand_columns, reduce_columns)
    weights_before = (project_weight, output_weight, expand_weight, reduce_weight)
    full_rows = (
        project_full.shape[0],
        output_full.shape[0],
        expand_full.shape[0],
        reduce_full.shape[0],
    )
    updated_weights = []
    columns_after = []
    for position in range(4):
        columns_new = decay_rate * column_before[position] + (1.0 - decay_rate) * (
            summed[position] / full_rows[position]
        )
        row_mean = summed[4][position] / full_rows[position]
        denominator = row_after[position][:, None] * columns_new[None, :] / row_mean
        updated_weights.append(
            weights_before[position] - learn_rate * gradients[position] * lax.rsqrt(denominator)
        )
        columns_after.append(columns_new)
    gains_gradient = summed[5] * gradient_scale
    table_gradient = summed[6] * gradient_scale
    gains_moment_new = decay_rate * gains_moment + (1.0 - decay_rate) * (
        gains_gradient * gains_gradient + tiny_term
    )
    gains_updated = norm_gains - learn_rate * gains_gradient * lax.rsqrt(gains_moment_new)
    table_moment_new = decay_rate * table_moment + (1.0 - decay_rate) * (
        table_gradient * table_gradient + tiny_term
    )
    table_updated = bias_table - learn_rate * table_gradient * lax.rsqrt(table_moment_new)
    return (
        layer_output,
        input_gradient,
        gains_gradient,
        table_gradient,
        gradients[0],
        gradients[1],
        gradients[2],
        gradients[3],
        gains_updated,
        table_updated,
        updated_weights[0],
        updated_weights[1],
        updated_weights[2],
        updated_weights[3],
        row_after[0],
        columns_after[0],
        row_after[1],
        columns_after[1],
        row_after[2],
        columns_after[2],
        row_after[3],
        columns_after[3],
        gains_moment_new,
        table_moment_new,
    )


def solution(mesh):
    placed = (
        P("dp", "seq", None),
        P("dp", "seq", None),
        P("dp", None),
        P("dp", "seq", None),
        P(),
        P(),
        P(("seq", "dp"), None),
        P(("seq", "dp"), None),
        P(("seq", "dp"), None),
        P(("seq", "dp"), None),
        P(("seq", "dp")),
        P(),
        P(("seq", "dp")),
        P(),
        P(("seq", "dp")),
        P(),
        P(("seq", "dp")),
        P(),
        P(),
        P(),
    )
    return jax.shard_map(
        body,
        mesh=mesh,
        in_specs=placed,
        out_specs=(
            P("dp", "seq", None),
            P("dp", "seq", None),
            P(),
            P(),
            P(("seq", "dp"), None),
            P(("seq", "dp"), None),
            P(("seq", "dp"), None),
            P(("seq", "dp"), None),
            P(),
            P(),
            P(("seq", "dp"), None),
            P(("seq", "dp"), None),
            P(("seq", "dp"), None),
            P(("seq", "dp"), None),
            P(("seq", "dp")),
            P(),
            P(("seq", "dp")),
            P(),
            P(("seq", "dp")),
            P(),
            P(("seq", "dp")),
            P(),
            P(),
            P(),
        ),
        check_vma=False,
    )
```

```python
import functools
import math

import jax
import jax.numpy as jnp
from jax import lax
from jax.experimental import pallas as pl
from jax.experimental.pallas import tpu as pltpu
from jax.sharding import PartitionSpec as P

D = 768
HEADS = 12
HEAD = 64
BLK = 128
PAIR = 2 * HEAD
PAIRS = HEADS // 2
DOCS = 5
TERMS = 3

score_scale = 0.125
masked_score = -1e30
norm_epsilon = 1e-06
tiny_term = 1e-30
learn_rate = 0.3
decay_rate = 1.0 - 2.0 ** (-0.8)
back_step = 768
vmem_bytes = 56 * 2**20

low_type = jnp.bfloat16
f32 = jnp.float32


def dot(former, latter, former_axis, latter_axis):
    return lax.dot_general(
        former,
        latter,
        (((former_axis,), (latter_axis,)), ((), ())),
        preferred_element_type=f32,
    )


def rms_norm(values, gain_vector):
    return (
        values
        * lax.rsqrt(jnp.mean(values * values, axis=-1, keepdims=True) + norm_epsilon)
        * gain_vector
    )


def gelu_tanh(values):
    return (
        0.5
        * values
        * (1.0 + jnp.tanh(0.7978845608028654 * (values + 0.044715 * values * values * values)))
    )


def documents(lengths, row_length):
    doc_ends = jnp.cumsum(lengths)
    position = jnp.arange(row_length, dtype=jnp.int32)
    return jnp.sum((position[:, None] >= doc_ends[None, :]).astype(jnp.int32), axis=1)


def split_terms(values):
    terms = []
    rest = values
    for _ in range(TERMS):
        term = lax.reduce_precision(rest, 8, 7)
        terms.append(term)
        rest = rest - term
    return terms


def extra_columns(blocks):
    return TERMS * blocks, TERMS * blocks + DOCS


def query_extra(doc_query, blocks):
    count = doc_query.shape[0]
    doc_start, one_start = extra_columns(blocks)
    lane = lax.broadcasted_iota(jnp.int32, (count, 128), 1)
    block = lax.broadcasted_iota(jnp.int32, (count, 128), 0) // BLK
    is_block = (lane < doc_start) & (lane % blocks == block)
    is_doc = (lane >= doc_start) & (lane < one_start) & (lane - doc_start == doc_query[:, None])
    return (is_block | is_doc).astype(low_type)


def with_row_terms(extra, values, blocks):
    _, one_start = extra_columns(blocks)
    lane = lax.broadcasted_iota(jnp.int32, (1, 1, 128), 2)
    result = jnp.broadcast_to(extra.astype(f32)[None], (HEADS,) + extra.shape)
    for place, term in enumerate(split_terms(values)):
        result = jnp.where(lane == one_start + place, term[:, :, None], result)
    return result.astype(low_type)


def key_picks(bucket_rows, doc_all, buckets):
    blocks, row_length = bucket_rows.shape
    one_hot = (
        bucket_rows.T[:, :, None] == jnp.arange(buckets, dtype=jnp.int32)[None, None, :]
    ).reshape(row_length, blocks * buckets)
    other_doc = doc_all[:, None] != jnp.arange(DOCS, dtype=jnp.int32)[None, :]
    ones = jnp.ones((row_length, 1), jnp.bool_)
    return jnp.concatenate([one_hot, other_doc, ones], axis=1).astype(low_type)


def key_extra(picks, bias_table, blocks):
    buckets = bias_table.shape[0]
    doc_start, one_start = extra_columns(blocks)
    terms = jnp.stack(split_terms(bias_table), axis=0)
    lane = jnp.arange(128, dtype=jnp.int32)
    place = jnp.clip(lane // blocks, 0, TERMS - 1)
    spread = jnp.transpose(terms[place], (1, 2, 0))
    at_block = (lane[None, :] % blocks == jnp.arange(blocks, dtype=jnp.int32)[:, None]) & (
        lane[None, :] < doc_start
    )
    bias_part = jnp.where(at_block[:, None, None, :], spread[None], 0.0).reshape(
        blocks * buckets, HEADS, 128
    )
    doc_part = jnp.where(
        lane[None, :] - doc_start == jnp.arange(DOCS, dtype=jnp.int32)[:, None], masked_score, 0.0
    )
    one_part = ((lane >= one_start) & (lane < one_start + TERMS)).astype(f32)[None]
    rest = jnp.concatenate([doc_part, one_part], axis=0)
    rest = jnp.broadcast_to(rest[:, None, :], (DOCS + 1, HEADS, 128))
    whole = jnp.concatenate([bias_part, rest], axis=0).reshape(-1, HEADS * 128).astype(low_type)
    return dot(picks, whole, 1, 0).astype(low_type)


def forward_kernel(queries, extra, keys, values_t, keys_extra, context_t, log_total):
    count = queries.shape[0]
    lane = lax.broadcasted_iota(jnp.int32, (count, PAIR), 1)
    query_pair = queries[...]
    for head in range(2):
        mine = (lane < HEAD) if head == 0 else (lane >= HEAD)
        query_side = jnp.concatenate(
            [jnp.where(mine, query_pair, jnp.zeros_like(query_pair)), extra[...]], axis=1
        )
        key_side = jnp.concatenate([keys[...], keys_extra[:, 128 * head : 128 * head + 128]], axis=1)
        scores = dot(key_side, query_side, 1, 1)
        top = jnp.max(scores, axis=0, keepdims=True)
        unscaled = jnp.exp(scores - top).astype(low_type)
        value_side = jnp.concatenate(
            [
                values_t[HEAD * head : HEAD * head + HEAD, :],
                jnp.ones((16, unscaled.shape[0]), low_type),
            ],
            axis=0,
        )
        weighted = dot(value_side, unscaled, 1, 0)
        total = weighted[HEAD : HEAD + 1]
        context_t[pl.ds(HEAD * head, HEAD), :] = weighted[:HEAD] / total
        log_total[pl.ds(8 * head, 8), :] = jnp.broadcast_to(top + jnp.log(total), (8, count))


def attend(queries, extra, keys, values_t, keys_extra):
    count, row_length = queries.shape[0], keys.shape[0]
    return pl.pallas_call(
        forward_kernel,
        grid=(PAIRS,),
        out_shape=[
            jax.ShapeDtypeStruct((D, count), f32),
            jax.ShapeDtypeStruct((HEADS * 8, count), f32),
        ],
        in_specs=[
            pl.BlockSpec((count, PAIR), lambda pair: (0, pair)),
            pl.BlockSpec((count, 128), lambda pair: (0, 0)),
            pl.BlockSpec((row_length, PAIR), lambda pair: (0, pair)),
            pl.BlockSpec((PAIR, row_length), lambda pair: (pair, 0)),
            pl.BlockSpec((row_length, 256), lambda pair: (0, pair)),
        ],
        out_specs=[
            pl.BlockSpec((PAIR, count), lambda pair: (pair, 0)),
            pl.BlockSpec((16, count), lambda pair: (pair, 0)),
        ],
        compiler_params=pltpu.CompilerParams(vmem_limit_bytes=vmem_bytes),
        cost_estimate=pl.CostEstimate(
            flops=4 * HEADS * count * row_length * 256,
            bytes_accessed=HEADS * row_length * 1024,
            transcendentals=HEADS * count * row_length,
        ),
        name="attention_forward",
    )(queries, extra, keys, values_t, keys_extra)


def backward_kernel(
    queries,
    query_rows,
    delta_rows,
    context_grad,
    queries_t,
    context_grad_t,
    keys,
    values_t,
    keys_extra,
    query_grad,
    key_grad_t,
    value_grad_t,
    folded,
):
    step = pl.program_id(1)
    count, amount = queries.shape[0], keys.shape[0]
    lane = lax.broadcasted_iota(jnp.int32, (count, PAIR), 1)
    query_pair, grad_pair = queries[...], context_grad[...]
    zeros = jnp.zeros_like(query_pair)

    @pl.when(step == 0)
    def _():
        query_grad[...] = jnp.zeros_like(query_grad)

    query_grads = []
    for head in range(2):
        mine = (lane < HEAD) if head == 0 else (lane >= HEAD)
        rows = pl.ds(HEAD * head, HEAD)
        more = keys_extra[:, 128 * head : 128 * head + 128]
        query_side = jnp.concatenate([jnp.where(mine, query_pair, zeros), query_rows[head]], axis=1)
        grad_side = jnp.concatenate([jnp.where(mine, grad_pair, zeros), delta_rows[head]], axis=1)
        key_side = jnp.concatenate([keys[...], more], axis=1)
        value_side = jnp.concatenate(
            [values_t[...], jnp.ones((128, amount), low_type)], axis=0
        )
        attention = jnp.exp(dot(query_side, key_side, 1, 1))
        score_grad = attention * dot(grad_side, value_side, 1, 0)
        attention_low = attention.astype(low_type)
        score_low = score_grad.astype(low_type)
        for block in range(count // BLK):
            folded[head, pl.ds(block, 1), :] = jnp.sum(
                score_grad[BLK * block : BLK * block + BLK], axis=0, keepdims=True
            )
        query_grads.append(dot(score_low, keys[...], 1, 0))
        value_grad_t[rows, :] = dot(context_grad_t[rows, :], attention_low, 1, 0).astype(low_type)
        key_grad_t[rows, :] = dot(queries_t[rows, :], score_low, 1, 0).astype(low_type)
    query_grad[...] += jnp.where(lane < HEAD, query_grads[0], query_grads[1])


def attend_back(
    queries, query_rows, delta_rows, context_grad, queries_t, context_grad_t, keys, values_t, keys_extra
):
    count, row_length = queries.shape[0], keys.shape[0]
    blocks = count // BLK
    of_pair = pl.BlockSpec((count, PAIR), lambda pair, step: (0, pair))
    of_pair_t = pl.BlockSpec((PAIR, count), lambda pair, step: (pair, 0))
    of_heads = pl.BlockSpec((2, count, 128), lambda pair, step: (pair, 0, 0))
    key_t = pl.BlockSpec((PAIR, back_step), lambda pair, step: (pair, step))
    return pl.pallas_call(
        backward_kernel,
        grid=(PAIRS, row_length // back_step),
        out_shape=[
            jax.ShapeDtypeStruct((count, D), f32),
            jax.ShapeDtypeStruct((D, row_length), low_type),
            jax.ShapeDtypeStruct((D, row_length), low_type),
            jax.ShapeDtypeStruct((HEADS, blocks, row_length), f32),
        ],
        in_specs=[
            of_pair,
            of_heads,
            of_heads,
            of_pair,
            of_pair_t,
            of_pair_t,
            pl.BlockSpec((back_step, PAIR), lambda pair, step: (step, pair)),
            key_t,
            pl.BlockSpec((back_step, 256), lambda pair, step: (step, pair)),
        ],
        out_specs=[
            of_pair,
            key_t,
            key_t,
            pl.BlockSpec((2, blocks, back_step), lambda pair, step: (pair, 0, step)),
        ],
        compiler_params=pltpu.CompilerParams(vmem_limit_bytes=vmem_bytes),
        cost_estimate=pl.CostEstimate(
            flops=10 * HEADS * count * row_length * 200,
            bytes_accessed=HEADS * row_length * 2048,
            transcendentals=HEADS * count * row_length,
        ),
        name="attention_backward",
    )(
        queries,
        query_rows,
        delta_rows,
        context_grad,
        queries_t,
        context_grad_t,
        keys,
        values_t,
        keys_extra,
    )


MESH = pl.DeviceIdType.MESH


class Place:
    def __init__(self):
        self.seq, self.dp = lax.axis_index("seq"), lax.axis_index("dp")
        self.core, self.x, self.y = self.dp % 2, self.dp // 2 % 2, self.dp // 4
        self.by_core = (self.seq, self.dp + 1 - 2 * self.core)
        self.by_x = (self.seq, self.dp + 2 - 4 * self.x)
        self.by_y = (self.seq, self.dp + 4 - 8 * self.y)
        self.others = [((self.seq + step) % 4, self.dp) for step in (1, 2, 3)]

    def greet(self):
        barrier = pltpu.get_barrier_semaphore()
        partners = [self.by_core, self.by_x, self.by_y] + self.others
        for partner in partners:
            pl.semaphore_signal(barrier, inc=1, device_id=partner, device_id_type=MESH)
        pl.semaphore_wait(barrier, len(partners))


def send(source, target, sems, index, partner):
    return pltpu.make_async_remote_copy(
        src_ref=source,
        dst_ref=target,
        send_sem=sems.at[0, index],
        recv_sem=sems.at[1, index],
        device_id=partner,
        device_id_type=MESH,
    )


def half_of(width, which):
    return pl.ds(pl.multiple_of(which * (width // 2), 128), width // 2)


class Gather:
    steps = 6

    def __init__(self, at, shard, pair, low, whole, sems, local_sems, x_first):
        self.at, self.shard, self.pair, self.low, self.whole = at, shard, pair, low, whole
        rows, width = shard.shape
        mine, other = half_of(width, at.core), half_of(width, 1 - at.core)
        own_rows = pl.ds(pl.multiple_of(rows * at.core, 8), rows)
        place = whole.at[at.seq, at.y, at.x, :, mine]
        along_x, along_y = (whole.at[:, at.y, at.x, :, mine], whole.at[:, at.y, :, :, mine])
        if not x_first:
            along_x, along_y = (whole.at[:, :, at.x, :, mine], along_x)
        self.local = [
            pltpu.make_async_copy(shard.at[:, mine], pair.at[own_rows], local_sems.at[0]),
            pltpu.make_async_copy(low, place, local_sems.at[1]),
        ]
        self.first = send(shard.at[:, other], pair.at[own_rows], sems, 0, at.by_core)
        self.over_z = [send(low, place, sems, 1 + k, at.others[k]) for k in range(3)]
        self.over_x = send(along_x, along_x, sems, 4, at.by_x)
        self.over_y = send(along_y, along_y, sems, 5, at.by_y)
        self.order = [self.over_x, self.over_y] if x_first else [self.over_y, self.over_x]
        self.last = send(whole.at[:, :, :, :, mine], whole.at[:, :, :, :, mine], sems, 6, at.by_core)

    def step(self, number):
        if number == 0:
            self.local[0].start()
            self.first.start()
        elif number == 1:
            self.local[0].wait()
            self.first.wait()
            self.low[...] = self.pair[...].astype(low_type)
            self.local[1].start()
            for copy in self.over_z:
                copy.start()
        elif number == 2:
            self.local[1].wait()
            for copy in self.over_z:
                copy.wait()
            self.order[0].start()
        elif number == 3:
            self.order[0].wait()
            self.order[1].start()
        elif number == 4:
            self.order[1].wait()
            self.last.start()
        else:
            self.last.wait()


class Scatter:
    steps = 6

    def __init__(self, at, term, held, arrived, total, share, sems, local_sems, x_first):
        self.at, self.held, self.arrived, self.total = at, held, arrived, total
        self.x_first = x_first
        width = term.shape[4]
        rows = term.shape[3] // 2
        mine, other = half_of(width, at.core), half_of(width, 1 - at.core)
        of_core = lambda which: pl.ds(pl.multiple_of(rows * which, 8), rows)
        self.local = [
            pltpu.make_async_copy(term.at[:, :, :, :, mine], held, local_sems.at[0]),
            pltpu.make_async_copy(total.at[of_core(at.core)], share.at[:, mine], local_sems.at[1]),
        ]
        self.first = send(term.at[:, :, :, :, other], arrived[0], sems, 0, at.by_core)
        if x_first:
            self.second = send(held.at[:, :, 1 - at.x], arrived[1], sems, 1, at.by_x)
            self.third = send(held.at[:, 1 - at.y, at.x], arrived[2], sems, 2, at.by_y)
        else:
            self.second = send(held.at[:, 1 - at.y], arrived[1], sems, 1, at.by_y)
            self.third = send(held.at[:, at.y, 1 - at.x], arrived[2], sems, 2, at.by_x)
        self.over_z = [
            send(held.at[at.others[k][0], at.y, at.x], arrived[3].at[k], sems, 3 + k, at.others[k])
            for k in range(3)
        ]
        self.last = send(total.at[of_core(1 - at.core)], share.at[:, mine], sems, 6, at.by_core)

    def add(self, place, values):
        self.held[place] = (self.held[place].astype(f32) + values.astype(f32)).astype(low_type)

    def step(self, number):
        at = self.at
        if number == 0:
            self.local[0].start()
            self.first.start()
        elif number == 1:
            self.local[0].wait()
            self.first.wait()

            @pl.loop(0, 4)
            def _(row):
                for across in range(4):
                    place = (row, across // 2, across % 2)
                    self.add(place, self.arrived[0][place])

            self.second.start()
        elif number == 2:
            self.second.wait()

            @pl.loop(0, 4)
            def _(row):
                for across in range(2):
                    place = (row, across, at.x) if self.x_first else (row, at.y, across)
                    self.add(place, self.arrived[1][row, across])

            self.third.start()
        elif number == 3:
            self.third.wait()

            @pl.loop(0, 4)
            def _(row):
                self.add((row, at.y, at.x), self.arrived[2][row])

            for copy in self.over_z:
                copy.start()
        elif number == 4:
            for copy in self.over_z:
                copy.wait()
            total = self.held[at.seq, at.y, at.x].astype(f32)
            for k in range(3):
                total = total + self.arrived[3][k].astype(f32)
            self.total[...] = total
            self.local[1].start()
            self.last.start()
        else:
            self.local[1].wait()
            self.last.wait()


class Ring:
    def __init__(self, at, own, blocks, sems, local_sem):
        self.at = at
        seq = at.seq
        self.local = pltpu.make_async_copy(own, blocks.at[seq], local_sem)
        right, left = ((seq + 1) % 4, at.dp), ((seq + 3) % 4, at.dp)
        self.hops = []
        for hop in range(3):
            back, ahead = (seq + 4 - hop) % 4, (seq + hop) % 4
            block_back = own if hop == 0 else blocks.at[back]
            block_ahead = own if hop == 0 else blocks.at[ahead]
            self.hops.append(
                [
                    (
                        (seq >= hop) & (seq < 3),
                        send(block_back, blocks.at[back], sems, hop, right),
                        seq >= hop + 1,
                    ),
                    (
                        (seq + hop <= 3) & (seq > 0),
                        send(block_ahead, blocks.at[ahead], sems, 3 + hop, left),
                        seq + hop + 1 <= 3,
                    ),
                ]
            )

    def start(self, hop):
        if hop == 0:
            self.local.start()
        for sends, copy, _ in self.hops[hop]:
            pl.when(sends)(copy.start)

    def arrive(self, hop):
        for _, copy, receives in self.hops[hop]:
            pl.when(receives)(copy.wait_recv)

    def finish(self):
        self.local.wait()
        for hop in self.hops:
            for sends, copy, _ in hop:
                pl.when(sends)(copy.wait_send)


X_FIRST = (True, False, False, True)


def remote_scratch(shapes):
    return [pltpu.SemaphoreType.DMA((2, 7)), pltpu.SemaphoreType.DMA((2,))] * len(shapes)


def gather_kernel(*refs):
    shards, own, wholes, blocks = refs[:4], refs[4], refs[5:9], refs[9]
    scratch = refs[10:]
    pairs, lows, sems = scratch[:4], scratch[4:8], scratch[8:16]
    ring_sems, ring_local = scratch[16:]
    at = Place()
    at.greet()
    gathers = [
        Gather(
            at,
            shards[k],
            pairs[k],
            lows[k],
            wholes[k],
            sems[2 * k],
            sems[2 * k + 1],
            X_FIRST[k],
        )
        for k in range(4)
    ]
    ring = Ring(at, own, blocks, ring_sems, ring_local.at[0])
    for gather in gathers:
        gather.step(0)
    gathers[0].step(1)
    ring.start(0)
    for number in range(2, 4):
        gathers[0].step(number)
    for gather in gathers[1:]:
        gather.step(1)
    ring.arrive(0)
    ring.start(1)
    for number in range(4, 6):
        gathers[0].step(number)
    for gather in gathers[1:]:
        gather.step(2)
    ring.arrive(1)
    ring.start(2)
    for number in range(3, 6):
        for gather in gathers[1:]:
            gather.step(number)
    ring.arrive(2)
    ring.finish()


def gather_weights(shards, own):
    low_shape = lambda shard: (2 * shard.shape[0], shard.shape[1] // 2)
    anywhere = pl.BlockSpec(memory_space=pl.ANY)
    return pl.pallas_call(
        gather_kernel,
        out_shape=[
            jax.ShapeDtypeStruct((4, 2, 2, 2 * shard.shape[0], shard.shape[1]), low_type)
            for shard in shards
        ]
        + [jax.ShapeDtypeStruct((4,) + own.shape, low_type)],
        in_specs=[anywhere] * 5,
        out_specs=[anywhere] * 5,
        scratch_shapes=[pltpu.VMEM(low_shape(shard), f32) for shard in shards]
        + [pltpu.VMEM(low_shape(shard), low_type) for shard in shards]
        + remote_scratch(shards)
        + [pltpu.SemaphoreType.DMA((2, 6)), pltpu.SemaphoreType.DMA((1,))],
        compiler_params=pltpu.CompilerParams(
            collective_id=0, has_side_effects=True, vmem_limit_bytes=vmem_bytes
        ),
        name="gather_weights",
    )(*shards, own)


def scatter_kernel(count, *refs):
    terms, shares, scratch = refs[:count], refs[count : 2 * count], refs[2 * count :]
    held, arrived, totals, sems = (
        scratch[:count],
        scratch[count : 5 * count],
        scratch[5 * count : 6 * count],
        scratch[6 * count :],
    )
    at = Place()
    at.greet()
    scatters = [
        Scatter(
            at,
            terms[k],
            held[k],
            arrived[4 * k : 4 * k + 4],
            totals[k],
            shares[k],
            sems[2 * k],
            sems[2 * k + 1],
            k % 2 == 0,
        )
        for k in range(count)
    ]
    for number in range(Scatter.steps):
        for scatter in scatters:
            scatter.step(number)


def scatter_scratch(terms, x_firsts):
    held, arrived, totals = [], [], []
    for term, x_first in zip(terms, x_firsts):
        rows, half = term.shape[3], term.shape[4] // 2
        held.append(pltpu.VMEM((4, 2, 2, rows, half), low_type))
        arrived += [
            pltpu.VMEM((4, 2, 2, rows, half), low_type),
            pltpu.VMEM((4, 2, rows, half), low_type),
            pltpu.VMEM((4, rows, half), low_type),
            pltpu.VMEM((3, rows, half), low_type),
        ]
        totals.append(pltpu.VMEM((rows, half), f32))
    return held + arrived + totals + remote_scratch(terms)


def scatter_terms(terms, number):
    terms = [
        term.reshape(4, 2, 2, term.shape[0] // 16, term.shape[1]) for term in terms
    ]
    anywhere = pl.BlockSpec(memory_space=pl.ANY)
    return pl.pallas_call(
        functools.partial(scatter_kernel, len(terms)),
        out_shape=[
            jax.ShapeDtypeStruct((term.shape[3] // 2, term.shape[4]), f32) for term in terms
        ],
        in_specs=[anywhere] * len(terms),
        out_specs=[anywhere] * len(terms),
        scratch_shapes=scatter_scratch(terms, [k % 2 == 0 for k in range(len(terms))]),
        compiler_params=pltpu.CompilerParams(
            collective_id=number, has_side_effects=True, vmem_limit_bytes=vmem_bytes
        ),
        name="scatter_terms",
    )(*terms)


def body(
    hidden_states,
    output_cotangent,
    document_lengths,
    bucket_index,
    norm_gains,
    bias_table,
    project_weight,
    output_weight,
    expand_weight,
    reduce_weight,
    project_rows,
    project_columns,
    output_rows,
    output_columns,
    expand_rows,
    expand_columns,
    reduce_rows,
    reduce_columns,
    gains_moment,
    table_moment,
):
    every = ("seq", "dp")
    local_rows = hidden_states.shape[1]
    row_length = local_rows * lax.axis_size("seq")
    gradient_scale = 1.0 / math.sqrt(row_length * lax.axis_size("dp"))
    place = lax.axis_index("seq")
    blocks = local_rows // BLK

    shards = (project_weight, output_weight, expand_weight, reduce_weight)
    direct = (
        lax.axis_size("seq") == 4
        and lax.axis_size("dp") == 8
        and all(shard.shape[0] % 8 == 0 and shard.shape[1] % 256 == 0 for shard in shards)
    )
    if direct:
        *wholes, row_states = gather_weights(shards, hidden_states[0])
        project_full, output_full, expand_full, reduce_full = (
            whole.reshape(-1, whole.shape[4]) for whole in wholes
        )
        row_states = row_states.reshape(row_length, -1)
    else:
        project_full, output_full, expand_full, reduce_full = (
            lax.all_gather(shard.astype(low_type), every, axis=0, tiled=True) for shard in shards
        )
        row_states = lax.all_gather(hidden_states[0], "seq", axis=0, tiled=True)

    doc_all = documents(document_lengths[0], row_length)
    doc_query = lax.dynamic_slice_in_dim(doc_all, place * local_rows, local_rows)
    picks = key_picks(bucket_index[0], doc_all, bias_table.shape[0])
    keys_extra = key_extra(picks, bias_table, blocks)
    extra = query_extra(doc_query, blocks)

    inputs = hidden_states[0].astype(f32)
    normed_one, pullback_one = jax.vjp(rms_norm, inputs, norm_gains[0])
    normed_low = normed_one.astype(low_type)
    normed_all = rms_norm(row_states.astype(f32), norm_gains[0]).astype(low_type)
    query_weight, key_weight, value_weight = (
        project_full[:, :D],
        project_full[:, D : 2 * D],
        project_full[:, 2 * D :],
    )
    queries = (dot(normed_low, query_weight, 1, 0).astype(low_type).astype(f32) * score_scale).astype(
        low_type
    )
    queries_t = (
        dot(query_weight, normed_low, 0, 1).astype(low_type).astype(f32) * score_scale
    ).astype(low_type)
    keys = dot(normed_all, key_weight, 1, 0).astype(low_type)
    values_t = dot(value_weight, normed_all, 0, 1).astype(low_type)

    context_t, log_total = attend(queries, extra, keys, values_t, keys_extra)
    log_total = log_total.reshape(HEADS, 8, local_rows)[:, 0]
    context_low_t = context_t.astype(low_type)
    residual = inputs + dot(context_low_t, output_full, 0, 0)
    normed_two, pullback_two = jax.vjp(rms_norm, residual, norm_gains[1])
    normed_two_low = normed_two.astype(low_type)
    expanded = dot(normed_two_low, expand_full, 1, 0)
    activated, pullback_gelu = jax.vjp(gelu_tanh, expanded)
    activated_low = activated.astype(low_type)
    layer_output = (residual + dot(activated_low, reduce_full, 1, 0)).astype(low_type)[None]

    upstream_low = output_cotangent[0].astype(low_type)
    upstream = upstream_low.astype(f32)
    reduce_term = dot(activated_low, upstream_low, 0, 0)
    (expanded_grad,) = pullback_gelu(dot(upstream_low, reduce_full, 1, 1))
    expanded_low = expanded_grad.astype(low_type)
    expand_term = dot(normed_two_low, expanded_low, 0, 0)
    residual_part, gain_two_grad = pullback_two(dot(expanded_low, expand_full, 1, 1))
    residual_grad = upstream + residual_part
    residual_low = residual_grad.astype(low_type)
    output_term = dot(context_low_t, residual_low, 1, 0)
    context_grad = dot(residual_low, output_full, 1, 1).astype(low_type)
    context_grad_t = dot(output_full, residual_low, 1, 1).astype(low_type)
    delta = jnp.sum(
        (context_grad_t.astype(f32) * context_t).reshape(HEADS, HEAD, local_rows), axis=1
    )

    query_grad, key_grad_t, value_grad_t, folded = attend_back(
        queries,
        with_row_terms(extra, -log_total, blocks),
        with_row_terms(jnp.zeros_like(extra), -delta, blocks),
        context_grad,
        queries_t,
        context_grad_t,
        keys,
        values_t,
        keys_extra,
    )
    buckets = bias_table.shape[0]
    picked = jnp.dot(
        folded.reshape(HEADS * blocks, row_length),
        picks[:, : blocks * buckets].astype(f32),
        precision=lax.Precision.HIGHEST,
    )
    table_grad = jnp.einsum("hkkb->bh", picked.reshape(HEADS, blocks, blocks, buckets))

    query_grad_low = (query_grad * score_scale).astype(low_type)
    project_term = jnp.concatenate(
        [
            dot(normed_low, query_grad_low, 0, 0),
            dot(normed_all, key_grad_t, 0, 1),
            dot(normed_all, value_grad_t, 0, 1),
        ],
        axis=1,
    )
    key_part = dot(key_grad_t, key_weight, 0, 1) + dot(value_grad_t, value_weight, 0, 1)
    key_part = lax.psum_scatter(
        key_part.astype(low_type), "seq", scatter_dimension=0, tiled=True
    ).astype(f32)
    input_part, gain_one_grad = pullback_one(dot(query_grad_low, query_weight, 1, 1) + key_part)
    input_gradient = (residual_grad + input_part).astype(low_type)[None]

    terms = [
        term.astype(low_type) for term in (project_term, output_term, expand_term, reduce_term)
    ]
    if direct:
        shares = scatter_terms(terms, 1)
    else:
        shares = [
            lax.psum_scatter(term, every, scatter_dimension=0, tiled=True).astype(f32)
            for term in terms
        ]

    gradients = tuple((share * gradient_scale for share in shares))
    row_before = (project_rows, output_rows, expand_rows, reduce_rows)
    row_after = []
    column_parts = []
    row_sums = []
    for gradient, previous in zip(gradients, row_before):
        squares = gradient * gradient + tiny_term
        updated_rows = decay_rate * previous + (1.0 - decay_rate) * jnp.mean(squares, axis=1)
        row_after.append(updated_rows)
        column_parts.append(jnp.sum(squares, axis=0))
        row_sums.append(jnp.sum(updated_rows))
    summed = lax.psum(
        (
            column_parts[0],
            column_parts[1],
            column_parts[2],
            column_parts[3],
            jnp.stack(row_sums),
            jnp.stack([gain_one_grad, gain_two_grad]),
            table_grad,
        ),
        every,
    )
    column_before = (project_columns, output_columns, expand_columns, reduce_columns)
    weights_before = (project_weight, output_weight, expand_weight, reduce_weight)
    full_rows = (
        project_full.shape[0],
        output_full.shape[0],
        expand_full.shape[0],
        reduce_full.shape[0],
    )
    updated_weights = []
    columns_after = []
    for position in range(4):
        columns_new = decay_rate * column_before[position] + (1.0 - decay_rate) * (
            summed[position] / full_rows[position]
        )
        row_mean = summed[4][position] / full_rows[position]
        denominator = row_after[position][:, None] * columns_new[None, :] / row_mean
        updated_weights.append(
            weights_before[position] - learn_rate * gradients[position] * lax.rsqrt(denominator)
        )
        columns_after.append(columns_new)
    gains_gradient = summed[5] * gradient_scale
    table_gradient = summed[6] * gradient_scale
    gains_moment_new = decay_rate * gains_moment + (1.0 - decay_rate) * (
        gains_gradient * gains_gradient + tiny_term
    )
    gains_updated = norm_gains - learn_rate * gains_gradient * lax.rsqrt(gains_moment_new)
    table_moment_new = decay_rate * table_moment + (1.0 - decay_rate) * (
        table_gradient * table_gradient + tiny_term
    )
    table_updated = bias_table - learn_rate * table_gradient * lax.rsqrt(table_moment_new)
    return (
        layer_output,
        input_gradient,
        gains_gradient,
        table_gradient,
        gradients[0],
        gradients[1],
        gradients[2],
        gradients[3],
        gains_updated,
        table_updated,
        updated_weights[0],
        updated_weights[1],
        updated_weights[2],
        updated_weights[3],
        row_after[0],
        columns_after[0],
        row_after[1],
        columns_after[1],
        row_after[2],
        columns_after[2],
        row_after[3],
        columns_after[3],
        gains_moment_new,
        table_moment_new,
    )


def solution(mesh):
    placed = (
        P("dp", "seq", None),
        P("dp", "seq", None),
        P("dp", None),
        P("dp", "seq", None),
        P(),
        P(),
        P(("seq", "dp"), None),
        P(("seq", "dp"), None),
        P(("seq", "dp"), None),
        P(("seq", "dp"), None),
        P(("seq", "dp")),
        P(),
        P(("seq", "dp")),
        P(),
        P(("seq", "dp")),
        P(),
        P(("seq", "dp")),
        P(),
        P(),
        P(),
    )
    return jax.shard_map(
        body,
        mesh=mesh,
        in_specs=placed,
        out_specs=(
            P("dp", "seq", None),
            P("dp", "seq", None),
            P(),
            P(),
            P(("seq", "dp"), None),
            P(("seq", "dp"), None),
            P(("seq", "dp"), None),
            P(("seq", "dp"), None),
            P(),
            P(),
            P(("seq", "dp"), None),
            P(("seq", "dp"), None),
            P(("seq", "dp"), None),
            P(("seq", "dp"), None),
            P(("seq", "dp")),
            P(),
            P(("seq", "dp")),
            P(),
            P(("seq", "dp")),
            P(),
            P(("seq", "dp")),
            P(),
            P(),
            P(),
        ),
        check_vma=False,
    )
```

```python
import functools
import math

import jax
import jax.numpy as jnp
from jax import lax
from jax.experimental import pallas as pl
from jax.experimental.pallas import tpu as pltpu
from jax.sharding import PartitionSpec as P

D = 768
HEADS = 12
HEAD = 64
BLK = 128
PAIR = 2 * HEAD
PAIRS = HEADS // 2
DOCS = 5
TERMS = 3

score_scale = 0.125
masked_score = -1e30
norm_epsilon = 1e-06
tiny_term = 1e-30
learn_rate = 0.3
decay_rate = 1.0 - 2.0 ** (-0.8)
back_step = 768
vmem_bytes = 56 * 2**20

low_type = jnp.bfloat16
f32 = jnp.float32


def dot(former, latter, former_axis, latter_axis):
    return lax.dot_general(
        former,
        latter,
        (((former_axis,), (latter_axis,)), ((), ())),
        preferred_element_type=f32,
    )


def rms_norm(values, gain_vector):
    return (
        values
        * lax.rsqrt(jnp.mean(values * values, axis=-1, keepdims=True) + norm_epsilon)
        * gain_vector
    )


def gelu_tanh(values):
    return (
        0.5
        * values
        * (1.0 + jnp.tanh(0.7978845608028654 * (values + 0.044715 * values * values * values)))
    )


def documents(lengths, row_length):
    doc_ends = jnp.cumsum(lengths)
    position = jnp.arange(row_length, dtype=jnp.int32)
    return jnp.sum((position[:, None] >= doc_ends[None, :]).astype(jnp.int32), axis=1)


def split_terms(values):
    terms = []
    rest = values
    for _ in range(TERMS):
        term = lax.reduce_precision(rest, 8, 7)
        terms.append(term)
        rest = rest - term
    return terms


def extra_columns(blocks):
    return TERMS * blocks, TERMS * blocks + DOCS


def query_extra(doc_query, blocks):
    count = doc_query.shape[0]
    doc_start, one_start = extra_columns(blocks)
    lane = lax.broadcasted_iota(jnp.int32, (count, 128), 1)
    block = lax.broadcasted_iota(jnp.int32, (count, 128), 0) // BLK
    is_block = (lane < doc_start) & (lane % blocks == block)
    is_doc = (lane >= doc_start) & (lane < one_start) & (lane - doc_start == doc_query[:, None])
    return (is_block | is_doc).astype(low_type)


def with_row_terms(extra, values, blocks):
    _, one_start = extra_columns(blocks)
    lane = lax.broadcasted_iota(jnp.int32, (1, 1, 128), 2)
    result = jnp.broadcast_to(extra.astype(f32)[None], (HEADS,) + extra.shape)
    for place, term in enumerate(split_terms(values)):
        result = jnp.where(lane == one_start + place, term[:, :, None], result)
    return result.astype(low_type)


def key_picks(bucket_rows, doc_all, buckets):
    blocks, row_length = bucket_rows.shape
    one_hot = (
        bucket_rows.T[:, :, None] == jnp.arange(buckets, dtype=jnp.int32)[None, None, :]
    ).reshape(row_length, blocks * buckets)
    other_doc = doc_all[:, None] != jnp.arange(DOCS, dtype=jnp.int32)[None, :]
    ones = jnp.ones((row_length, 1), jnp.bool_)
    return jnp.concatenate([one_hot, other_doc, ones], axis=1).astype(low_type)


def key_extra(picks, bias_table, blocks):
    buckets = bias_table.shape[0]
    doc_start, one_start = extra_columns(blocks)
    terms = jnp.stack(split_terms(bias_table), axis=0)
    lane = jnp.arange(128, dtype=jnp.int32)
    place = jnp.clip(lane // blocks, 0, TERMS - 1)
    spread = jnp.transpose(terms[place], (1, 2, 0))
    at_block = (lane[None, :] % blocks == jnp.arange(blocks, dtype=jnp.int32)[:, None]) & (
        lane[None, :] < doc_start
    )
    bias_part = jnp.where(at_block[:, None, None, :], spread[None], 0.0).reshape(
        blocks * buckets, HEADS, 128
    )
    doc_part = jnp.where(
        lane[None, :] - doc_start == jnp.arange(DOCS, dtype=jnp.int32)[:, None], masked_score, 0.0
    )
    one_part = ((lane >= one_start) & (lane < one_start + TERMS)).astype(f32)[None]
    rest = jnp.concatenate([doc_part, one_part], axis=0)
    rest = jnp.broadcast_to(rest[:, None, :], (DOCS + 1, HEADS, 128))
    whole = jnp.concatenate([bias_part, rest], axis=0).reshape(-1, HEADS * 128).astype(low_type)
    return dot(picks, whole, 1, 0).astype(low_type)


def forward_kernel(queries, extra, keys, values_t, keys_extra, context_t, log_total):
    count = queries.shape[0]
    lane = lax.broadcasted_iota(jnp.int32, (count, PAIR), 1)
    query_pair = queries[...]
    for head in range(2):
        mine = (lane < HEAD) if head == 0 else (lane >= HEAD)
        query_side = jnp.concatenate(
            [jnp.where(mine, query_pair, jnp.zeros_like(query_pair)), extra[...]], axis=1
        )
        key_side = jnp.concatenate([keys[...], keys_extra[:, 128 * head : 128 * head + 128]], axis=1)
        scores = dot(key_side, query_side, 1, 1)
        top = jnp.max(scores, axis=0, keepdims=True)
        unscaled = jnp.exp(scores - top).astype(low_type)
        value_side = jnp.concatenate(
            [
                values_t[HEAD * head : HEAD * head + HEAD, :],
                jnp.ones((16, unscaled.shape[0]), low_type),
            ],
            axis=0,
        )
        weighted = dot(value_side, unscaled, 1, 0)
        total = weighted[HEAD : HEAD + 1]
        context_t[pl.ds(HEAD * head, HEAD), :] = weighted[:HEAD] / total
        log_total[pl.ds(8 * head, 8), :] = jnp.broadcast_to(top + jnp.log(total), (8, count))


def attend(queries, extra, keys, values_t, keys_extra):
    count, row_length = queries.shape[0], keys.shape[0]
    return pl.pallas_call(
        forward_kernel,
        grid=(PAIRS,),
        out_shape=[
            jax.ShapeDtypeStruct((D, count), f32),
            jax.ShapeDtypeStruct((HEADS * 8, count), f32),
        ],
        in_specs=[
            pl.BlockSpec((count, PAIR), lambda pair: (0, pair)),
            pl.BlockSpec((count, 128), lambda pair: (0, 0)),
            pl.BlockSpec((row_length, PAIR), lambda pair: (0, pair)),
            pl.BlockSpec((PAIR, row_length), lambda pair: (pair, 0)),
            pl.BlockSpec((row_length, 256), lambda pair: (0, pair)),
        ],
        out_specs=[
            pl.BlockSpec((PAIR, count), lambda pair: (pair, 0)),
            pl.BlockSpec((16, count), lambda pair: (pair, 0)),
        ],
        compiler_params=pltpu.CompilerParams(vmem_limit_bytes=vmem_bytes),
        cost_estimate=pl.CostEstimate(
            flops=4 * HEADS * count * row_length * 256,
            bytes_accessed=HEADS * row_length * 1024,
            transcendentals=HEADS * count * row_length,
        ),
        name="attention_forward",
    )(queries, extra, keys, values_t, keys_extra)


MESH = pl.DeviceIdType.MESH


class Place:
    def __init__(self):
        self.seq, self.dp = lax.axis_index("seq"), lax.axis_index("dp")
        self.core, self.x, self.y = self.dp % 2, self.dp // 2 % 2, self.dp // 4
        self.by_core = (self.seq, self.dp + 1 - 2 * self.core)
        self.by_x = (self.seq, self.dp + 2 - 4 * self.x)
        self.by_y = (self.seq, self.dp + 4 - 8 * self.y)
        self.others = [((self.seq + step) % 4, self.dp) for step in (1, 2, 3)]

    def greet(self):
        barrier = pltpu.get_barrier_semaphore()
        partners = [self.by_core, self.by_x, self.by_y] + self.others
        for partner in partners:
            pl.semaphore_signal(barrier, inc=1, device_id=partner, device_id_type=MESH)
        pl.semaphore_wait(barrier, len(partners))


def send(source, target, sems, index, partner):
    return pltpu.make_async_remote_copy(
        src_ref=source,
        dst_ref=target,
        send_sem=sems.at[0, index],
        recv_sem=sems.at[1, index],
        device_id=partner,
        device_id_type=MESH,
    )


def half_of(width, which):
    return pl.ds(pl.multiple_of(which * (width // 2), 128), width // 2)


class Gather:
    steps = 6

    def __init__(self, at, shard, pair, low, whole, sems, local_sems, x_first):
        self.at, self.shard, self.pair, self.low, self.whole = at, shard, pair, low, whole
        rows, width = shard.shape
        mine, other = half_of(width, at.core), half_of(width, 1 - at.core)
        own_rows = pl.ds(pl.multiple_of(rows * at.core, 8), rows)
        place = whole.at[at.seq, at.y, at.x, :, mine]
        along_x, along_y = (whole.at[:, at.y, at.x, :, mine], whole.at[:, at.y, :, :, mine])
        if not x_first:
            along_x, along_y = (whole.at[:, :, at.x, :, mine], along_x)
        self.local = [
            pltpu.make_async_copy(shard.at[:, mine], pair.at[own_rows], local_sems.at[0]),
            pltpu.make_async_copy(low, place, local_sems.at[1]),
        ]
        self.first = send(shard.at[:, other], pair.at[own_rows], sems, 0, at.by_core)
        self.over_z = [send(low, place, sems, 1 + k, at.others[k]) for k in range(3)]
        self.over_x = send(along_x, along_x, sems, 4, at.by_x)
        self.over_y = send(along_y, along_y, sems, 5, at.by_y)
        self.order = [self.over_x, self.over_y] if x_first else [self.over_y, self.over_x]
        self.last = send(whole.at[:, :, :, :, mine], whole.at[:, :, :, :, mine], sems, 6, at.by_core)

    def step(self, number):
        if number == 0:
            self.local[0].start()
            self.first.start()
        elif number == 1:
            self.local[0].wait()
            self.first.wait()
            self.low[...] = self.pair[...].astype(low_type)
            self.local[1].start()
            for copy in self.over_z:
                copy.start()
        elif number == 2:
            self.local[1].wait()
            for copy in self.over_z:
                copy.wait()
            self.order[0].start()
        elif number == 3:
            self.order[0].wait()
            self.order[1].start()
        elif number == 4:
            self.order[1].wait()
            self.last.start()
        else:
            self.last.wait()


class Scatter:
    steps = 6

    def __init__(self, at, plan, term, share, scratch, sems):
        start, width, share_start, self.x_first = plan
        self.at, self.held, self.arrived, self.total = at, scratch[0], scratch[1:5], scratch[5]
        held, arrived, total, x_first = self.held, self.arrived, self.total, self.x_first
        sems, local_sems = sems
        rows = term.shape[3] // 2
        columns = lambda first, which: pl.ds(
            pl.multiple_of(first + which * (width // 2), 128), width // 2
        )
        mine, other = columns(start, at.core), columns(start, 1 - at.core)
        share_mine = columns(share_start, at.core)
        of_core = lambda which: pl.ds(pl.multiple_of(rows * which, 8), rows)
        self.local = [
            pltpu.make_async_copy(term.at[:, :, :, :, mine], held, local_sems.at[0]),
            pltpu.make_async_copy(
                total.at[of_core(at.core)], share.at[:, share_mine], local_sems.at[1]
            ),
        ]
        self.first = send(term.at[:, :, :, :, other], arrived[0], sems, 0, at.by_core)
        if x_first:
            self.second = send(held.at[:, :, 1 - at.x], arrived[1], sems, 1, at.by_x)
            self.third = send(held.at[:, 1 - at.y, at.x], arrived[2], sems, 2, at.by_y)
        else:
            self.second = send(held.at[:, 1 - at.y], arrived[1], sems, 1, at.by_y)
            self.third = send(held.at[:, at.y, 1 - at.x], arrived[2], sems, 2, at.by_x)
        self.over_z = [
            send(held.at[at.others[k][0], at.y, at.x], arrived[3].at[k], sems, 3 + k, at.others[k])
            for k in range(3)
        ]
        self.last = send(
            total.at[of_core(1 - at.core)], share.at[:, share_mine], sems, 6, at.by_core
        )

    def add(self, place, values):
        self.held[place] = (self.held[place].astype(f32) + values.astype(f32)).astype(low_type)

    def step(self, number):
        at = self.at
        if number == 0:
            self.local[0].start()
            self.first.start()
        elif number == 1:
            self.local[0].wait()
            self.first.wait()

            @pl.loop(0, 4)
            def _(row):
                for across in range(4):
                    place = (row, across // 2, across % 2)
                    self.add(place, self.arrived[0][place])

            self.second.start()
        elif number == 2:
            self.second.wait()

            @pl.loop(0, 4)
            def _(row):
                for across in range(2):
                    place = (row, across, at.x) if self.x_first else (row, at.y, across)
                    self.add(place, self.arrived[1][row, across])

            self.third.start()
        elif number == 3:
            self.third.wait()

            @pl.loop(0, 4)
            def _(row):
                self.add((row, at.y, at.x), self.arrived[2][row])

            for copy in self.over_z:
                copy.start()
        elif number == 4:
            for copy in self.over_z:
                copy.wait()
            total = self.held[at.seq, at.y, at.x].astype(f32)
            for k in range(3):
                total = total + self.arrived[3][k].astype(f32)
            self.total[...] = total
            self.local[1].start()
            self.last.start()
        else:
            self.local[1].wait()
            self.last.wait()


class Ring:
    def __init__(self, at, own, blocks, sems, local_sem):
        self.at = at
        seq = at.seq
        self.local = pltpu.make_async_copy(own, blocks.at[seq], local_sem)
        right, left = ((seq + 1) % 4, at.dp), ((seq + 3) % 4, at.dp)
        self.hops = []
        for hop in range(3):
            back, ahead = (seq + 4 - hop) % 4, (seq + hop) % 4
            block_back = own if hop == 0 else blocks.at[back]
            block_ahead = own if hop == 0 else blocks.at[ahead]
            self.hops.append(
                [
                    (
                        (seq >= hop) & (seq < 3),
                        send(block_back, blocks.at[back], sems, hop, right),
                        seq >= hop + 1,
                    ),
                    (
                        (seq + hop <= 3) & (seq > 0),
                        send(block_ahead, blocks.at[ahead], sems, 3 + hop, left),
                        seq + hop + 1 <= 3,
                    ),
                ]
            )

    def start(self, hop):
        if hop == 0:
            self.local.start()
        for sends, copy, _ in self.hops[hop]:
            pl.when(sends)(copy.start)

    def arrive(self, hop):
        for _, copy, receives in self.hops[hop]:
            pl.when(receives)(copy.wait_recv)

    def finish(self):
        for hop in self.hops:
            for sends, copy, _ in hop:
                pl.when(sends)(copy.wait_send)


X_FIRST = (True, False, False, True)


def remote_scratch(shapes):
    return [pltpu.SemaphoreType.DMA((2, 7)), pltpu.SemaphoreType.DMA((2,))] * len(shapes)


def opening_kernel(*refs):
    shards, own = refs[:4], refs[4]
    gains, bucket_rows, bias_table, lengths = refs[5:9]
    wholes, outs = refs[9:13], refs[13:21]
    normed_out, keys_out, values_out, keys_extra_out, queries, queries_t, context_t, log_total = outs
    extra = refs[21]
    scratch = refs[22:]
    pairs, lows, sems = scratch[:4], scratch[4:8], scratch[8:16]
    ring_sems, ring_local, out_sems, blocks, project, normed, keys, values_t = scratch[16:24]
    keys_extra, picks, sums, tops = scratch[24:]
    at = Place()
    at.greet()
    gathers = [
        Gather(
            at,
            shards[k],
            pairs[k],
            lows[k],
            project if k == 0 else wholes[k],
            sems[2 * k],
            sems[2 * k + 1],
            X_FIRST[k],
        )
        for k in range(4)
    ]
    first, rest = gathers[0], gathers[1:]
    ring = Ring(at, own, blocks, ring_sems, ring_local.at[0])

    def rest_step(number):
        for gather in rest:
            gather.step(number)

    for gather in gathers:
        gather.step(0)
    first.step(1)
    rest_step(1)

    count, buckets = own.shape[0], bias_table.shape[0]
    row_length = keys_extra.shape[0]
    query_blocks = count // BLK
    doc_start, one_start = extra_columns(query_blocks)
    picked = query_blocks * buckets
    ends = []
    for doc in range(DOCS):
        ends.append(lengths[0, doc] + (ends[-1] if ends else 0))

    def documents_at(position):
        return sum((position >= end).astype(jnp.int32) for end in ends)

    bucket_at = lax.broadcasted_iota(jnp.int32, (buckets, row_length), 0)
    for block in range(query_blocks):
        picks[buckets * block : buckets * block + buckets, :] = (
            (bucket_rows[block : block + 1, :] == bucket_at).astype(f32).astype(low_type)
        )
    last = picks.shape[0] - picked
    row = lax.broadcasted_iota(jnp.int32, (last, row_length), 0)
    key_doc = documents_at(lax.broadcasted_iota(jnp.int32, (last, row_length), 1))
    picks[picked:, :] = (
        jnp.where(row < DOCS, (key_doc != row).astype(f32), (row == DOCS).astype(f32))
    ).astype(low_type)

    table = jnp.concatenate([bias_table[...]] * query_blocks, axis=0)
    table_lane = lax.broadcasted_iota(jnp.int32, table.shape, 1)
    lane = lax.broadcasted_iota(jnp.int32, (picked, 128), 1)
    lane_block = lax.broadcasted_iota(jnp.int32, (picked, 128), 0) // buckets
    lane_last = lax.broadcasted_iota(jnp.int32, (last, 128), 1)
    row_last = lax.broadcasted_iota(jnp.int32, (last, 128), 0)
    below = jnp.where(
        (row_last < DOCS) & (lane_last - doc_start == row_last),
        masked_score,
        jnp.where(
            (row_last == DOCS) & (lane_last >= one_start) & (lane_last < one_start + TERMS), 1.0, 0.0
        ),
    ).astype(low_type)

    @pl.loop(0, PAIRS)
    def _(pair):
        sides = []
        for head in range(2):
            rest_of = jnp.sum(
                jnp.where(table_lane == 2 * pair + head, table, 0.0), axis=1, keepdims=True
            )
            side = jnp.zeros((picked, 128), f32)
            for term in range(TERMS):
                part = rest_of.astype(low_type).astype(f32)
                rest_of = rest_of - part
                side = jnp.where(lane == term * query_blocks + lane_block, part, side)
            sides.append(jnp.concatenate([side.astype(low_type), below], axis=0))
        keys_extra[:, pl.ds(pl.multiple_of(256 * pair, 256), 256)] = dot(
            picks[...], jnp.concatenate(sides, axis=1), 0, 0
        ).astype(low_type)

    extra_lane = lax.broadcasted_iota(jnp.int32, (count, 128), 1)
    extra_row = lax.broadcasted_iota(jnp.int32, (count, 128), 0)
    query_doc = documents_at(extra_row + at.seq * count)
    extra[...] = (
        (
            ((extra_lane < doc_start) & (extra_lane % query_blocks == extra_row // BLK))
            | ((extra_lane < one_start) & (extra_lane - doc_start == query_doc))
        )
        .astype(f32)
        .astype(low_type)
    )
    sums[...] = jnp.zeros_like(sums)
    tops[...] = jnp.full_like(tops, masked_score)

    first.step(2)
    ring.start(0)
    first.step(3)
    ring.local.wait()
    first.step(4)
    first.step(5)

    copies = [
        pltpu.make_async_copy(keys_extra, keys_extra_out, out_sems.at[0]),
        pltpu.make_async_copy(project, wholes[0], out_sems.at[1]),
    ]
    for copy in copies:
        copy.start()
    weights = [project[:, :, :, :, D * part : D * part + D].reshape(D, D) for part in range(3)]
    pair_lane = lax.broadcasted_iota(jnp.int32, (count, PAIR), 1)

    def attend_pair(block, pair):
        lanes = pl.ds(pl.multiple_of(pair * PAIR, PAIR), PAIR)
        key_rows = pl.ds(pl.multiple_of(block * count, count), count)
        query_pair, key_pair = queries[:, lanes], keys[block, :, lanes]
        for head in range(2):
            which = 2 * pair + head
            mine = (pair_lane < HEAD) if head == 0 else (pair_lane >= HEAD)
            query_side = jnp.concatenate(
                [jnp.where(mine, query_pair, jnp.zeros_like(query_pair)), extra[...]], axis=1
            )
            more = keys_extra[key_rows, pl.ds(pl.multiple_of(128 * which, 128), 128)]
            scores = dot(jnp.concatenate([key_pair, more], axis=1), query_side, 1, 1)
            top_before = tops[which, 0:1]
            top = jnp.maximum(top_before, jnp.max(scores, axis=0, keepdims=True))
            unscaled = jnp.exp(scores - top).astype(low_type)
            value_side = jnp.concatenate(
                [
                    values_t[block, pl.ds(pl.multiple_of(HEAD * which, HEAD), HEAD), :],
                    jnp.ones((16, count), low_type),
                ],
                axis=0,
            )
            sums[which] = sums[which] * jnp.exp(top_before - top) + dot(value_side, unscaled, 1, 0)
            tops[which] = jnp.broadcast_to(top, (8, count))

    side = at.seq // 2
    order = [at.seq, 1 - at.seq + 4 * side, 2 - side, 3 - 3 * side]
    events = {
        (0, 1): [lambda: (ring.arrive(0), ring.start(1))],
        (0, 3): [lambda: rest_step(2)],
        (1, 1): [lambda: rest_step(3)],
        (1, 5): [lambda: (ring.arrive(1), ring.start(2))],
        (2, 5): [lambda: (ring.arrive(2), rest_step(4))],
    }
    for slot, block in enumerate(order):
        values = blocks[block].astype(f32)
        normed_low = (
            values
            * lax.rsqrt(jnp.mean(values * values, axis=1, keepdims=True) + norm_epsilon)
            * gains[0:1, :]
        ).astype(low_type)
        normed[block] = normed_low
        keys[block] = dot(normed_low, weights[1], 1, 0).astype(low_type)
        values_t[block] = dot(weights[2], normed_low, 0, 1).astype(low_type)
        for place, (source, target) in enumerate(
            ((normed, normed_out), (keys, keys_out), (values_t, values_out))
        ):
            copy = pltpu.make_async_copy(
                source.at[block], target.at[block], out_sems.at[2 + 3 * slot + place]
            )
            copy.start()
            copies.append(copy)
        if slot == 0:
            scaled = lambda values: (values.astype(low_type).astype(f32) * score_scale).astype(low_type)
            queries[...] = scaled(dot(normed_low, weights[0], 1, 0))
            queries_t[...] = scaled(dot(weights[0], normed_low, 0, 1))

        @pl.loop(0, PAIRS)
        def _(pair, slot=slot, block=block):
            for (when, which), actions in events.items():
                if when == slot:

                    @pl.when(pair == which)
                    def _(actions=actions):
                        for action in actions:
                            action()

            attend_pair(block, pair)

    for head in range(HEADS):
        total = sums[head, HEAD : HEAD + 1]
        context_t[HEAD * head : HEAD * head + HEAD, :] = sums[head, :HEAD] / total
        log_total[head : head + 1, :] = tops[head, 0:1] + jnp.log(total)
    rest_step(5)
    ring.finish()
    for copy in copies:
        copy.wait()


def open_layer(shards, own, gains, bucket_rows, bias_table, lengths):
    low_shape = lambda shard: (2 * shard.shape[0], shard.shape[1] // 2)
    anywhere = pl.BlockSpec(memory_space=pl.ANY)
    in_place = pl.BlockSpec(memory_space=pltpu.VMEM)
    count, blocks = own.shape[0], bucket_rows.shape[0]
    row_length = 4 * count
    picked = blocks * bias_table.shape[0] + 16
    low = lambda *shape: jax.ShapeDtypeStruct(shape, low_type)
    whole_shapes = [(4, 2, 2, 2 * shard.shape[0], shard.shape[1]) for shard in shards]
    return pl.pallas_call(
        opening_kernel,
        out_shape=[low(*shape) for shape in whole_shapes]
        + [low(4, count, D)] * 2
        + [low(4, D, count), low(row_length, HEADS * 128), low(count, D), low(D, count)]
        + [jax.ShapeDtypeStruct((D, count), f32), jax.ShapeDtypeStruct((16, count), f32)]
        + [low(count, 128)],
        in_specs=[anywhere] * 5 + [in_place] * 3 + [pl.BlockSpec(memory_space=pltpu.SMEM)],
        out_specs=[anywhere] * 8 + [in_place] * 5,
        scratch_shapes=[pltpu.VMEM(low_shape(shard), f32) for shard in shards]
        + [pltpu.VMEM(low_shape(shard), low_type) for shard in shards]
        + remote_scratch(shards)
        + [
            pltpu.SemaphoreType.DMA((2, 6)),
            pltpu.SemaphoreType.DMA((1,)),
            pltpu.SemaphoreType.DMA((14,)),
            pltpu.VMEM((4, count, D), low_type),
            pltpu.VMEM(whole_shapes[0], low_type),
            pltpu.VMEM((4, count, D), low_type),
            pltpu.VMEM((4, count, D), low_type),
            pltpu.VMEM((4, D, count), low_type),
            pltpu.VMEM((row_length, HEADS * 128), low_type),
            pltpu.VMEM((picked, row_length), low_type),
            pltpu.VMEM((HEADS, HEAD + 16, count), f32),
            pltpu.VMEM((HEADS, 8, count), f32),
        ],
        compiler_params=pltpu.CompilerParams(
            collective_id=0, has_side_effects=True, vmem_limit_bytes=vmem_bytes
        ),
        name="open_layer",
    )(*shards, own, gains, bucket_rows, bias_table, lengths)


def scatter_scratch(terms, plans):
    buffers, sems = [], []
    for term, (_, width, _, _) in zip(terms, plans):
        rows, half = term.shape[3], width // 2
        buffers += [
            pltpu.VMEM((4, 2, 2, rows, half), low_type),
            pltpu.VMEM((4, 2, 2, rows, half), low_type),
            pltpu.VMEM((4, 2, rows, half), low_type),
            pltpu.VMEM((4, rows, half), low_type),
            pltpu.VMEM((3, rows, half), low_type),
            pltpu.VMEM((rows, half), f32),
        ]
        sems += [pltpu.SemaphoreType.DMA((2, 7)), pltpu.SemaphoreType.DMA((2,))]
    return buffers + sems


def make_scatters(at, plans, terms, shares, scratch):
    buffers, sems = scratch[: 6 * len(plans)], scratch[6 * len(plans) :]
    return [
        Scatter(
            at,
            plans[k],
            terms[k],
            shares[k],
            buffers[6 * k : 6 * k + 6],
            sems[2 * k : 2 * k + 2],
        )
        for k in range(len(plans))
    ]


def by_chip(term):
    return term.reshape(4, 2, 2, term.shape[0] // 16, term.shape[1])


class AllSum:
    def __init__(self, at, own, arrived, summed, rows, sems):
        self.at, self.own, self.arrived, self.summed, self.rows = at, own, arrived, summed, rows
        place = rows.at[at.seq]
        self.by_core = send(own, arrived.at[0], sems, 0, at.by_core)
        self.by_x = send(summed.at[0], arrived.at[1], sems, 1, at.by_x)
        self.by_y = send(summed.at[1], arrived.at[2], sems, 2, at.by_y)
        self.over_z = [send(place, place, sems, 3 + k, at.others[k]) for k in range(3)]

    def step(self, number):
        if number == 0:
            self.by_core.start()
        elif number == 1:
            self.by_core.wait()
            self.summed[0] = self.own[...] + self.arrived[0]
            self.by_x.start()
        elif number == 2:
            self.by_x.wait()
            self.summed[1] = self.summed[0] + self.arrived[1]
            self.by_y.start()
        elif number == 3:
            self.by_y.wait()
            self.rows[self.at.seq] = self.summed[1] + self.arrived[2]
            for copy in self.over_z:
                copy.start()
        else:
            for copy in self.over_z:
                copy.wait()

    def total(self):
        return (self.rows[0] + self.rows[1]) + (self.rows[2] + self.rows[3])


def sum_scratch(width):
    return [
        pltpu.VMEM((8, width), f32),
        pltpu.VMEM((3, 8, width), f32),
        pltpu.VMEM((2, 8, width), f32),
        pltpu.VMEM((4, 8, width), f32),
        pltpu.SemaphoreType.DMA((2, 6)),
    ]


FINISH_PLANS = ((0, D, 0, True), (0, D, D, False), (0, D, 2 * D, True))


def statistics(gradient, previous):
    squares = gradient * gradient + tiny_term
    rows_new = decay_rate * previous + (1.0 - decay_rate) * jnp.mean(squares, axis=1, keepdims=True)
    return (
        rows_new,
        jnp.sum(squares, axis=0, keepdims=True),
        jnp.sum(rows_new, axis=0, keepdims=True),
    )


def finish_kernel(scale, *refs):
    terms, shares = refs[:3], refs[3:6]
    weights, rows_before, columns_before = refs[6:10], refs[10:14], refs[14:18]
    gain_two, table_part, gains, moments, own_gains, own_weight = refs[18:24]
    refs = refs[24:]
    gradients, updated, rows_after, columns_after = refs[:4], refs[4:8], refs[8:12], refs[12:16]
    gains_gradient, gains_updated, moments_after, table_total = refs[16:20]
    scratch = refs[20:]
    share = scratch[0]
    early, late = scratch[1:6], scratch[6:11]
    at = Place()
    at.greet()
    scatters = make_scatters(at, FINISH_PLANS, terms, [share] * 3, scratch[11:])
    first, second = AllSum(at, *early), AllSum(at, *late)
    for scatter in scatters:
        scatter.step(0)

    row_counts = [16 * 2 * weight.shape[0] for weight in weights]
    early_own, late_own = early[0], late[0]
    early_own[...] = jnp.zeros_like(early_own)
    late_own[...] = jnp.zeros_like(late_own)
    rows_new, row_sums = [None] * 4, [None] * 4

    def take(position, raw):
        gradient = raw * scale
        gradients[position][...] = gradient
        rows_new[position], columns, row_sum = statistics(gradient, rows_before[position][...])
        rows_after[position][...] = rows_new[position]
        return columns, jnp.broadcast_to(row_sum, (1, 128))

    for position, row in ((1, 0), (2, 1), (3, 2)):
        columns, row_sum = take(position, shares[position - 1][...])
        early_own[row : row + 1, D + 128 : D + 256] = row_sum
        if position == 1:
            early_own[0:1, :D] = columns
        elif position == 3:
            early_own[1:2, :D] = columns
        else:
            for part in range(4):
                early_own[4 + part : 5 + part, :D] = columns[:, D * part : D * part + D]
    early_own[2:3, :D] = gain_two[...]
    early_own[:, D : D + 128] = table_part[...]

    def finish(position, columns, row_sum):
        columns_new = decay_rate * columns_before[position][...] + (1.0 - decay_rate) * (
            columns / row_counts[position]
        )
        columns_after[position][...] = columns_new
        row_mean = row_sum / row_counts[position]
        denominator = rows_new[position] * columns_new / row_mean
        updated[position][...] = weights[position][...] - learn_rate * gradients[position][
            ...
        ] * lax.rsqrt(denominator)

    for number in range(5):
        first.step(number)
        for scatter in scatters:
            scatter.step(number + 1)

    raw = share[...]
    columns, row_sum = take(0, raw)
    for part in range(3):
        late_own[part : part + 1, :D] = columns[:, D * part : D * part + D]
    late_own[4:5, :128] = row_sum
    gain_one = (
        jnp.sum(raw * own_weight[...].astype(low_type).astype(f32), axis=1, keepdims=True)
        / own_gains[...]
    )
    rows = gain_one.shape[0]
    lane = lax.broadcasted_iota(jnp.int32, (rows, D), 1)
    row = lax.broadcasted_iota(jnp.int32, (rows, D), 0)
    start = (at.seq * 8 + at.dp) * rows
    late_own[3:4, :] = jnp.sum(
        jnp.where(lane == row + start, jnp.broadcast_to(gain_one, (rows, D)), 0.0),
        axis=0,
        keepdims=True,
    )
    second.step(0)
    sums = first.total()
    finish(1, sums[0:1, :D], sums[0:1, D + 128 : D + 129])
    table_total[...] = sums[:, D : D + 128]
    second.step(1)
    finish(3, sums[1:2, :D], sums[2:3, D + 128 : D + 129])
    second.step(2)
    finish(
        2,
        jnp.concatenate([sums[4 + part : 5 + part, :D] for part in range(4)], axis=1),
        sums[1:2, D + 128 : D + 129],
    )
    second.step(3)
    second.step(4)
    sums_late = second.total()
    finish(
        0,
        jnp.concatenate([sums_late[part : part + 1] for part in range(3)], axis=1),
        sums_late[4:5, 0:1],
    )
    gradient = jnp.concatenate([sums_late[3:4], sums[2:3, :D]], axis=0) * scale
    moment = decay_rate * moments[...] + (1.0 - decay_rate) * (gradient * gradient + tiny_term)
    gains_gradient[...] = gradient
    moments_after[...] = moment
    gains_updated[...] = gains[...] - learn_rate * gradient * lax.rsqrt(moment)


def finish(scale, terms, shares, weights, rows_before, columns_before, rest):
    in_place = pl.BlockSpec(memory_space=pltpu.VMEM)
    anywhere = pl.BlockSpec(memory_space=pl.ANY)
    shapes = [weight.shape for weight in weights]
    out_shapes = (
        shapes
        + shapes
        + [(rows, 1) for rows, _ in shapes]
        + [(1, columns) for _, columns in shapes]
        + [(2, D)] * 3
        + [(8, 128)]
    )
    terms = [by_chip(term) for term in terms]
    return pl.pallas_call(
        functools.partial(finish_kernel, scale),
        out_shape=[jax.ShapeDtypeStruct(shape, f32) for shape in out_shapes],
        in_specs=[anywhere] * 3 + [in_place] * (3 + 12 + 6),
        out_specs=[in_place] * len(out_shapes),
        scratch_shapes=[pltpu.VMEM(shapes[0], f32)]
        + sum_scratch(D + 256)
        + sum_scratch(D)
        + scatter_scratch(terms, FINISH_PLANS),
        compiler_params=pltpu.CompilerParams(
            collective_id=2, has_side_effects=True, vmem_limit_bytes=vmem_bytes
        ),
        cost_estimate=pl.CostEstimate(
            flops=30 * 10**9, bytes_accessed=30 * 10**6, transcendentals=10**6
        ),
        name="finish",
    )(*terms, *shares, *weights, *rows_before, *columns_before, *rest)


BACK_TERMS = (1, 2, 1, 2, 0)
BACK_PLANS = (
    (0, 1536, 0, False),
    (0, 512, 0, True),
    (1536, 1536, 1536, False),
    (512, 256, 512, True),
    (0, D, 0, True),
)
EARLY, LATE = (0, 1), (2, 3, 4)
BACK_TIMES = (
    (0, None),
    (0, (EARLY, 0)),
    (1, (LATE, 0)),
    (2, (EARLY, 1)),
    (7, (EARLY, 2)),
    (7, (LATE, 1)),
    (12, (EARLY, 3)),
    (14, (LATE, 2)),
    (17, (EARLY, 4)),
    (17, (LATE, 3)),
    (19, (EARLY, 5)),
    (22, (LATE, 4)),
    (23, (LATE, 5)),
)


def backward_kernel(
    queries,
    query_rows,
    delta_rows,
    context_grad,
    queries_t,
    context_grad_t,
    keys,
    values_t,
    keys_extra,
    *refs,
):
    if len(refs) > 4:
        terms, refs = refs[:3], refs[3:]
        shares, scratch = refs[4:7], refs[7:]
        at = Place()
        scatters = make_scatters(
            at,
            BACK_PLANS,
            [terms[which] for which in BACK_TERMS],
            [shares[which] for which in BACK_TERMS],
            scratch,
        )
        now = pl.program_id(0) * pl.num_programs(1) + pl.program_id(1)
        for when, doing in BACK_TIMES:

            @pl.when(now == when)
            def _(doing=doing):
                if doing is None:
                    at.greet()
                else:
                    for which in doing[0]:
                        scatters[which].step(doing[1])

    query_grad, key_grad_t, value_grad_t, folded = refs[:4]
    step = pl.program_id(1)
    count, amount = queries.shape[0], keys.shape[0]
    lane = lax.broadcasted_iota(jnp.int32, (count, PAIR), 1)
    query_pair, grad_pair = queries[...], context_grad[...]
    zeros = jnp.zeros_like(query_pair)

    @pl.when(step == 0)
    def _():
        query_grad[...] = jnp.zeros_like(query_grad)

    query_grads = []
    for head in range(2):
        mine = (lane < HEAD) if head == 0 else (lane >= HEAD)
        rows = pl.ds(HEAD * head, HEAD)
        more = keys_extra[:, 128 * head : 128 * head + 128]
        query_side = jnp.concatenate([jnp.where(mine, query_pair, zeros), query_rows[head]], axis=1)
        grad_side = jnp.concatenate([jnp.where(mine, grad_pair, zeros), delta_rows[head]], axis=1)
        key_side = jnp.concatenate([keys[...], more], axis=1)
        value_side = jnp.concatenate(
            [values_t[0], jnp.ones((128, amount), low_type)], axis=0
        )
        attention = jnp.exp(dot(query_side, key_side, 1, 1))
        score_grad = attention * dot(grad_side, value_side, 1, 0)
        attention_low = attention.astype(low_type)
        score_low = score_grad.astype(low_type)
        for block in range(count // BLK):
            folded[head, pl.ds(block, 1), :] = jnp.sum(
                score_grad[BLK * block : BLK * block + BLK], axis=0, keepdims=True
            )
        query_grads.append(dot(score_low, keys[...], 1, 0))
        value_grad_t[rows, :] = dot(context_grad_t[rows, :], attention_low, 1, 0).astype(low_type)
        key_grad_t[rows, :] = dot(queries_t[rows, :], score_low, 1, 0).astype(low_type)
    query_grad[...] += jnp.where(lane < HEAD, query_grads[0], query_grads[1])


def attend_back(
    queries,
    query_rows,
    delta_rows,
    context_grad,
    queries_t,
    context_grad_t,
    keys,
    values_t,
    keys_extra,
    terms,
):
    terms = [by_chip(term) for term in terms]
    anywhere = [pl.BlockSpec(memory_space=pl.ANY)] * len(terms)
    remote = {"collective_id": 1, "has_side_effects": True} if terms else {}
    count, row_length = queries.shape[0], keys.shape[0]
    blocks = count // BLK
    of_pair = pl.BlockSpec((count, PAIR), lambda pair, step: (0, pair))
    of_pair_t = pl.BlockSpec((PAIR, count), lambda pair, step: (pair, 0))
    of_heads = pl.BlockSpec((2, count, 128), lambda pair, step: (pair, 0, 0))
    key_t = pl.BlockSpec((PAIR, back_step), lambda pair, step: (pair, step))
    return pl.pallas_call(
        backward_kernel,
        grid=(PAIRS, row_length // back_step),
        out_shape=[
            jax.ShapeDtypeStruct((count, D), f32),
            jax.ShapeDtypeStruct((D, row_length), low_type),
            jax.ShapeDtypeStruct((D, row_length), low_type),
            jax.ShapeDtypeStruct((HEADS, blocks, row_length), f32),
        ]
        + [jax.ShapeDtypeStruct((term.shape[3] // 2, term.shape[4]), f32) for term in terms],
        in_specs=[
            of_pair,
            of_heads,
            of_heads,
            of_pair,
            of_pair_t,
            of_pair_t,
            pl.BlockSpec((back_step, PAIR), lambda pair, step: (step, pair)),
            pl.BlockSpec((1, PAIR, back_step), lambda pair, step: (step, pair, 0)),
            pl.BlockSpec((back_step, 256), lambda pair, step: (step, pair)),
        ]
        + anywhere,
        out_specs=[
            of_pair,
            key_t,
            key_t,
            pl.BlockSpec((2, blocks, back_step), lambda pair, step: (pair, 0, step)),
        ]
        + anywhere,
        scratch_shapes=scatter_scratch([terms[which] for which in BACK_TERMS], BACK_PLANS)
        if terms
        else [],
        compiler_params=pltpu.CompilerParams(vmem_limit_bytes=vmem_bytes, **remote),
        cost_estimate=pl.CostEstimate(
            flops=10 * HEADS * count * row_length * 200,
            bytes_accessed=HEADS * row_length * 2048,
            transcendentals=HEADS * count * row_length,
        ),
        name="attention_backward",
    )(
        queries,
        query_rows,
        delta_rows,
        context_grad,
        queries_t,
        context_grad_t,
        keys,
        values_t,
        keys_extra,
        *terms,
    )


def body(
    hidden_states,
    output_cotangent,
    document_lengths,
    bucket_index,
    norm_gains,
    bias_table,
    project_weight,
    output_weight,
    expand_weight,
    reduce_weight,
    project_rows,
    project_columns,
    output_rows,
    output_columns,
    expand_rows,
    expand_columns,
    reduce_rows,
    reduce_columns,
    gains_moment,
    table_moment,
):
    every = ("seq", "dp")
    local_rows = hidden_states.shape[1]
    row_length = local_rows * lax.axis_size("seq")
    gradient_scale = 1.0 / math.sqrt(row_length * lax.axis_size("dp"))
    place = lax.axis_index("seq")
    blocks = local_rows // BLK

    shards = (project_weight, output_weight, expand_weight, reduce_weight)
    direct = (
        lax.axis_size("seq") == 4
        and lax.axis_size("dp") == 8
        and all(shard.shape[0] % 8 == 0 and shard.shape[1] % 256 == 0 for shard in shards)
    )
    inputs = hidden_states[0].astype(f32)
    if direct:
        opened = open_layer(
            shards, hidden_states[0], norm_gains, bucket_index[0], bias_table, document_lengths
        )
        project_full, output_full, expand_full, reduce_full = (
            whole.reshape(-1, whole.shape[4]) for whole in opened[:4]
        )
        normed_all, keys = (blocks_of.reshape(row_length, D) for blocks_of in opened[4:6])
        values_t, keys_extra, queries, queries_t, context_t, log_total, extra = opened[6:]
        log_total = log_total[:HEADS]
        normed_low = lax.dynamic_slice_in_dim(normed_all, place * local_rows, local_rows)
    else:
        project_full, output_full, expand_full, reduce_full = (
            lax.all_gather(shard.astype(low_type), every, axis=0, tiled=True) for shard in shards
        )
        row_states = lax.all_gather(hidden_states[0], "seq", axis=0, tiled=True)
        normed_low = rms_norm(inputs, norm_gains[0]).astype(low_type)
        normed_all = rms_norm(row_states.astype(f32), norm_gains[0]).astype(low_type)
        doc_all = documents(document_lengths[0], row_length)
        doc_query = lax.dynamic_slice_in_dim(doc_all, place * local_rows, local_rows)
        picks = key_picks(bucket_index[0], doc_all, bias_table.shape[0])
        keys_extra = key_extra(picks, bias_table, blocks)
        extra = query_extra(doc_query, blocks)
        scaled = lambda values: (values.astype(low_type).astype(f32) * score_scale).astype(low_type)
        queries = scaled(dot(normed_low, project_full[:, :D], 1, 0))
        queries_t = scaled(dot(project_full[:, :D], normed_low, 0, 1))
        keys = dot(normed_all, project_full[:, D : 2 * D], 1, 0).astype(low_type)
        values_t = dot(project_full[:, 2 * D :], normed_all, 0, 1).astype(low_type)
        context_t, log_total = attend(queries, extra, keys, values_t, keys_extra)
        log_total = log_total.reshape(HEADS, 8, local_rows)[:, 0]
        values_t = jnp.transpose(values_t.reshape(D, -1, local_rows), (1, 0, 2))
    _, pullback_one = jax.vjp(rms_norm, inputs, norm_gains[0])
    query_weight, key_weight, value_weight = (
        project_full[:, :D],
        project_full[:, D : 2 * D],
        project_full[:, 2 * D :],
    )
    context_low_t = context_t.astype(low_type)
    residual = inputs + dot(context_low_t, output_full, 0, 0)
    normed_two, pullback_two = jax.vjp(rms_norm, residual, norm_gains[1])
    normed_two_low = normed_two.astype(low_type)
    expanded = dot(normed_two_low, expand_full, 1, 0)
    activated, pullback_gelu = jax.vjp(gelu_tanh, expanded)
    activated_low = activated.astype(low_type)
    layer_output = (residual + dot(activated_low, reduce_full, 1, 0)).astype(low_type)[None]

    upstream_low = output_cotangent[0].astype(low_type)
    upstream = upstream_low.astype(f32)
    reduce_term = dot(activated_low, upstream_low, 0, 0)
    (expanded_grad,) = pullback_gelu(dot(upstream_low, reduce_full, 1, 1))
    expanded_low = expanded_grad.astype(low_type)
    expand_term = dot(normed_two_low, expanded_low, 0, 0)
    residual_part, gain_two_grad = pullback_two(dot(expanded_low, expand_full, 1, 1))
    residual_grad = upstream + residual_part
    residual_low = residual_grad.astype(low_type)
    output_term = dot(context_low_t, residual_low, 1, 0)
    context_grad = dot(residual_low, output_full, 1, 1).astype(low_type)
    context_grad_t = dot(output_full, residual_low, 1, 1).astype(low_type)
    delta = jnp.sum(
        (context_grad_t.astype(f32) * context_t).reshape(HEADS, HEAD, local_rows), axis=1
    )

    query_grad, key_grad_t, value_grad_t, folded, *rest_shares = attend_back(
        queries,
        with_row_terms(extra, -log_total, blocks),
        with_row_terms(jnp.zeros_like(extra), -delta, blocks),
        context_grad,
        queries_t,
        context_grad_t,
        keys,
        values_t,
        keys_extra,
        [term.astype(low_type) for term in (output_term, expand_term, reduce_term)]
        if direct
        else [],
    )
    buckets = bias_table.shape[0]
    one_hot = (
        bucket_index[0].T[:, :, None] == jnp.arange(buckets, dtype=jnp.int32)[None, None, :]
    ).reshape(row_length, blocks * buckets)
    picked = jnp.dot(
        folded.reshape(HEADS * blocks, row_length),
        one_hot.astype(f32),
        precision=lax.Precision.HIGHEST,
    )
    table_grad = jnp.einsum("hkkb->bh", picked.reshape(HEADS, blocks, blocks, buckets))

    query_grad_low = (query_grad * score_scale).astype(low_type)
    project_terms = [
        term.astype(low_type)
        for term in (
            dot(normed_low, query_grad_low, 0, 0),
            dot(normed_all, key_grad_t, 0, 1),
            dot(normed_all, value_grad_t, 0, 1),
        )
    ]
    key_part = dot(key_grad_t, key_weight, 0, 1) + dot(value_grad_t, value_weight, 0, 1)
    key_part = lax.psum_scatter(
        key_part.astype(low_type), "seq", scatter_dimension=0, tiled=True
    ).astype(f32)
    input_part, gain_one_grad = pullback_one(dot(query_grad_low, query_weight, 1, 1) + key_part)
    input_gradient = (residual_grad + input_part).astype(low_type)[None]

    if direct:
        rows_of = lambda array: array[:, None]
        own_rows = project_weight.shape[0]
        own_gains = lax.dynamic_slice_in_dim(
            norm_gains[0], (place * lax.axis_size("dp") + lax.axis_index("dp")) * own_rows, own_rows
        )
        table_part = jnp.pad(
            jnp.pad(table_grad, ((0, 0), (0, 16 - HEADS))).reshape(-1, 128), ((0, 4), (0, 0))
        )
        results = finish(
            gradient_scale,
            project_terms,
            rest_shares,
            shards,
            [rows_of(rows) for rows in (project_rows, output_rows, expand_rows, reduce_rows)],
            [
                columns[None]
                for columns in (project_columns, output_columns, expand_columns, reduce_columns)
            ],
            (
                gain_two_grad[None],
                table_part,
                norm_gains,
                gains_moment,
                rows_of(own_gains),
                project_weight,
            ),
        )
        gradients, updated_weights = results[:4], results[4:8]
        row_after = [rows[:, 0] for rows in results[8:12]]
        columns_after = [columns[0] for columns in results[12:16]]
        gains_gradient, gains_updated, gains_moment_new, table_total = results[16:]
        table_gradient = (
            table_total[:4].reshape(buckets, 16)[:, :HEADS] * gradient_scale
        )
        table_moment_new = decay_rate * table_moment + (1.0 - decay_rate) * (
            table_gradient * table_gradient + tiny_term
        )
        table_updated = bias_table - learn_rate * table_gradient * lax.rsqrt(table_moment_new)
        return (
            layer_output,
            input_gradient,
            gains_gradient,
            table_gradient,
            *gradients,
            gains_updated,
            table_updated,
            *updated_weights,
            row_after[0],
            columns_after[0],
            row_after[1],
            columns_after[1],
            row_after[2],
            columns_after[2],
            row_after[3],
            columns_after[3],
            gains_moment_new,
            table_moment_new,
        )

    terms = [
        term.astype(low_type)
        for term in (jnp.concatenate(project_terms, axis=1), output_term, expand_term, reduce_term)
    ]
    shares = [
        lax.psum_scatter(term, every, scatter_dimension=0, tiled=True).astype(f32)
        for term in terms
    ]
    gradients = tuple((share * gradient_scale for share in shares))
    row_before = (project_rows, output_rows, expand_rows, reduce_rows)
    row_after = []
    column_parts = []
    row_sums = []
    for gradient, previous in zip(gradients, row_before):
        squares = gradient * gradient + tiny_term
        updated_rows = decay_rate * previous + (1.0 - decay_rate) * jnp.mean(squares, axis=1)
        row_after.append(updated_rows)
        column_parts.append(jnp.sum(squares, axis=0))
        row_sums.append(jnp.sum(updated_rows))
    summed = lax.psum(
        (
            column_parts[0],
            column_parts[1],
            column_parts[2],
            column_parts[3],
            jnp.stack(row_sums),
            jnp.stack([gain_one_grad, gain_two_grad]),
            table_grad,
        ),
        every,
    )
    column_before = (project_columns, output_columns, expand_columns, reduce_columns)
    weights_before = (project_weight, output_weight, expand_weight, reduce_weight)
    full_rows = (
        project_full.shape[0],
        output_full.shape[0],
        expand_full.shape[0],
        reduce_full.shape[0],
    )
    updated_weights = []
    columns_after = []
    for position in range(4):
        columns_new = decay_rate * column_before[position] + (1.0 - decay_rate) * (
            summed[position] / full_rows[position]
        )
        row_mean = summed[4][position] / full_rows[position]
        denominator = row_after[position][:, None] * columns_new[None, :] / row_mean
        updated_weights.append(
            weights_before[position] - learn_rate * gradients[position] * lax.rsqrt(denominator)
        )
        columns_after.append(columns_new)
    gains_gradient = summed[5] * gradient_scale
    table_gradient = summed[6] * gradient_scale
    gains_moment_new = decay_rate * gains_moment + (1.0 - decay_rate) * (
        gains_gradient * gains_gradient + tiny_term
    )
    gains_updated = norm_gains - learn_rate * gains_gradient * lax.rsqrt(gains_moment_new)
    table_moment_new = decay_rate * table_moment + (1.0 - decay_rate) * (
        table_gradient * table_gradient + tiny_term
    )
    table_updated = bias_table - learn_rate * table_gradient * lax.rsqrt(table_moment_new)
    return (
        layer_output,
        input_gradient,
        gains_gradient,
        table_gradient,
        gradients[0],
        gradients[1],
        gradients[2],
        gradients[3],
        gains_updated,
        table_updated,
        updated_weights[0],
        updated_weights[1],
        updated_weights[2],
        updated_weights[3],
        row_after[0],
        columns_after[0],
        row_after[1],
        columns_after[1],
        row_after[2],
        columns_after[2],
        row_after[3],
        columns_after[3],
        gains_moment_new,
        table_moment_new,
    )


def solution(mesh):
    placed = (
        P("dp", "seq", None),
        P("dp", "seq", None),
        P("dp", None),
        P("dp", "seq", None),
        P(),
        P(),
        P(("seq", "dp"), None),
        P(("seq", "dp"), None),
        P(("seq", "dp"), None),
        P(("seq", "dp"), None),
        P(("seq", "dp")),
        P(),
        P(("seq", "dp")),
        P(),
        P(("seq", "dp")),
        P(),
        P(("seq", "dp")),
        P(),
        P(),
        P(),
    )
    return jax.shard_map(
        body,
        mesh=mesh,
        in_specs=placed,
        out_specs=(
            P("dp", "seq", None),
            P("dp", "seq", None),
            P(),
            P(),
            P(("seq", "dp"), None),
            P(("seq", "dp"), None),
            P(("seq", "dp"), None),
            P(("seq", "dp"), None),
            P(),
            P(),
            P(("seq", "dp"), None),
            P(("seq", "dp"), None),
            P(("seq", "dp"), None),
            P(("seq", "dp"), None),
            P(("seq", "dp")),
            P(),
            P(("seq", "dp")),
            P(),
            P(("seq", "dp")),
            P(),
            P(("seq", "dp")),
            P(),
            P(),
            P(),
        ),
        check_vma=False,
    )
```

```python
import functools
import math

import jax
import jax.numpy as jnp
from jax import lax
from jax.experimental import pallas as pl
from jax.experimental.pallas import tpu as pltpu
from jax.sharding import PartitionSpec as P

D = 768
HEADS = 12
HEAD = 64
BLK = 128
PAIR = 2 * HEAD
PAIRS = HEADS // 2
DOCS = 5
TERMS = 3

score_scale = 0.125
masked_score = -1e30
norm_epsilon = 1e-06
tiny_term = 1e-30
learn_rate = 0.3
decay_rate = 1.0 - 2.0 ** (-0.8)
vmem_bytes = 56 * 2**20
open_vmem = 48 * 2**20
back_vmem = 48 * 2**20
close_vmem = 48 * 2**20
apply_vmem = 16 * 2**20

low_type = jnp.bfloat16
f32 = jnp.float32


def dot(former, latter, former_axis, latter_axis):
    return lax.dot_general(
        former,
        latter,
        (((former_axis,), (latter_axis,)), ((), ())),
        preferred_element_type=f32,
    )


def rms_norm(values, gain_vector):
    return (
        values
        * lax.rsqrt(jnp.mean(values * values, axis=-1, keepdims=True) + norm_epsilon)
        * gain_vector
    )


def gelu_tanh(values):
    return (
        0.5
        * values
        * (1.0 + jnp.tanh(0.7978845608028654 * (values + 0.044715 * values * values * values)))
    )


def documents(lengths, row_length):
    doc_ends = jnp.cumsum(lengths)
    position = jnp.arange(row_length, dtype=jnp.int32)
    return jnp.sum((position[:, None] >= doc_ends[None, :]).astype(jnp.int32), axis=1)


def split_terms(values):
    terms = []
    rest = values
    for _ in range(TERMS):
        term = lax.reduce_precision(rest, 8, 7)
        terms.append(term)
        rest = rest - term
    return terms


def extra_columns(blocks):
    return TERMS * blocks, TERMS * blocks + DOCS


def query_extra(doc_query, blocks):
    count = doc_query.shape[0]
    doc_start, one_start = extra_columns(blocks)
    lane = lax.broadcasted_iota(jnp.int32, (count, 128), 1)
    block = lax.broadcasted_iota(jnp.int32, (count, 128), 0) // BLK
    is_block = (lane < doc_start) & (lane % blocks == block)
    is_doc = (lane >= doc_start) & (lane < one_start) & (lane - doc_start == doc_query[:, None])
    return (is_block | is_doc).astype(low_type)


def key_picks(bucket_rows, doc_all, buckets):
    blocks, row_length = bucket_rows.shape
    one_hot = (
        bucket_rows.T[:, :, None] == jnp.arange(buckets, dtype=jnp.int32)[None, None, :]
    ).reshape(row_length, blocks * buckets)
    other_doc = doc_all[:, None] != jnp.arange(DOCS, dtype=jnp.int32)[None, :]
    ones = jnp.ones((row_length, 1), jnp.bool_)
    return jnp.concatenate([one_hot, other_doc, ones], axis=1).astype(low_type)


def key_extra(picks, bias_table, blocks):
    buckets = bias_table.shape[0]
    doc_start, one_start = extra_columns(blocks)
    terms = jnp.stack(split_terms(bias_table), axis=0)
    lane = jnp.arange(128, dtype=jnp.int32)
    place = jnp.clip(lane // blocks, 0, TERMS - 1)
    spread = jnp.transpose(terms[place], (1, 2, 0))
    at_block = (lane[None, :] % blocks == jnp.arange(blocks, dtype=jnp.int32)[:, None]) & (
        lane[None, :] < doc_start
    )
    bias_part = jnp.where(at_block[:, None, None, :], spread[None], 0.0).reshape(
        blocks * buckets, HEADS, 128
    )
    doc_part = jnp.where(
        lane[None, :] - doc_start == jnp.arange(DOCS, dtype=jnp.int32)[:, None], masked_score, 0.0
    )
    one_part = ((lane >= one_start) & (lane < one_start + TERMS)).astype(f32)[None]
    rest = jnp.concatenate([doc_part, one_part], axis=0)
    rest = jnp.broadcast_to(rest[:, None, :], (DOCS + 1, HEADS, 128))
    whole = jnp.concatenate([bias_part, rest], axis=0).reshape(-1, HEADS * 128).astype(low_type)
    return dot(picks, whole, 1, 0).astype(low_type)


def forward_kernel(queries, extra, keys, values_t, keys_extra, context_t, log_total):
    count = queries.shape[0]
    lane = lax.broadcasted_iota(jnp.int32, (count, PAIR), 1)
    query_pair = queries[...]
    for head in range(2):
        mine = (lane < HEAD) if head == 0 else (lane >= HEAD)
        query_side = jnp.concatenate(
            [jnp.where(mine, query_pair, jnp.zeros_like(query_pair)), extra[...]], axis=1
        )
        key_side = jnp.concatenate([keys[...], keys_extra[:, 128 * head : 128 * head + 128]], axis=1)
        scores = dot(key_side, query_side, 1, 1)
        top = jnp.max(scores, axis=0, keepdims=True)
        unscaled = jnp.exp(scores - top).astype(low_type)
        value_side = jnp.concatenate(
            [
                values_t[HEAD * head : HEAD * head + HEAD, :],
                jnp.ones((16, unscaled.shape[0]), low_type),
            ],
            axis=0,
        )
        weighted = dot(value_side, unscaled, 1, 0)
        total = weighted[HEAD : HEAD + 1]
        context_t[pl.ds(HEAD * head, HEAD), :] = weighted[:HEAD] / total
        log_total[pl.ds(8 * head, 8), :] = jnp.broadcast_to(top + jnp.log(total), (8, count))


def attend(queries, extra, keys, values_t, keys_extra):
    count, row_length = queries.shape[0], keys.shape[0]
    return pl.pallas_call(
        forward_kernel,
        grid=(PAIRS,),
        out_shape=[
            jax.ShapeDtypeStruct((D, count), f32),
            jax.ShapeDtypeStruct((HEADS * 8, count), f32),
        ],
        in_specs=[
            pl.BlockSpec((count, PAIR), lambda pair: (0, pair)),
            pl.BlockSpec((count, 128), lambda pair: (0, 0)),
            pl.BlockSpec((row_length, PAIR), lambda pair: (0, pair)),
            pl.BlockSpec((PAIR, row_length), lambda pair: (pair, 0)),
            pl.BlockSpec((row_length, 256), lambda pair: (0, pair)),
        ],
        out_specs=[
            pl.BlockSpec((PAIR, count), lambda pair: (pair, 0)),
            pl.BlockSpec((16, count), lambda pair: (pair, 0)),
        ],
        compiler_params=pltpu.CompilerParams(vmem_limit_bytes=vmem_bytes),
        cost_estimate=pl.CostEstimate(
            flops=4 * HEADS * count * row_length * 256,
            bytes_accessed=HEADS * row_length * 1024,
            transcendentals=HEADS * count * row_length,
        ),
        name="attention_forward",
    )(queries, extra, keys, values_t, keys_extra)


MESH = pl.DeviceIdType.MESH


class Place:
    def __init__(self):
        self.seq, self.dp = lax.axis_index("seq"), lax.axis_index("dp")
        self.core, self.x, self.y = self.dp % 2, self.dp // 2 % 2, self.dp // 4
        self.by_core = (self.seq, self.dp + 1 - 2 * self.core)
        self.by_x = (self.seq, self.dp + 2 - 4 * self.x)
        self.by_y = (self.seq, self.dp + 4 - 8 * self.y)
        self.plane = [(self.seq, (self.dp + step) % 8) for step in range(1, 8)]
        self.others = [((self.seq + step) % 4, self.dp) for step in (1, 2, 3)]

    def turn(self, block):
        flip = 3 - self.seq
        return 2 * ((block // 2 + flip // 2) % 2) + (block + flip) % 2

    def greet(self, whole_plane=False):
        barrier = pltpu.get_barrier_semaphore()
        beside = self.plane if whole_plane else [self.by_core, self.by_x, self.by_y]
        partners = beside + self.others
        for partner in partners:
            pl.semaphore_signal(barrier, inc=1, device_id=partner, device_id_type=MESH)
        pl.semaphore_wait(barrier, len(partners))


def send(source, target, sems, index, partner):
    return pltpu.make_async_remote_copy(
        src_ref=source,
        dst_ref=target,
        send_sem=sems.at[0, index],
        recv_sem=sems.at[1, index],
        device_id=partner,
        device_id_type=MESH,
    )


def half_of(start, width, which):
    return pl.ds(pl.multiple_of(start + which * (width // 2), 128), width // 2)


class Gather:
    steps = 6

    def __init__(self, at, plan, shard, whole, pair, low, sems, local_sems):
        _, start, width, x_first = plan
        self.at, self.shard, self.pair, self.low, self.whole = at, shard, pair, low, whole
        rows = shard.shape[0]
        mine, other = half_of(start, width, at.core), half_of(start, width, 1 - at.core)
        own_rows = pl.ds(pl.multiple_of(rows * at.core, 8), rows)
        place = whole.at[at.seq, at.y, at.x, :, mine]
        along_x, along_y = (whole.at[:, at.y, at.x, :, mine], whole.at[:, at.y, :, :, mine])
        if not x_first:
            along_x, along_y = (whole.at[:, :, at.x, :, mine], along_x)
        self.local = [
            pltpu.make_async_copy(shard.at[:, mine], pair.at[own_rows], local_sems.at[0]),
            pltpu.make_async_copy(low, place, local_sems.at[1]),
        ]
        self.first = send(shard.at[:, other], pair.at[own_rows], sems, 0, at.by_core)
        self.over_z = [send(low, place, sems, 1 + k, at.others[k]) for k in range(3)]
        self.over_x = send(along_x, along_x, sems, 4, at.by_x)
        self.over_y = send(along_y, along_y, sems, 5, at.by_y)
        self.order = [self.over_x, self.over_y] if x_first else [self.over_y, self.over_x]
        self.last = send(whole.at[:, :, :, :, mine], whole.at[:, :, :, :, mine], sems, 6, at.by_core)

    def step(self, number):
        if number == 0:
            self.local[0].start()
            self.first.start()
        elif number == 1:
            self.local[0].wait()
            self.first.wait()
            self.low[...] = self.pair[...].astype(low_type)
            self.local[1].start()
            for copy in self.over_z:
                copy.start()
        elif number == 2:
            self.local[1].wait()
            for copy in self.over_z:
                copy.wait()
            self.order[0].start()
        elif number == 3:
            self.order[0].wait()
            self.order[1].start()
        elif number == 4:
            self.order[1].wait()
            self.last.start()
        else:
            self.last.wait()


class ScatterPlane:
    steps = 5

    def __init__(self, at, plan, term, kept, held, arrived, sems, local_sems):
        _, start, width, self.x_first = plan
        self.at, self.held, self.arrived = at, held, arrived
        mine, other = half_of(start, width, at.core), half_of(start, width, 1 - at.core)
        self.local = [
            pltpu.make_async_copy(term.at[:, :, :, :, mine], held, local_sems.at[0]),
            pltpu.make_async_copy(held.at[:, at.y, at.x], kept, local_sems.at[1]),
        ]
        self.first = send(term.at[:, :, :, :, other], arrived[0], sems, 0, at.by_core)
        if self.x_first:
            self.second = send(held.at[:, :, 1 - at.x], arrived[1], sems, 1, at.by_x)
            self.third = send(held.at[:, 1 - at.y, at.x], arrived[2], sems, 2, at.by_y)
        else:
            self.second = send(held.at[:, 1 - at.y], arrived[1], sems, 1, at.by_y)
            self.third = send(held.at[:, at.y, 1 - at.x], arrived[2], sems, 2, at.by_x)

    def add(self, place, values):
        self.held[place] = (self.held[place].astype(f32) + values.astype(f32)).astype(low_type)

    def step(self, number):
        at = self.at
        if number == 0:
            self.local[0].start()
            self.first.start()
        elif number == 1:
            self.local[0].wait()
            self.first.wait()

            @pl.loop(0, 4)
            def _(row):
                for across in range(4):
                    place = (row, across // 2, across % 2)
                    self.add(place, self.arrived[0][place])

            self.second.start()
        elif number == 2:
            self.second.wait()

            @pl.loop(0, 4)
            def _(row):
                for across in range(2):
                    place = (row, across, at.x) if self.x_first else (row, at.y, across)
                    self.add(place, self.arrived[1][row, across])

            self.third.start()
        elif number == 3:
            self.third.wait()

            @pl.loop(0, 4)
            def _(row):
                self.add((row, at.y, at.x), self.arrived[2][row])

            self.local[1].start()
        else:
            self.local[1].wait()


class ScatterLine:
    def __init__(self, at, share_start, kept, share, own, arrived, total, sems, local_sems):
        self.at, self.own, self.arrived, self.total = at, own, arrived, total
        rows, half = total.shape[0] // 2, total.shape[1]
        of_core = lambda which: pl.ds(pl.multiple_of(rows * which, 8), rows)
        mine = half_of(share_start, 2 * half, at.core)
        self.local = [
            pltpu.make_async_copy(kept.at[at.seq], own, local_sems.at[0]),
            pltpu.make_async_copy(
                total.at[of_core(at.core)], share.at[:, mine], local_sems.at[1]
            ),
        ]
        self.over_z = [
            send(kept.at[at.others[k][0]], arrived.at[k], sems, k, at.others[k]) for k in range(3)
        ]
        self.last = send(total.at[of_core(1 - at.core)], share.at[:, mine], sems, 3, at.by_core)

    def step(self, number):
        if number == 0:
            self.local[0].start()
            for copy in self.over_z:
                copy.start()
        elif number == 1:
            self.local[0].wait()
            for copy in self.over_z:
                copy.wait()
            total = self.own[...].astype(f32)
            for k in range(3):
                total = total + self.arrived[k].astype(f32)
            self.total[...] = total
            self.local[1].start()
            self.last.start()
        else:
            self.local[1].wait()
            self.last.wait()


class Ring:
    def __init__(self, at, own, blocks, sems, local_sem):
        self.at = at
        seq = at.seq
        self.local = pltpu.make_async_copy(own, blocks.at[seq], local_sem)
        right, left = ((seq + 1) % 4, at.dp), ((seq + 3) % 4, at.dp)
        self.hops = []
        for hop in range(3):
            back, ahead = (seq + 4 - hop) % 4, (seq + hop) % 4
            block_back = own if hop == 0 else blocks.at[back]
            block_ahead = own if hop == 0 else blocks.at[ahead]
            self.hops.append(
                [
                    (
                        (seq >= hop) & (seq < 3),
                        send(block_back, blocks.at[back], sems, hop, right),
                        seq >= hop + 1,
                    ),
                    (
                        (seq + hop <= 3) & (seq > 0),
                        send(block_ahead, blocks.at[ahead], sems, 3 + hop, left),
                        seq + hop + 1 <= 3,
                    ),
                ]
            )

    def start(self, hop):
        if hop == 0:
            self.local.start()
        for sends, copy, _ in self.hops[hop]:
            pl.when(sends)(copy.start)

    def arrive(self, hop):
        for _, copy, receives in self.hops[hop]:
            pl.when(receives)(copy.wait_recv)

    def finish(self):
        for hop in self.hops:
            for sends, copy, _ in hop:
                pl.when(sends)(copy.wait_send)


GATHERS = (
    (0, 0, 1280, True),
    (0, 1280, 1024, False),
    (1, 0, D, False),
    (2, 0, 4 * D, False),
    (3, 0, D, True),
)


def opening_kernel(*refs):
    shards, own = refs[:4], refs[4]
    gains, bucket_rows, bias_table, lengths = refs[5:9]
    wholes, outs = refs[9:13], refs[13:18]
    normed_out, keys_out, values_out, keys_extra_out, picks_out = outs
    queries, queries_t, context_t, log_total, extra = refs[18:23]
    scratch = refs[23:]
    many = len(GATHERS)
    of_gathers, scratch = scratch[: 4 * many], scratch[4 * many :]
    ring_sems, ring_local, out_sems, blocks, project, normed, keys, values_t = scratch[:8]
    keys_extra, picks, sums, tops = scratch[8:]
    at = Place()
    at.greet()
    gathers = [
        Gather(
            at,
            plan,
            shards[plan[0]],
            project if plan[0] == 0 else wholes[plan[0]],
            *of_gathers[4 * k : 4 * k + 4],
        )
        for k, plan in enumerate(GATHERS)
    ]
    ring = Ring(at, own, blocks, ring_sems, ring_local.at[0])

    def first_step(number):
        for gather in gathers[:2]:
            gather.step(number)

    def rest_step(number):
        for gather in gathers[2:]:
            gather.step(number)

    first_step(0)
    rest_step(0)
    first_step(1)

    count, buckets = own.shape[0], bias_table.shape[0]
    row_length = keys_extra.shape[0]
    query_blocks = count // BLK
    doc_start, one_start = extra_columns(query_blocks)
    picked = query_blocks * buckets
    ends = []
    for doc in range(DOCS):
        ends.append(lengths[0, doc] + (ends[-1] if ends else 0))

    def documents_at(position):
        return sum((position >= end).astype(jnp.int32) for end in ends)

    bucket_at = lax.broadcasted_iota(jnp.int32, (buckets, row_length), 0)
    for block in range(query_blocks):
        picks[buckets * block : buckets * block + buckets, :] = (
            (bucket_rows[block : block + 1, :] == bucket_at).astype(f32).astype(low_type)
        )
    last = picks.shape[0] - picked
    row = lax.broadcasted_iota(jnp.int32, (last, row_length), 0)
    key_doc = documents_at(lax.broadcasted_iota(jnp.int32, (last, row_length), 1))
    picks[picked:, :] = (
        jnp.where(row < DOCS, (key_doc != row).astype(f32), (row == DOCS).astype(f32))
    ).astype(low_type)

    table = jnp.concatenate([bias_table[...]] * query_blocks, axis=0)
    table_lane = lax.broadcasted_iota(jnp.int32, table.shape, 1)
    lane = lax.broadcasted_iota(jnp.int32, (picked, 128), 1)
    lane_block = lax.broadcasted_iota(jnp.int32, (picked, 128), 0) // buckets
    lane_last = lax.broadcasted_iota(jnp.int32, (last, 128), 1)
    row_last = lax.broadcasted_iota(jnp.int32, (last, 128), 0)
    below = jnp.where(
        (row_last < DOCS) & (lane_last - doc_start == row_last),
        masked_score,
        jnp.where(
            (row_last == DOCS) & (lane_last >= one_start) & (lane_last < one_start + TERMS), 1.0, 0.0
        ),
    ).astype(low_type)

    first_step(2)
    ring.start(0)
    rest_step(1)

    def make_extra(pair):
        sides = []
        for head in range(2):
            rest_of = jnp.sum(
                jnp.where(table_lane == 2 * pair + head, table, 0.0), axis=1, keepdims=True
            )
            side = jnp.zeros((picked, 128), f32)
            for term in range(TERMS):
                part = rest_of.astype(low_type).astype(f32)
                rest_of = rest_of - part
                side = jnp.where(lane == term * query_blocks + lane_block, part, side)
            sides.append(jnp.concatenate([side.astype(low_type), below], axis=0))
        keys_extra[:, pl.ds(pl.multiple_of(256 * pair, 256), 256)] = dot(
            picks[...], jnp.concatenate(sides, axis=1), 0, 0
        ).astype(low_type)

    pl.loop(0, PAIRS // 2)(make_extra)
    first_step(3)
    pl.loop(PAIRS // 2, PAIRS)(make_extra)
    first_step(4)
    extra_lane = lax.broadcasted_iota(jnp.int32, (count, 128), 1)
    extra_row = lax.broadcasted_iota(jnp.int32, (count, 128), 0)
    query_doc = documents_at(extra_row + at.seq * count)
    extra[...] = (
        (
            ((extra_lane < doc_start) & (extra_lane % query_blocks == extra_row // BLK))
            | ((extra_lane < one_start) & (extra_lane - doc_start == query_doc))
        )
        .astype(f32)
        .astype(low_type)
    )
    sums[...] = jnp.zeros_like(sums)
    tops[...] = jnp.full_like(tops, masked_score)
    ring.local.wait()
    first_step(5)

    copies = [pltpu.make_async_copy(project, wholes[0], out_sems.at[0])]
    for block in range(4):
        columns = pl.ds(count * block, count)
        into = pl.ds(pl.multiple_of(count * at.turn(block), count), count)
        copies += [
            pltpu.make_async_copy(
                keys_extra.at[columns], keys_extra_out.at[into], out_sems.at[1 + block]
            ),
            pltpu.make_async_copy(
                picks.at[:, columns], picks_out.at[:, into], out_sems.at[5 + block]
            ),
        ]
    for copy in copies:
        copy.start()
    weights = [project[:, :, :, :, D * part : D * part + D].reshape(D, D) for part in range(3)]
    pair_lane = lax.broadcasted_iota(jnp.int32, (count, PAIR), 1)

    def attend_pair(block, pair):
        lanes = pl.ds(pl.multiple_of(pair * PAIR, PAIR), PAIR)
        key_rows = pl.ds(pl.multiple_of(block * count, count), count)
        query_pair, key_pair = queries[:, lanes], keys[block, :, lanes]
        for head in range(2):
            which = 2 * pair + head
            mine = (pair_lane < HEAD) if head == 0 else (pair_lane >= HEAD)
            query_side = jnp.concatenate(
                [jnp.where(mine, query_pair, jnp.zeros_like(query_pair)), extra[...]], axis=1
            )
            more = keys_extra[key_rows, pl.ds(pl.multiple_of(128 * which, 128), 128)]
            scores = dot(jnp.concatenate([key_pair, more], axis=1), query_side, 1, 1)
            top_before = tops[which, 0:1]
            top = jnp.maximum(top_before, jnp.max(scores, axis=0, keepdims=True))
            unscaled = jnp.exp(scores - top).astype(low_type)
            value_side = jnp.concatenate(
                [
                    values_t[block, pl.ds(pl.multiple_of(HEAD * which, HEAD), HEAD), :],
                    jnp.ones((16, count), low_type),
                ],
                axis=0,
            )
            sums[which] = sums[which] * jnp.exp(top_before - top) + dot(value_side, unscaled, 1, 0)
            tops[which] = jnp.broadcast_to(top, (8, count))

    side = at.seq // 2
    order = [at.seq, 1 - at.seq + 4 * side, 2 - side, 3 - 3 * side]
    events = {
        (0, 5): [lambda: (ring.arrive(0), ring.start(1), rest_step(2))],
        (1, 4): [lambda: rest_step(3)],
        (1, 5): [lambda: (ring.arrive(1), ring.start(2))],
        (2, 5): [lambda: (rest_step(4), ring.arrive(2))],
    }
    for slot, block in enumerate(order):
        values = blocks[block].astype(f32)
        normed_low = (
            values
            * lax.rsqrt(jnp.mean(values * values, axis=1, keepdims=True) + norm_epsilon)
            * gains[0:1, :]
        ).astype(low_type)
        normed[block] = normed_low
        keys[block] = dot(normed_low, weights[1], 1, 0).astype(low_type)
        values_t[block] = dot(weights[2], normed_low, 0, 1).astype(low_type)
        for place, (source, target) in enumerate(
            ((normed, normed_out), (keys, keys_out), (values_t, values_out))
        ):
            copy = pltpu.make_async_copy(
                source.at[block], target.at[at.turn(block)], out_sems.at[9 + 3 * slot + place]
            )
            copy.start()
            copies.append(copy)
        if slot == 0:
            scaled = lambda values: (values.astype(low_type).astype(f32) * score_scale).astype(low_type)
            queries[...] = scaled(dot(normed_low, weights[0], 1, 0))
            queries_t[...] = scaled(dot(weights[0], normed_low, 0, 1))

        @pl.loop(0, PAIRS)
        def _(pair, slot=slot, block=block):
            for (when, which), actions in events.items():
                if when == slot:

                    @pl.when(pair == which)
                    def _(actions=actions):
                        for action in actions:
                            action()

            attend_pair(block, pair)

    for head in range(HEADS):
        total = sums[head, HEAD : HEAD + 1]
        context_t[HEAD * head : HEAD * head + HEAD, :] = sums[head, :HEAD] / total
        log_total[head : head + 1, :] = tops[head, 0:1] + jnp.log(total)
    rest_step(5)
    ring.finish()
    for copy in copies:
        copy.wait()


def open_layer(shards, own, gains, bucket_rows, bias_table, lengths):
    anywhere = pl.BlockSpec(memory_space=pl.ANY)
    in_place = pl.BlockSpec(memory_space=pltpu.VMEM)
    count, blocks = own.shape[0], bucket_rows.shape[0]
    row_length = 4 * count
    picked = blocks * bias_table.shape[0] + 16
    low = lambda *shape: jax.ShapeDtypeStruct(shape, low_type)
    whole_shapes = [(4, 2, 2, 2 * shard.shape[0], shard.shape[1]) for shard in shards]
    of_gathers = []
    for which, _, width, _ in GATHERS:
        half = (2 * shards[which].shape[0], width // 2)
        of_gathers += [
            pltpu.VMEM(half, f32),
            pltpu.VMEM(half, low_type),
            pltpu.SemaphoreType.DMA((2, 7)),
            pltpu.SemaphoreType.DMA((2,)),
        ]
    return pl.pallas_call(
        opening_kernel,
        out_shape=[low(*shape) for shape in whole_shapes]
        + [low(4, count, D)] * 2
        + [low(4, D, count), low(row_length, HEADS * 128), low(picked, row_length)]
        + [low(count, D), low(D, count)]
        + [jax.ShapeDtypeStruct((D, count), f32), jax.ShapeDtypeStruct((16, count), f32)]
        + [low(count, 128)],
        in_specs=[anywhere] * 5 + [in_place] * 3 + [pl.BlockSpec(memory_space=pltpu.SMEM)],
        out_specs=[anywhere] * 9 + [in_place] * 5,
        scratch_shapes=of_gathers
        + [
            pltpu.SemaphoreType.DMA((2, 6)),
            pltpu.SemaphoreType.DMA((1,)),
            pltpu.SemaphoreType.DMA((21,)),
            pltpu.VMEM((4, count, D), low_type),
            pltpu.VMEM(whole_shapes[0], low_type),
            pltpu.VMEM((4, count, D), low_type),
            pltpu.VMEM((4, count, D), low_type),
            pltpu.VMEM((4, D, count), low_type),
            pltpu.VMEM((row_length, HEADS * 128), low_type),
            pltpu.VMEM((picked, row_length), low_type),
            pltpu.VMEM((HEADS, HEAD + 16, count), f32),
            pltpu.VMEM((HEADS, 8, count), f32),
        ],
        compiler_params=pltpu.CompilerParams(
            collective_id=0, has_side_effects=True, vmem_limit_bytes=open_vmem
        ),
        name="open_layer",
    )(*shards, own, gains, bucket_rows, bias_table, lengths)


def plane_scratch(rows, width):
    half = width // 2
    return [
        pltpu.VMEM((4, 2, 2, rows, half), low_type),
        pltpu.VMEM((4, 2, 2, rows, half), low_type),
        pltpu.VMEM((4, 2, rows, half), low_type),
        pltpu.VMEM((4, rows, half), low_type),
        pltpu.SemaphoreType.DMA((2, 3)),
        pltpu.SemaphoreType.DMA((2,)),
    ]


def line_scratch(rows, width):
    half = width // 2
    return [
        pltpu.VMEM((rows, half), low_type),
        pltpu.VMEM((3, rows, half), low_type),
        pltpu.VMEM((rows, half), f32),
        pltpu.SemaphoreType.DMA((2, 4)),
        pltpu.SemaphoreType.DMA((2,)),
    ]


def take_plane(at, plan, term, kept, scratch):
    return ScatterPlane(at, plan, term, kept, scratch[0], scratch[1:4], scratch[4], scratch[5])


def by_chip(term):
    return term.reshape(4, 2, 2, term.shape[0] // 16, term.shape[1])


class AllSum:
    def __init__(self, at, own, plane, line, sems):
        self.at, self.own, self.plane, self.line = at, own, plane, line
        self.local = pltpu.make_async_copy(own, plane.at[at.dp], sems.at[0, 10])
        self.beside = [
            send(own, plane.at[at.dp], sems, k, partner) for k, partner in enumerate(at.plane)
        ]
        place = line.at[at.seq]
        self.over_z = [
            send(place, place, sems, 7 + k, partner) for k, partner in enumerate(at.others)
        ]

    def step(self, number):
        if number == 0:
            self.local.start()
            for copy in self.beside:
                copy.start()
        elif number == 1:
            self.local.wait()
            for copy in self.beside:
                copy.wait()
            total = self.plane[0]
            for k in range(1, 8):
                total = total + self.plane[k]
            self.line[self.at.seq] = total
            for copy in self.over_z:
                copy.start()
        else:
            for copy in self.over_z:
                copy.wait()

    def total(self):
        return (self.line[0] + self.line[1]) + (self.line[2] + self.line[3])


def sum_scratch(width):
    return [
        pltpu.VMEM((8, width), f32),
        pltpu.VMEM((8, 8, width), f32),
        pltpu.VMEM((4, 8, width), f32),
        pltpu.SemaphoreType.DMA((2, 11)),
    ]


EARLY_WIDTH, LATE_WIDTH = D + 512, D
CLOSE_PLANS = ((2, 0, D, True), (1, 0, D, False), (0, 0, D, True))


def split_low(values):
    terms = []
    for _ in range(TERMS):
        terms.append(values.astype(low_type))
        values = values - terms[-1].astype(f32)
    return terms


def close_kernel(scale, *refs):
    normed, key_grad_t, value_grad_t, query_grad, project, key_part_t = refs[:6]
    inputs, residual_grad, folded, picks, gains, gain_two, own_weight = refs[6:13]
    kept_rest, rows_before, refs = refs[13:18], refs[18:22], refs[22:]
    input_grad, shares, early_total, late_total = refs[0], refs[1:5], refs[5], refs[6]
    scratch = refs[7:]
    normed_in, key_in, value_in, weight_in, part_in, residual_in, load_sems = scratch[:7]
    early, late, scratch = scratch[7:11], scratch[11:15], scratch[15:]
    terms, kept, scratch = scratch[:3], scratch[3:6], scratch[6:]
    at = Place()
    loads = [
        pltpu.make_async_copy(source, target, load_sems.at[k])
        for k, (source, target) in enumerate(
            (
                (value_grad_t, value_in),
                (normed, normed_in),
                (key_grad_t, key_in),
                (project.at[:, 0:D], weight_in),
                (key_part_t, part_in),
                (residual_grad, residual_in),
            )
        )
    ]
    for load in loads:
        load.start()
    at.greet(whole_plane=True)
    planes, lines = [], []
    for k, plan in enumerate(CLOSE_PLANS):
        planes.append(take_plane(at, plan, terms[k], kept[k], scratch[:6]))
        lines.append(ScatterLine(at, D * plan[0], kept[k], shares[0], *scratch[6:11]))
        scratch = scratch[11:]
    rest_lines = []
    for k, (which, start, _, _) in enumerate(BACK_PLANS):
        rest_lines.append(
            ScatterLine(at, start, kept_rest[k], shares[which + 1], *scratch[5 * k : 5 * k + 5])
        )
    first, second = AllSum(at, *early), AllSum(at, *late)

    for line in rest_lines:
        line.step(0)
    early_own, late_own = early[0], late[0]
    early_own[...] = jnp.zeros_like(early_own)
    late_own[...] = jnp.zeros_like(late_own)
    count = inputs.shape[0]
    query_low = (query_grad[...] * score_scale).astype(low_type)

    def put(term, values):
        term[...] = values.astype(low_type).reshape(term.shape)

    def of_blocks(parts):
        total = None
        for block in range(4):
            piece = dot(parts[:, count * block : count * block + count], normed_in[block], 1, 0)
            total = piece if total is None else total + piece
        return total.T

    loads[0].wait()
    loads[1].wait()
    put(terms[0], of_blocks(value_in))
    planes[0].step(0)
    loads[2].wait()
    put(terms[1], of_blocks(key_in))
    planes[1].step(0)
    planes[0].step(1)
    put(terms[2], dot(normed_in[3], query_low, 0, 0))
    planes[2].step(0)
    planes[1].step(1)

    for load in loads[3:]:
        load.wait()
    source = inputs[...].astype(f32)
    scaled = (dot(query_low, weight_in[...], 1, 1) + part_in[...].T) * gains[0:1, :]
    inverse = lax.rsqrt(jnp.mean(source * source, axis=1, keepdims=True) + norm_epsilon)
    along = jnp.mean(source * scaled, axis=1, keepdims=True)
    input_grad[...] = (
        residual_in[...] + inverse * scaled - source * (inverse * inverse * inverse * along)
    ).astype(low_type)
    planes[2].step(1)
    planes[0].step(2)

    blocks = query_blocks_of(picks.shape[0])
    buckets = (picks.shape[0] - 16) // blocks
    rows = folded.shape[0] * folded.shape[1]
    flat = split_low(folded[...].reshape(rows, folded.shape[2]))
    parted = dot(jnp.concatenate(flat, axis=0), picks[: blocks * buckets, :], 1, 1)
    parted = parted[:rows] + parted[rows : 2 * rows] + parted[2 * rows :]
    row = lax.broadcasted_iota(jnp.int32, parted.shape, 0) % folded.shape[1]
    lane = lax.broadcasted_iota(jnp.int32, parted.shape, 1)
    parted = jnp.where(row == lane // buckets, parted, 0.0)
    at_bucket = (
        lax.broadcasted_iota(jnp.int32, (blocks * buckets, buckets), 0) % buckets
        == lax.broadcasted_iota(jnp.int32, (blocks * buckets, buckets), 1)
    )
    at_bucket = at_bucket.astype(f32).astype(low_type)
    table = sum(dot(term, at_bucket, 1, 0) for term in split_low(parted))
    table = jnp.sum(table.reshape(HEADS, folded.shape[1], buckets), axis=1)
    early_own[:, D + 256 : D + 256 + buckets] = table[:8]
    early_own[0 : HEADS - 8, D + 384 : D + 384 + buckets] = table[8:]
    early_own[2:3, :D] = gain_two[...]

    planes[1].step(2)
    for line in rest_lines:
        line.step(1)
    planes[2].step(2)

    def statistics(raw, previous):
        gradient = raw * scale
        squares = gradient * gradient + tiny_term
        means = jnp.sum(jnp.mean(squares, axis=1, keepdims=True), axis=0, keepdims=True)
        before = jnp.sum(previous.reshape(1, previous.shape[0]), axis=1, keepdims=True)
        row_sum = decay_rate * before + (1.0 - decay_rate) * means
        return jnp.sum(squares, axis=0, keepdims=True), jnp.broadcast_to(row_sum, (1, 128))

    planes[0].step(3)
    planes[0].step(4)
    lines[0].step(0)
    for line in rest_lines:
        line.step(2)
    for position in (1, 2, 3):
        columns, row_sum = statistics(shares[position][...], rows_before[position][...])
        early_own[position : position + 1, D : D + 128] = row_sum
        if position == 2:
            for part in range(4):
                early_own[4 + part : 5 + part, :D] = columns[:, D * part : D * part + D]
        else:
            early_own[position // 2 : position // 2 + 1, :D] = columns
    first.step(0)
    planes[1].step(3)
    planes[1].step(4)
    lines[1].step(0)
    planes[2].step(3)
    planes[2].step(4)
    lines[2].step(0)
    lines[0].step(1)
    first.step(1)
    lines[1].step(1)
    lines[2].step(1)
    first.step(2)
    early_total[...] = first.total()
    for line in lines:
        line.step(2)

    raw = shares[0][...]
    columns, row_sum = statistics(raw, rows_before[0][...])
    for part in range(3):
        late_own[part : part + 1, :] = columns[:, D * part : D * part + D]
    late_own[4:5, :128] = row_sum
    own_rows = raw.shape[0]
    lane = lax.broadcasted_iota(jnp.int32, (own_rows, D), 1)
    row = lax.broadcasted_iota(jnp.int32, (own_rows, D), 0)
    mine = lane == row + (at.seq * 8 + at.dp) * own_rows
    gain_one = jnp.sum(
        raw * own_weight[...].astype(low_type).astype(f32), axis=1, keepdims=True
    )
    spread = jnp.where(mine, jnp.broadcast_to(gain_one, (own_rows, D)), 0.0)
    late_own[3:4, :] = jnp.sum(spread, axis=0, keepdims=True) / gains[0:1, :]
    second.step(0)
    second.step(1)
    second.step(2)
    late_total[...] = second.total()


def query_blocks_of(rows):
    return (rows - 16) // 32


def close(scale, large, small, kept_rest, rows_before, weight_shapes):
    in_place = pl.BlockSpec(memory_space=pltpu.VMEM)
    anywhere = pl.BlockSpec(memory_space=pl.ANY)
    count, row_length = small[0].shape[0], large[1].shape[1]
    scratch = [
        pltpu.VMEM((4, count, D), low_type),
        pltpu.VMEM((D, row_length), low_type),
        pltpu.VMEM((D, row_length), low_type),
        pltpu.VMEM((D, D), low_type),
        pltpu.VMEM((D, count), f32),
        pltpu.VMEM((count, D), f32),
        pltpu.SemaphoreType.DMA((6,)),
    ]
    scratch += sum_scratch(EARLY_WIDTH) + sum_scratch(LATE_WIDTH)
    scratch += [pltpu.VMEM((4, 2, 2, D // 16, D), low_type)] * 3
    scratch += [pltpu.VMEM((4, D // 16, D // 2), low_type)] * 3
    for _ in CLOSE_PLANS:
        scratch += plane_scratch(D // 16, D) + line_scratch(D // 16, D)
    for which, _, width, _ in BACK_PLANS:
        scratch += line_scratch(2 * weight_shapes[which + 1][0], width)
    return pl.pallas_call(
        functools.partial(close_kernel, scale),
        out_shape=[jax.ShapeDtypeStruct((count, D), low_type)]
        + [jax.ShapeDtypeStruct(shape, f32) for shape in weight_shapes]
        + [
            jax.ShapeDtypeStruct((8, EARLY_WIDTH), f32),
            jax.ShapeDtypeStruct((8, LATE_WIDTH), f32),
        ],
        in_specs=[anywhere] * 3
        + [in_place]
        + [anywhere] * 2
        + [in_place, anywhere]
        + [in_place] * 5
        + [anywhere] * 5
        + [in_place] * 4,
        out_specs=[in_place] * 7,
        scratch_shapes=scratch,
        compiler_params=pltpu.CompilerParams(
            collective_id=2, has_side_effects=True, vmem_limit_bytes=close_vmem
        ),
        name="close_layer",
    )(*large, *small, *kept_rest, *rows_before)


def apply_kernel(scale, *refs):
    shares, weights, rows_before, columns_before = refs[:4], refs[4:8], refs[8:12], refs[12:16]
    early, late, gains, gains_moment, table, table_moment = refs[16:22]
    refs = refs[22:]
    gradients, updated, rows_after, columns_after = refs[:4], refs[4:8], refs[8:12], refs[12:16]
    gains_out, table_out = refs[16:19], refs[19:22]
    early_sums, late_sums = early[...], late[...]
    sums = [
        jnp.concatenate([late_sums[part : part + 1] for part in range(3)], axis=1),
        early_sums[0:1, :D],
        jnp.concatenate([early_sums[4 + part : 5 + part, :D] for part in range(4)], axis=1),
        early_sums[1:2, :D],
    ]
    row_sums = [late_sums[4:5, 0:1]] + [early_sums[k : k + 1, D : D + 1] for k in (1, 2, 3)]
    for position in range(4):
        rows, width = shares[position].shape
        full = rows * 32
        gradient = shares[position][...] * scale
        gradients[position][...] = gradient
        squares = gradient * gradient + tiny_term
        eye = lax.broadcasted_iota(jnp.int32, (rows, rows), 0) == lax.broadcasted_iota(
            jnp.int32, (rows, rows), 1
        )
        before = jnp.broadcast_to(rows_before[position][...].reshape(1, rows), (rows, rows))
        before = jnp.sum(jnp.where(eye, before, 0.0), axis=1, keepdims=True)
        rows_new = decay_rate * before + (1.0 - decay_rate) * jnp.mean(
            squares, axis=1, keepdims=True
        )
        rows_after[position][...] = jnp.sum(
            jnp.where(eye, jnp.broadcast_to(rows_new, (rows, rows)), 0.0), axis=0, keepdims=True
        ).reshape(rows)
        columns_new = decay_rate * columns_before[position][...].reshape(1, width) + (
            1.0 - decay_rate
        ) * (sums[position] / full)
        columns_after[position][...] = columns_new.reshape(width)
        denominator = rows_new * columns_new / (row_sums[position] / full)
        updated[position][...] = weights[position][...] - learn_rate * gradient * lax.rsqrt(
            denominator
        )

    def moments(gradient, old, moment, results):
        moment_new = decay_rate * moment[...] + (1.0 - decay_rate) * (
            gradient * gradient + tiny_term
        )
        results[0][...] = gradient
        results[1][...] = old[...] - learn_rate * gradient * lax.rsqrt(moment_new)
        results[2][...] = moment_new

    moments(
        jnp.concatenate([late_sums[3:4, :D], early_sums[2:3, :D]], axis=0) * scale,
        gains,
        gains_moment,
        gains_out,
    )
    buckets = table.shape[0]
    of_table = jnp.concatenate(
        [
            early_sums[:, D + 256 : D + 256 + buckets],
            early_sums[0 : HEADS - 8, D + 384 : D + 384 + buckets],
        ],
        axis=0,
    )
    moments(of_table.T * scale, table, table_moment, table_out)


def apply_updates(scale, shares, weights, rows_before, columns_before, rest):
    in_place = pl.BlockSpec(memory_space=pltpu.VMEM)
    same = lambda arrays: [jax.ShapeDtypeStruct(array.shape, f32) for array in arrays]
    gains, table = rest[2], rest[4]
    return pl.pallas_call(
        functools.partial(apply_kernel, scale),
        out_shape=same(weights)
        + same(weights)
        + same(rows_before)
        + same(columns_before)
        + same([gains] * 3)
        + same([table] * 3),
        in_specs=[in_place] * 22,
        out_specs=[in_place] * 22,
        compiler_params=pltpu.CompilerParams(vmem_limit_bytes=apply_vmem),
        name="apply_updates",
    )(*shares, *weights, *rows_before, *columns_before, *rest)


BACK_PLANS = (
    (1, 0, 2 * D, False),
    (2, 0, 512, True),
    (1, 2 * D, 2 * D, False),
    (2, 512, 256, True),
    (0, 0, D, True),
)
EARLY, LATE = (0, 1), (2, 3, 4)
BACK_TIMES = (
    (0, None),
    (0, (EARLY, 0)),
    (1, (LATE, 0)),
    (2, (EARLY, 1)),
    (6, (EARLY, 2)),
    (6, (LATE, 1)),
    (9, (EARLY, 3)),
    (11, (LATE, 2)),
    (14, (LATE, 3)),
    (23, (EARLY, 4)),
    (23, (LATE, 4)),
)


class Relay:
    def __init__(self, at, kept, arrived, sems):
        self.kept, self.arrived = kept, arrived
        seq = at.seq
        self.is_end = (seq == 0) | (seq == 3)
        self.is_inner = (seq == 1) | (seq == 2)
        inwards = (1 + seq // 3, at.dp)
        outwards = ((3 * seq + 1) % 4, at.dp)
        across = ((7 - seq) % 4, at.dp)
        self.from_end = [send(kept.at[k], arrived.at[k], sems, k, inwards) for k in range(3)]
        self.to_peer = [
            send(kept.at[1], arrived.at[3], sems, 3, across),
            send(kept.at[0], arrived.at[4], sems, 4, across),
        ]
        self.to_end = send(kept.at[2], arrived.at[0], sems, 5, outwards)

    def turn(self, number, part, total):
        kept, arrived = self.kept, self.arrived
        low = lambda values: values.astype(low_type)
        wide = lambda ref, k: ref[k].astype(f32)
        if number < 3:

            @pl.when(self.is_end)
            def _():
                kept[number] = low(part)
                self.from_end[number].start()

        if number == 0:

            @pl.when(self.is_inner)
            def _():
                kept[0] = low(part)

        elif number == 1:

            @pl.when(self.is_inner)
            def _():
                self.from_end[0].wait_recv()
                kept[1] = low(part + wide(arrived, 0))
                self.to_peer[0].start()

        elif number == 2:

            @pl.when(self.is_inner)
            def _():
                self.from_end[1].wait_recv()
                kept[0] = low(wide(kept, 0) + wide(arrived, 1))
                self.to_peer[1].start()
                self.to_peer[0].wait_recv()
                kept[2] = low(part + wide(arrived, 3))
                self.to_end.start()

        else:

            @pl.when(self.is_end)
            def _():
                self.to_end.wait_recv()
                total[...] = part + wide(arrived, 0)
                for copy in self.from_end:
                    copy.wait_send()

            @pl.when(self.is_inner)
            def _():
                self.from_end[2].wait_recv()
                self.to_peer[1].wait_recv()
                total[...] = part + wide(arrived, 2) + wide(arrived, 4)
                for copy in self.to_peer:
                    copy.wait_send()
                self.to_end.wait_send()


def backward_kernel(
    queries,
    extra,
    row_columns,
    context_grad,
    queries_t,
    context_grad_t,
    keys,
    values_t,
    keys_extra,
    *refs,
):
    turn, pair = pl.program_id(0), pl.program_id(1)
    remote = len(refs) > 4
    if remote:
        weights, terms, refs = refs[0], refs[1:4], refs[4:]
        total, kept_rest, scratch = refs[4], refs[5:10], refs[10:]
        parts, kept, arrived, relay_sems = scratch[:4]
        at = Place()
        relay = Relay(at, kept, arrived, relay_sems)
        scatters = [
            take_plane(at, plan, terms[plan[0]], kept_rest[k], scratch[4 + 6 * k : 10 + 6 * k])
            for k, plan in enumerate(BACK_PLANS)
        ]
        now = turn * PAIRS + pair
        for when, doing in BACK_TIMES:

            @pl.when(now == when)
            def _(doing=doing):
                if doing is None:
                    at.greet()
                else:
                    for which in doing[0]:
                        scatters[which].step(doing[1])

    query_grad, key_grad_t, value_grad_t, folded = refs[:4]
    count = queries.shape[0]
    lane = lax.broadcasted_iota(jnp.int32, (count, PAIR), 1)
    query_pair, grad_pair = queries[...], context_grad[...]
    zeros = jnp.zeros_like(query_pair)
    lanes = pl.ds(pl.multiple_of(PAIR * pair, PAIR), PAIR)
    columns = pltpu.roll(row_columns[...], (128 - 2 * pair) % 128, 1)

    @pl.when(turn == 0)
    def _():
        query_grad[:, lanes] = jnp.zeros((count, PAIR), f32)

    query_grads = []
    for head in range(2):
        mine = (lane < HEAD) if head == 0 else (lane >= HEAD)
        rows = pl.ds(HEAD * head, HEAD)
        query_side = jnp.concatenate([jnp.where(mine, query_pair, zeros), extra[...]], axis=1)
        key_side = jnp.concatenate(
            [keys[...], keys_extra[:, 128 * head : 128 * head + 128]], axis=1
        )
        attention = jnp.exp(dot(query_side, key_side, 1, 1) - columns[:, head : head + 1])
        score_grad = attention * (
            dot(jnp.where(mine, grad_pair, zeros), values_t[0], 1, 0)
            - columns[:, HEADS + head : HEADS + head + 1]
        )
        attention_low = attention.astype(low_type)
        score_low = score_grad.astype(low_type)
        sums = [
            jnp.sum(score_grad[BLK * block : BLK * block + BLK], axis=0, keepdims=True)
            for block in range(count // BLK)
        ]
        spare = folded.shape[1] - len(sums)
        folded[head] = jnp.concatenate(sums + [jnp.zeros((spare, count), f32)] * (spare > 0), axis=0)
        query_grads.append(dot(score_low, keys[...], 1, 0))
        value_grad_t[rows, :] = dot(context_grad_t[rows, :], attention_low, 1, 0).astype(low_type)
        key_grad_t[rows, :] = dot(queries_t[rows, :], score_low, 1, 0).astype(low_type)
    query_grad[:, lanes] += jnp.where(lane < HEAD, query_grads[0], query_grads[1])

    if remote:
        parts[pl.ds(pl.multiple_of(PAIR * pair, PAIR), PAIR), :] = key_grad_t[...]
        parts[pl.ds(pl.multiple_of(D + PAIR * pair, PAIR), PAIR), :] = value_grad_t[...]
        for number in range(4):

            @pl.when(now == number * PAIRS + PAIRS - 1)
            def _(number=number):
                relay.turn(number, dot(weights[...], parts[...], 1, 0), total)


def attend_back(
    queries,
    extra,
    row_columns,
    context_grad,
    queries_t,
    context_grad_t,
    keys,
    values_t,
    keys_extra,
    weights,
    terms,
):
    count, row_length = queries.shape[0], keys.shape[0]
    fold_rows = -(-(count // BLK) // 8) * 8
    terms = [by_chip(term) for term in terms]
    anywhere = pl.BlockSpec(memory_space=pl.ANY)
    of_pair = pl.BlockSpec((count, PAIR), lambda turn, pair: (0, pair))
    of_pair_t = pl.BlockSpec((PAIR, count), lambda turn, pair: (pair, 0))
    key_t = pl.BlockSpec((PAIR, count), lambda turn, pair: (pair, turn))
    still = lambda *shape: pl.BlockSpec(shape, lambda turn, pair: (0,) * len(shape))
    remote, more_specs, more_shapes, more_out, scratch, more = {}, [], [], [], [], []
    if terms:
        remote = {"collective_id": 1, "has_side_effects": True}
        more = [weights, *terms]
        more_specs = [still(D, 2 * D)] + [anywhere] * 3
        more_shapes = [jax.ShapeDtypeStruct((D, count), f32)] + [
            jax.ShapeDtypeStruct((4, terms[which].shape[3], width // 2), low_type)
            for which, _, width, _ in BACK_PLANS
        ]
        more_out = [still(D, count)] + [anywhere] * len(BACK_PLANS)
        scratch = [
            pltpu.VMEM((2 * D, count), low_type),
            pltpu.VMEM((3, D, count), low_type),
            pltpu.VMEM((5, D, count), low_type),
            pltpu.SemaphoreType.DMA((2, 6)),
        ]
        for which, _, width, _ in BACK_PLANS:
            scratch += plane_scratch(terms[which].shape[3], width)
    return pl.pallas_call(
        backward_kernel,
        grid=(row_length // count, PAIRS),
        out_shape=[
            jax.ShapeDtypeStruct((count, D), f32),
            jax.ShapeDtypeStruct((D, row_length), low_type),
            jax.ShapeDtypeStruct((D, row_length), low_type),
            jax.ShapeDtypeStruct((HEADS, fold_rows, row_length), f32),
        ]
        + more_shapes,
        in_specs=[
            of_pair,
            still(count, 128),
            still(count, 128),
            of_pair,
            of_pair_t,
            of_pair_t,
            pl.BlockSpec((count, PAIR), lambda turn, pair: (turn, pair)),
            pl.BlockSpec((1, PAIR, count), lambda turn, pair: (turn, pair, 0)),
            pl.BlockSpec((count, 256), lambda turn, pair: (turn, pair)),
        ]
        + more_specs,
        out_specs=[
            still(count, D),
            key_t,
            key_t,
            pl.BlockSpec((2, fold_rows, count), lambda turn, pair: (pair, 0, turn)),
        ]
        + more_out,
        scratch_shapes=scratch,
        compiler_params=pltpu.CompilerParams(vmem_limit_bytes=back_vmem, **remote),
        cost_estimate=pl.CostEstimate(
            flops=10 * HEADS * count * row_length * 200,
            bytes_accessed=HEADS * row_length * 2048,
            transcendentals=HEADS * count * row_length,
        ),
        name="attention_backward",
    )(
        queries,
        extra,
        row_columns,
        context_grad,
        queries_t,
        context_grad_t,
        keys,
        values_t,
        keys_extra,
        *more,
    )


def body(
    hidden_states,
    output_cotangent,
    document_lengths,
    bucket_index,
    norm_gains,
    bias_table,
    project_weight,
    output_weight,
    expand_weight,
    reduce_weight,
    project_rows,
    project_columns,
    output_rows,
    output_columns,
    expand_rows,
    expand_columns,
    reduce_rows,
    reduce_columns,
    gains_moment,
    table_moment,
):
    every = ("seq", "dp")
    local_rows = hidden_states.shape[1]
    row_length = local_rows * lax.axis_size("seq")
    gradient_scale = 1.0 / math.sqrt(row_length * lax.axis_size("dp"))
    place = lax.axis_index("seq")
    blocks = local_rows // BLK

    shards = (project_weight, output_weight, expand_weight, reduce_weight)
    direct = (
        lax.axis_size("seq") == 4
        and lax.axis_size("dp") == 8
        and all(shard.shape[0] % 8 == 0 and shard.shape[1] % 256 == 0 for shard in shards)
    )
    inputs = hidden_states[0].astype(f32)
    if direct:
        opened = open_layer(
            shards, hidden_states[0], norm_gains, bucket_index[0], bias_table, document_lengths
        )
        project_full, output_full, expand_full, reduce_full = (
            whole.reshape(-1, whole.shape[4]) for whole in opened[:4]
        )
        normed_all, keys = (blocks_of.reshape(row_length, D) for blocks_of in opened[4:6])
        values_t, keys_extra, picks, queries, queries_t, context_t, log_total, extra = opened[6:]
        log_total = log_total[:HEADS]
        normed_low = normed_all[row_length - local_rows :]
    else:
        project_full, output_full, expand_full, reduce_full = (
            lax.all_gather(shard.astype(low_type), every, axis=0, tiled=True) for shard in shards
        )
        row_states = lax.all_gather(hidden_states[0], "seq", axis=0, tiled=True)
        normed_low = rms_norm(inputs, norm_gains[0]).astype(low_type)
        normed_all = rms_norm(row_states.astype(f32), norm_gains[0]).astype(low_type)
        doc_all = documents(document_lengths[0], row_length)
        doc_query = lax.dynamic_slice_in_dim(doc_all, place * local_rows, local_rows)
        picks = key_picks(bucket_index[0], doc_all, bias_table.shape[0])
        one_hot = picks[:, : blocks * bias_table.shape[0]]
        keys_extra = key_extra(picks, bias_table, blocks)
        extra = query_extra(doc_query, blocks)
        scaled = lambda values: (values.astype(low_type).astype(f32) * score_scale).astype(low_type)
        queries = scaled(dot(normed_low, project_full[:, :D], 1, 0))
        queries_t = scaled(dot(project_full[:, :D], normed_low, 0, 1))
        keys = dot(normed_all, project_full[:, D : 2 * D], 1, 0).astype(low_type)
        values_t = dot(project_full[:, 2 * D :], normed_all, 0, 1).astype(low_type)
        context_t, log_total = attend(queries, extra, keys, values_t, keys_extra)
        log_total = log_total.reshape(HEADS, 8, local_rows)[:, 0]
        values_t = jnp.transpose(values_t.reshape(D, -1, local_rows), (1, 0, 2))
    _, pullback_one = jax.vjp(rms_norm, inputs, norm_gains[0])
    query_weight, key_weight, value_weight = (
        project_full[:, :D],
        project_full[:, D : 2 * D],
        project_full[:, 2 * D :],
    )
    context_low_t = context_t.astype(low_type)
    residual = inputs + dot(context_low_t, output_full, 0, 0)
    normed_two, pullback_two = jax.vjp(rms_norm, residual, norm_gains[1])
    normed_two_low = normed_two.astype(low_type)
    expanded = dot(normed_two_low, expand_full, 1, 0)
    activated, pullback_gelu = jax.vjp(gelu_tanh, expanded)
    activated_low = activated.astype(low_type)
    layer_output = (residual + dot(activated_low, reduce_full, 1, 0)).astype(low_type)[None]

    upstream_low = output_cotangent[0].astype(low_type)
    upstream = upstream_low.astype(f32)
    reduce_term = dot(activated_low, upstream_low, 0, 0)
    (expanded_grad,) = pullback_gelu(dot(upstream_low, reduce_full, 1, 1))
    expanded_low = expanded_grad.astype(low_type)
    expand_term = dot(normed_two_low, expanded_low, 0, 0)
    residual_part, gain_two_grad = pullback_two(dot(expanded_low, expand_full, 1, 1))
    residual_grad = upstream + residual_part
    residual_low = residual_grad.astype(low_type)
    output_term = dot(context_low_t, residual_low, 1, 0)
    context_grad = dot(residual_low, output_full, 1, 1).astype(low_type)
    context_grad_t = dot(output_full, residual_low, 1, 1).astype(low_type)
    delta = jnp.sum(
        (context_grad_t.astype(f32) * context_t).reshape(HEADS, HEAD, local_rows), axis=1
    )

    row_columns = jnp.pad(
        jnp.concatenate([log_total, delta], axis=0).T, ((0, 0), (0, 128 - 2 * HEADS))
    )
    query_grad, key_grad_t, value_grad_t, folded, *summed_back = attend_back(
        queries,
        extra,
        row_columns,
        context_grad,
        queries_t,
        context_grad_t,
        keys,
        values_t,
        keys_extra,
        project_full[:, D:],
        [term.astype(low_type) for term in (output_term, expand_term, reduce_term)]
        if direct
        else [],
    )
    if direct:
        rows_before = [project_rows, output_rows, expand_rows, reduce_rows]
        input_gradient, *results = close(
            gradient_scale,
            (
                normed_all.reshape(4, local_rows, D),
                key_grad_t,
                value_grad_t,
                query_grad,
                project_full,
                summed_back[0],
            ),
            (
                hidden_states[0],
                residual_grad,
                folded,
                picks,
                norm_gains,
                gain_two_grad[None],
                project_weight,
            ),
            summed_back[1:],
            rows_before,
            [shard.shape for shard in shards],
        )
        results = apply_updates(
            gradient_scale,
            results[:4],
            shards,
            rows_before,
            [project_columns, output_columns, expand_columns, reduce_columns],
            (results[4], results[5], norm_gains, gains_moment, bias_table, table_moment),
        )
        gradients, updated_weights, row_after, columns_after = (
            results[:4],
            results[4:8],
            results[8:12],
            results[12:16],
        )
        gains_gradient, gains_updated, gains_moment_new = results[16:19]
        table_gradient, table_updated, table_moment_new = results[19:]
        return (
            layer_output,
            input_gradient[None],
            gains_gradient,
            table_gradient,
            *gradients,
            gains_updated,
            table_updated,
            *updated_weights,
            row_after[0],
            columns_after[0],
            row_after[1],
            columns_after[1],
            row_after[2],
            columns_after[2],
            row_after[3],
            columns_after[3],
            gains_moment_new,
            table_moment_new,
        )

    buckets = bias_table.shape[0]
    picked = jnp.dot(
        folded[:, :blocks].reshape(HEADS * blocks, row_length),
        one_hot.astype(f32),
        precision=lax.Precision.HIGHEST,
    )
    table_grad = jnp.einsum("hkkb->bh", picked.reshape(HEADS, blocks, blocks, buckets))

    query_grad_low = (query_grad * score_scale).astype(low_type)
    project_terms = [
        dot(normed_low, query_grad_low, 0, 0),
        dot(normed_all, key_grad_t, 0, 1),
        dot(normed_all, value_grad_t, 0, 1),
    ]
    key_part = dot(key_grad_t, key_weight, 0, 1) + dot(value_grad_t, value_weight, 0, 1)
    key_part = lax.psum_scatter(
        key_part.astype(low_type), "seq", scatter_dimension=0, tiled=True
    ).astype(f32)
    input_part, gain_one_grad = pullback_one(dot(query_grad_low, query_weight, 1, 1) + key_part)
    input_gradient = (residual_grad + input_part).astype(low_type)[None]
    terms = [
        term.astype(low_type)
        for term in (jnp.concatenate(project_terms, axis=1), output_term, expand_term, reduce_term)
    ]
    shares = [
        lax.psum_scatter(term, every, scatter_dimension=0, tiled=True).astype(f32)
        for term in terms
    ]
    gradients = tuple((share * gradient_scale for share in shares))
    row_before = (project_rows, output_rows, expand_rows, reduce_rows)
    row_after = []
    column_parts = []
    row_sums = []
    for gradient, previous in zip(gradients, row_before):
        squares = gradient * gradient + tiny_term
        updated_rows = decay_rate * previous + (1.0 - decay_rate) * jnp.mean(squares, axis=1)
        row_after.append(updated_rows)
        column_parts.append(jnp.sum(squares, axis=0))
        row_sums.append(jnp.sum(updated_rows))
    summed = lax.psum(
        (
            column_parts[0],
            column_parts[1],
            column_parts[2],
            column_parts[3],
            jnp.stack(row_sums),
            jnp.stack([gain_one_grad, gain_two_grad]),
            table_grad,
        ),
        every,
    )
    column_before = (project_columns, output_columns, expand_columns, reduce_columns)
    weights_before = (project_weight, output_weight, expand_weight, reduce_weight)
    full_rows = (
        project_full.shape[0],
        output_full.shape[0],
        expand_full.shape[0],
        reduce_full.shape[0],
    )
    updated_weights = []
    columns_after = []
    for position in range(4):
        columns_new = decay_rate * column_before[position] + (1.0 - decay_rate) * (
            summed[position] / full_rows[position]
        )
        row_mean = summed[4][position] / full_rows[position]
        denominator = row_after[position][:, None] * columns_new[None, :] / row_mean
        updated_weights.append(
            weights_before[position] - learn_rate * gradients[position] * lax.rsqrt(denominator)
        )
        columns_after.append(columns_new)
    gains_gradient = summed[5] * gradient_scale
    table_gradient = summed[6] * gradient_scale
    gains_moment_new = decay_rate * gains_moment + (1.0 - decay_rate) * (
        gains_gradient * gains_gradient + tiny_term
    )
    gains_updated = norm_gains - learn_rate * gains_gradient * lax.rsqrt(gains_moment_new)
    table_moment_new = decay_rate * table_moment + (1.0 - decay_rate) * (
        table_gradient * table_gradient + tiny_term
    )
    table_updated = bias_table - learn_rate * table_gradient * lax.rsqrt(table_moment_new)
    return (
        layer_output,
        input_gradient,
        gains_gradient,
        table_gradient,
        gradients[0],
        gradients[1],
        gradients[2],
        gradients[3],
        gains_updated,
        table_updated,
        updated_weights[0],
        updated_weights[1],
        updated_weights[2],
        updated_weights[3],
        row_after[0],
        columns_after[0],
        row_after[1],
        columns_after[1],
        row_after[2],
        columns_after[2],
        row_after[3],
        columns_after[3],
        gains_moment_new,
        table_moment_new,
    )


def solution(mesh):
    placed = (
        P("dp", "seq", None),
        P("dp", "seq", None),
        P("dp", None),
        P("dp", "seq", None),
        P(),
        P(),
        P(("seq", "dp"), None),
        P(("seq", "dp"), None),
        P(("seq", "dp"), None),
        P(("seq", "dp"), None),
        P(("seq", "dp")),
        P(),
        P(("seq", "dp")),
        P(),
        P(("seq", "dp")),
        P(),
        P(("seq", "dp")),
        P(),
        P(),
        P(),
    )
    return jax.shard_map(
        body,
        mesh=mesh,
        in_specs=placed,
        out_specs=(
            P("dp", "seq", None),
            P("dp", "seq", None),
            P(),
            P(),
            P(("seq", "dp"), None),
            P(("seq", "dp"), None),
            P(("seq", "dp"), None),
            P(("seq", "dp"), None),
            P(),
            P(),
            P(("seq", "dp"), None),
            P(("seq", "dp"), None),
            P(("seq", "dp"), None),
            P(("seq", "dp"), None),
            P(("seq", "dp")),
            P(),
            P(("seq", "dp")),
            P(),
            P(("seq", "dp")),
            P(),
            P(("seq", "dp")),
            P(),
            P(),
            P(),
        ),
        check_vma=False,
    )
```

```python
import functools
import math

import jax
import jax.numpy as jnp
from jax import lax
from jax.experimental import pallas as pl
from jax.experimental.pallas import tpu as pltpu
from jax.sharding import PartitionSpec as P

D = 768
HEADS = 12
HEAD = 64
BLK = 128
PAIR = 2 * HEAD
PAIRS = HEADS // 2
DOCS = 5
TERMS = 3

score_scale = 0.125
masked_score = -1e30
norm_epsilon = 1e-06
tiny_term = 1e-30
learn_rate = 0.3
decay_rate = 1.0 - 2.0 ** (-0.8)
vmem_bytes = 56 * 2**20
open_vmem = 48 * 2**20
back_vmem = 48 * 2**20
close_vmem = 48 * 2**20
apply_vmem = 16 * 2**20
middle_vmem = 52 * 2**20

low_type = jnp.bfloat16
f32 = jnp.float32


def dot(former, latter, former_axis, latter_axis):
    return lax.dot_general(
        former,
        latter,
        (((former_axis,), (latter_axis,)), ((), ())),
        preferred_element_type=f32,
    )


def rms_norm(values, gain_vector):
    return (
        values
        * lax.rsqrt(jnp.mean(values * values, axis=-1, keepdims=True) + norm_epsilon)
        * gain_vector
    )


def documents(lengths, row_length):
    doc_ends = jnp.cumsum(lengths)
    position = jnp.arange(row_length, dtype=jnp.int32)
    return jnp.sum((position[:, None] >= doc_ends[None, :]).astype(jnp.int32), axis=1)


def split_terms(values):
    terms = []
    rest = values
    for _ in range(TERMS):
        term = lax.reduce_precision(rest, 8, 7)
        terms.append(term)
        rest = rest - term
    return terms


def extra_columns(blocks):
    return TERMS * blocks, TERMS * blocks + DOCS


def query_extra(doc_query, blocks):
    count = doc_query.shape[0]
    doc_start, one_start = extra_columns(blocks)
    lane = lax.broadcasted_iota(jnp.int32, (count, 128), 1)
    block = lax.broadcasted_iota(jnp.int32, (count, 128), 0) // BLK
    is_block = (lane < doc_start) & (lane % blocks == block)
    is_doc = (lane >= doc_start) & (lane < one_start) & (lane - doc_start == doc_query[:, None])
    return (is_block | is_doc).astype(low_type)


def key_picks(bucket_rows, doc_all, buckets):
    blocks, row_length = bucket_rows.shape
    one_hot = (
        bucket_rows.T[:, :, None] == jnp.arange(buckets, dtype=jnp.int32)[None, None, :]
    ).reshape(row_length, blocks * buckets)
    other_doc = doc_all[:, None] != jnp.arange(DOCS, dtype=jnp.int32)[None, :]
    ones = jnp.ones((row_length, 1), jnp.bool_)
    return jnp.concatenate([one_hot, other_doc, ones], axis=1).astype(low_type)


def key_extra(picks, bias_table, blocks):
    buckets = bias_table.shape[0]
    doc_start, one_start = extra_columns(blocks)
    terms = jnp.stack(split_terms(bias_table), axis=0)
    lane = jnp.arange(128, dtype=jnp.int32)
    place = jnp.clip(lane // blocks, 0, TERMS - 1)
    spread = jnp.transpose(terms[place], (1, 2, 0))
    at_block = (lane[None, :] % blocks == jnp.arange(blocks, dtype=jnp.int32)[:, None]) & (
        lane[None, :] < doc_start
    )
    bias_part = jnp.where(at_block[:, None, None, :], spread[None], 0.0).reshape(
        blocks * buckets, HEADS, 128
    )
    doc_part = jnp.where(
        lane[None, :] - doc_start == jnp.arange(DOCS, dtype=jnp.int32)[:, None], masked_score, 0.0
    )
    one_part = ((lane >= one_start) & (lane < one_start + TERMS)).astype(f32)[None]
    rest = jnp.concatenate([doc_part, one_part], axis=0)
    rest = jnp.broadcast_to(rest[:, None, :], (DOCS + 1, HEADS, 128))
    whole = jnp.concatenate([bias_part, rest], axis=0).reshape(-1, HEADS * 128).astype(low_type)
    return dot(picks, whole, 1, 0).astype(low_type)


def forward_kernel(queries, extra, keys, values_t, keys_extra, context_t, log_total):
    count = queries.shape[0]
    lane = lax.broadcasted_iota(jnp.int32, (count, PAIR), 1)
    query_pair = queries[...]
    for head in range(2):
        mine = (lane < HEAD) if head == 0 else (lane >= HEAD)
        query_side = jnp.concatenate(
            [jnp.where(mine, query_pair, jnp.zeros_like(query_pair)), extra[...]], axis=1
        )
        key_side = jnp.concatenate([keys[...], keys_extra[:, 128 * head : 128 * head + 128]], axis=1)
        scores = dot(key_side, query_side, 1, 1)
        top = jnp.max(scores, axis=0, keepdims=True)
        unscaled = jnp.exp(scores - top).astype(low_type)
        value_side = jnp.concatenate(
            [
                values_t[HEAD * head : HEAD * head + HEAD, :],
                jnp.ones((16, unscaled.shape[0]), low_type),
            ],
            axis=0,
        )
        weighted = dot(value_side, unscaled, 1, 0)
        total = weighted[HEAD : HEAD + 1]
        context_t[pl.ds(HEAD * head, HEAD), :] = weighted[:HEAD] / total
        log_total[pl.ds(8 * head, 8), :] = jnp.broadcast_to(top + jnp.log(total), (8, count))


def attend(queries, extra, keys, values_t, keys_extra):
    count, row_length = queries.shape[0], keys.shape[0]
    return pl.pallas_call(
        forward_kernel,
        grid=(PAIRS,),
        out_shape=[
            jax.ShapeDtypeStruct((D, count), f32),
            jax.ShapeDtypeStruct((HEADS * 8, count), f32),
        ],
        in_specs=[
            pl.BlockSpec((count, PAIR), lambda pair: (0, pair)),
            pl.BlockSpec((count, 128), lambda pair: (0, 0)),
            pl.BlockSpec((row_length, PAIR), lambda pair: (0, pair)),
            pl.BlockSpec((PAIR, row_length), lambda pair: (pair, 0)),
            pl.BlockSpec((row_length, 256), lambda pair: (0, pair)),
        ],
        out_specs=[
            pl.BlockSpec((PAIR, count), lambda pair: (pair, 0)),
            pl.BlockSpec((16, count), lambda pair: (pair, 0)),
        ],
        compiler_params=pltpu.CompilerParams(vmem_limit_bytes=vmem_bytes),
        cost_estimate=pl.CostEstimate(
            flops=4 * HEADS * count * row_length * 256,
            bytes_accessed=HEADS * row_length * 1024,
            transcendentals=HEADS * count * row_length,
        ),
        name="attention_forward",
    )(queries, extra, keys, values_t, keys_extra)


MESH = pl.DeviceIdType.MESH


class Place:
    def __init__(self):
        self.seq, self.dp = lax.axis_index("seq"), lax.axis_index("dp")
        self.core, self.x, self.y = self.dp % 2, self.dp // 2 % 2, self.dp // 4
        self.by_core = (self.seq, self.dp + 1 - 2 * self.core)
        self.by_x = (self.seq, self.dp + 2 - 4 * self.x)
        self.by_y = (self.seq, self.dp + 4 - 8 * self.y)
        self.plane = [(self.seq, (self.dp + step) % 8) for step in range(1, 8)]
        self.others = [((self.seq + step) % 4, self.dp) for step in (1, 2, 3)]

    def turn(self, block):
        flip = 3 - self.seq
        return 2 * ((block // 2 + flip // 2) % 2) + (block + flip) % 2

    def greet(self, whole_plane=False):
        barrier = pltpu.get_barrier_semaphore()
        beside = self.plane if whole_plane else [self.by_core, self.by_x, self.by_y]
        partners = beside + self.others
        for partner in partners:
            pl.semaphore_signal(barrier, inc=1, device_id=partner, device_id_type=MESH)
        pl.semaphore_wait(barrier, len(partners))


def send(source, target, sems, index, partner):
    return pltpu.make_async_remote_copy(
        src_ref=source,
        dst_ref=target,
        send_sem=sems.at[0, index],
        recv_sem=sems.at[1, index],
        device_id=partner,
        device_id_type=MESH,
    )


def half_of(start, width, which):
    return pl.ds(pl.multiple_of(start + which * (width // 2), 128), width // 2)


class Gather:
    steps = 6

    def __init__(self, at, plan, shard, whole, pair, low, sems, local_sems):
        _, start, width, x_first = plan
        self.at, self.shard, self.pair, self.low, self.whole = at, shard, pair, low, whole
        rows = shard.shape[0]
        mine, other = half_of(start, width, at.core), half_of(start, width, 1 - at.core)
        own_rows = pl.ds(pl.multiple_of(rows * at.core, 8), rows)
        place = whole.at[at.seq, at.y, at.x, :, mine]
        along_x, along_y = (whole.at[:, at.y, at.x, :, mine], whole.at[:, at.y, :, :, mine])
        if not x_first:
            along_x, along_y = (whole.at[:, :, at.x, :, mine], along_x)
        self.local = [
            pltpu.make_async_copy(shard.at[:, mine], pair.at[own_rows], local_sems.at[0]),
            pltpu.make_async_copy(low, place, local_sems.at[1]),
        ]
        self.first = send(shard.at[:, other], pair.at[own_rows], sems, 0, at.by_core)
        self.over_z = [send(low, place, sems, 1 + k, at.others[k]) for k in range(3)]
        self.over_x = send(along_x, along_x, sems, 4, at.by_x)
        self.over_y = send(along_y, along_y, sems, 5, at.by_y)
        self.order = [self.over_x, self.over_y] if x_first else [self.over_y, self.over_x]
        self.last = send(whole.at[:, :, :, :, mine], whole.at[:, :, :, :, mine], sems, 6, at.by_core)

    def step(self, number):
        if number == 0:
            self.local[0].start()
            self.first.start()
        elif number == 1:
            self.local[0].wait()
            self.first.wait()
            self.low[...] = self.pair[...].astype(low_type)
            self.local[1].start()
            for copy in self.over_z:
                copy.start()
        elif number == 2:
            self.local[1].wait()
            for copy in self.over_z:
                copy.wait()
            self.order[0].start()
        elif number == 3:
            self.order[0].wait()
            self.order[1].start()
        elif number == 4:
            self.order[1].wait()
            self.last.start()
        else:
            self.last.wait()


class ScatterPlane:
    steps = 5

    def __init__(self, at, plan, term, kept, held, arrived, sems, local_sems):
        _, start, width, self.x_first = plan
        self.at, self.held, self.arrived = at, held, arrived
        mine, other = half_of(start, width, at.core), half_of(start, width, 1 - at.core)
        self.local = [
            pltpu.make_async_copy(term.at[:, :, :, :, mine], held, local_sems.at[0]),
            pltpu.make_async_copy(held.at[:, at.y, at.x], kept, local_sems.at[1]),
        ]
        self.first = send(term.at[:, :, :, :, other], arrived[0], sems, 0, at.by_core)
        if self.x_first:
            self.second = send(held.at[:, :, 1 - at.x], arrived[1], sems, 1, at.by_x)
            self.third = send(held.at[:, 1 - at.y, at.x], arrived[2], sems, 2, at.by_y)
        else:
            self.second = send(held.at[:, 1 - at.y], arrived[1], sems, 1, at.by_y)
            self.third = send(held.at[:, at.y, 1 - at.x], arrived[2], sems, 2, at.by_x)

    def add(self, place, values):
        self.held[place] = (self.held[place].astype(f32) + values.astype(f32)).astype(low_type)

    def step(self, number):
        at = self.at
        if number == 0:
            self.local[0].start()
            self.first.start()
        elif number == 1:
            self.local[0].wait()
            self.first.wait()

            @pl.loop(0, 4)
            def _(row):
                for across in range(4):
                    place = (row, across // 2, across % 2)
                    self.add(place, self.arrived[0][place])

            self.second.start()
        elif number == 2:
            self.second.wait()

            @pl.loop(0, 4)
            def _(row):
                for across in range(2):
                    place = (row, across, at.x) if self.x_first else (row, at.y, across)
                    self.add(place, self.arrived[1][row, across])

            self.third.start()
        elif number == 3:
            self.third.wait()

            @pl.loop(0, 4)
            def _(row):
                self.add((row, at.y, at.x), self.arrived[2][row])

            self.local[1].start()
        else:
            self.local[1].wait()


class ScatterLine:
    def __init__(self, at, share_start, kept, share, own, arrived, total, sems, local_sems):
        self.at, self.own, self.arrived, self.total = at, own, arrived, total
        rows, half = total.shape[0] // 2, total.shape[1]
        of_core = lambda which: pl.ds(pl.multiple_of(rows * which, 8), rows)
        mine = half_of(share_start, 2 * half, at.core)
        self.local = [
            pltpu.make_async_copy(kept.at[at.seq], own, local_sems.at[0]),
            pltpu.make_async_copy(
                total.at[of_core(at.core)], share.at[:, mine], local_sems.at[1]
            ),
        ]
        self.over_z = [
            send(kept.at[at.others[k][0]], arrived.at[k], sems, k, at.others[k]) for k in range(3)
        ]
        self.last = send(total.at[of_core(1 - at.core)], share.at[:, mine], sems, 3, at.by_core)

    def step(self, number):
        if number == 0:
            self.local[0].start()
            for copy in self.over_z:
                copy.start()
        elif number == 1:
            self.local[0].wait()
            for copy in self.over_z:
                copy.wait()
            total = self.own[...].astype(f32)
            for k in range(3):
                total = total + self.arrived[k].astype(f32)
            self.total[...] = total
            self.local[1].start()
            self.last.start()
        else:
            self.local[1].wait()
            self.last.wait()


class Ring:
    def __init__(self, at, own, blocks, sems, local_sem):
        self.at = at
        seq = at.seq
        self.local = pltpu.make_async_copy(own, blocks.at[seq], local_sem)
        right, left = ((seq + 1) % 4, at.dp), ((seq + 3) % 4, at.dp)
        half = own.shape[0] // 2
        self.hops = []
        for number, (hop, rows) in enumerate(
            ((0, pl.ds(0, 2 * half)), (1, pl.ds(0, 2 * half)), (2, pl.ds(0, half)), (2, pl.ds(half, half)))
        ):
            back, ahead = blocks.at[(seq + 4 - hop) % 4, rows], blocks.at[(seq + hop) % 4, rows]
            self.hops.append(
                [
                    (
                        (seq >= hop) & (seq < 3),
                        send(own if hop == 0 else back, back, sems, number, right),
                        seq >= hop + 1,
                    ),
                    (
                        (seq + hop <= 3) & (seq > 0),
                        send(own if hop == 0 else ahead, ahead, sems, 4 + number, left),
                        seq + hop + 1 <= 3,
                    ),
                ]
            )

    def start(self, hop):
        if hop == 0:
            self.local.start()
        for sends, copy, _ in self.hops[hop]:
            pl.when(sends)(copy.start)

    def arrive(self, hop):
        for _, copy, receives in self.hops[hop]:
            pl.when(receives)(copy.wait_recv)

    def finish(self):
        for hop in self.hops:
            for sends, copy, _ in hop:
                pl.when(sends)(copy.wait_send)


GATHERS = (
    (0, 0, 1280, True),
    (0, 1280, 1024, False),
    (1, 0, D, False),
    (2, 0, 512, True),
    (2, 512, 2560, False),
    (3, 0, D, True),
)


def opening_kernel(*refs):
    shards, own = refs[:4], refs[4]
    gains, bucket_rows, bias_table, lengths = refs[5:9]
    wholes, outs = refs[9:13], refs[13:18]
    normed_out, keys_out, values_out, keys_extra_out, picks_out = outs
    queries, queries_t, context_t, log_total, extra = refs[18:23]
    scratch = refs[23:]
    many = len(GATHERS)
    of_gathers, scratch = scratch[: 4 * many], scratch[4 * many :]
    ring_sems, ring_local, out_sems, blocks, project, normed, keys, values_t = scratch[:8]
    keys_extra, picks, sums, tops = scratch[8:]
    at = Place()
    at.greet()
    gathers = [
        Gather(
            at,
            plan,
            shards[plan[0]],
            project if plan[0] == 0 else wholes[plan[0]],
            *of_gathers[4 * k : 4 * k + 4],
        )
        for k, plan in enumerate(GATHERS)
    ]
    ring = Ring(at, own, blocks, ring_sems, ring_local.at[0])

    def first_step(number):
        for gather in gathers[:2]:
            gather.step(number)

    def rest_step(number):
        for gather in gathers[2:]:
            gather.step(number)

    first_step(0)
    rest_step(0)
    first_step(1)
    ring.start(0)

    count, buckets = own.shape[0], bias_table.shape[0]
    row_length = keys_extra.shape[0]
    query_blocks = count // BLK
    doc_start, one_start = extra_columns(query_blocks)
    picked = query_blocks * buckets
    ends = []
    for doc in range(DOCS):
        ends.append(lengths[0, doc] + (ends[-1] if ends else 0))

    def documents_at(position):
        return sum((position >= end).astype(jnp.int32) for end in ends)

    bucket_at = lax.broadcasted_iota(jnp.int32, (buckets, row_length), 0)
    for block in range(query_blocks):
        picks[buckets * block : buckets * block + buckets, :] = (
            (bucket_rows[block : block + 1, :] == bucket_at).astype(f32).astype(low_type)
        )
    last = picks.shape[0] - picked
    row = lax.broadcasted_iota(jnp.int32, (last, row_length), 0)
    key_doc = documents_at(lax.broadcasted_iota(jnp.int32, (last, row_length), 1))
    picks[picked:, :] = (
        jnp.where(row < DOCS, (key_doc != row).astype(f32), (row == DOCS).astype(f32))
    ).astype(low_type)

    table = jnp.concatenate([bias_table[...]] * query_blocks, axis=0)
    table_lane = lax.broadcasted_iota(jnp.int32, table.shape, 1)
    lane = lax.broadcasted_iota(jnp.int32, (picked, 128), 1)
    lane_block = lax.broadcasted_iota(jnp.int32, (picked, 128), 0) // buckets
    lane_last = lax.broadcasted_iota(jnp.int32, (last, 128), 1)
    row_last = lax.broadcasted_iota(jnp.int32, (last, 128), 0)
    below = jnp.where(
        (row_last < DOCS) & (lane_last - doc_start == row_last),
        masked_score,
        jnp.where(
            (row_last == DOCS) & (lane_last >= one_start) & (lane_last < one_start + TERMS), 1.0, 0.0
        ),
    ).astype(low_type)

    first_step(2)
    rest_step(1)

    def make_extra(pair):
        sides = []
        for head in range(2):
            rest_of = jnp.sum(
                jnp.where(table_lane == 2 * pair + head, table, 0.0), axis=1, keepdims=True
            )
            side = jnp.zeros((picked, 128), f32)
            for term in range(TERMS):
                part = rest_of.astype(low_type).astype(f32)
                rest_of = rest_of - part
                side = jnp.where(lane == term * query_blocks + lane_block, part, side)
            sides.append(jnp.concatenate([side.astype(low_type), below], axis=0))
        keys_extra[:, pl.ds(pl.multiple_of(256 * pair, 256), 256)] = dot(
            picks[...], jnp.concatenate(sides, axis=1), 0, 0
        ).astype(low_type)

    pl.loop(0, PAIRS // 2)(make_extra)
    first_step(3)
    pl.loop(PAIRS // 2, PAIRS)(make_extra)
    first_step(4)
    extra_lane = lax.broadcasted_iota(jnp.int32, (count, 128), 1)
    extra_row = lax.broadcasted_iota(jnp.int32, (count, 128), 0)
    query_doc = documents_at(extra_row + at.seq * count)
    extra[...] = (
        (
            ((extra_lane < doc_start) & (extra_lane % query_blocks == extra_row // BLK))
            | ((extra_lane < one_start) & (extra_lane - doc_start == query_doc))
        )
        .astype(f32)
        .astype(low_type)
    )
    sums[...] = jnp.zeros_like(sums)
    tops[...] = jnp.full_like(tops, masked_score)
    ring.local.wait()
    first_step(5)

    copies = [pltpu.make_async_copy(project, wholes[0], out_sems.at[0])]
    for block in range(4):
        columns = pl.ds(count * block, count)
        into = pl.ds(pl.multiple_of(count * at.turn(block), count), count)
        copies += [
            pltpu.make_async_copy(
                keys_extra.at[columns], keys_extra_out.at[into], out_sems.at[1 + block]
            ),
            pltpu.make_async_copy(
                picks.at[:, columns], picks_out.at[:, into], out_sems.at[5 + block]
            ),
        ]
    for copy in copies:
        copy.start()
    weights = [project[:, :, :, :, D * part : D * part + D].reshape(D, D) for part in range(3)]
    pair_lane = lax.broadcasted_iota(jnp.int32, (count, PAIR), 1)

    def attend_pair(block, rows, pair):
        lanes = pl.ds(pl.multiple_of(pair * PAIR, PAIR), PAIR)
        start = block * count + rows.start
        key_rows = pl.ds(pl.multiple_of(start, rows.size), rows.size)
        query_pair, key_pair = queries[:, lanes], keys[block, rows, lanes]
        for head in range(2):
            which = 2 * pair + head
            mine = (pair_lane < HEAD) if head == 0 else (pair_lane >= HEAD)
            query_side = jnp.concatenate(
                [jnp.where(mine, query_pair, jnp.zeros_like(query_pair)), extra[...]], axis=1
            )
            more = keys_extra[key_rows, pl.ds(pl.multiple_of(128 * which, 128), 128)]
            scores = dot(jnp.concatenate([key_pair, more], axis=1), query_side, 1, 1)
            top_before = tops[which, 0:1]
            top = jnp.maximum(top_before, jnp.max(scores, axis=0, keepdims=True))
            unscaled = jnp.exp(scores - top).astype(low_type)
            value_side = jnp.concatenate(
                [
                    values_t[block, pl.ds(pl.multiple_of(HEAD * which, HEAD), HEAD), rows],
                    jnp.ones((16, rows.size), low_type),
                ],
                axis=0,
            )
            sums[which] = sums[which] * jnp.exp(top_before - top) + dot(value_side, unscaled, 1, 0)
            tops[which] = jnp.broadcast_to(top, (8, count))

    side = at.seq // 2
    order = [at.seq, 1 - at.seq + 4 * side, 2 - side, 3 - 3 * side]
    whole_block, halves = pl.ds(0, count), [pl.ds(0, count // 2), pl.ds(count // 2, count // 2)]
    passes = [(block, whole_block) for block in order[:3]] + [(order[3], rows) for rows in halves]
    events = {
        (0, 0): [lambda: (ring.arrive(0), ring.start(1))],
        (0, 5): [lambda: rest_step(2)],
        (1, 4): [lambda: rest_step(3)],
        (1, 5): [lambda: (ring.arrive(1), ring.start(2), ring.start(3))],
        (2, 5): [lambda: ring.arrive(2)],
        (3, 3): [lambda: rest_step(4)],
        (3, 5): [lambda: ring.arrive(3)],
    }
    for number, (block, rows) in enumerate(passes):
        values = blocks[block, rows].astype(f32)
        normed_low = (
            values
            * lax.rsqrt(jnp.mean(values * values, axis=1, keepdims=True) + norm_epsilon)
            * gains[0:1, :]
        ).astype(low_type)
        normed[block, rows] = normed_low
        keys[block, rows] = dot(normed_low, weights[1], 1, 0).astype(low_type)
        values_t[block, :, rows] = dot(weights[2], normed_low, 0, 1).astype(low_type)
        turn = at.turn(block)
        for place, (source, target, index) in enumerate(
            (
                (normed, normed_out, (rows,)),
                (keys, keys_out, (rows,)),
                (values_t, values_out, (slice(None), rows)),
            )
        ):
            copy = pltpu.make_async_copy(
                source.at[(block, *index)],
                target.at[(turn, *index)],
                out_sems.at[9 + 3 * number + place],
            )
            copy.start()
            copies.append(copy)
        if number == 0:
            scaled = lambda values: (values.astype(low_type).astype(f32) * score_scale).astype(low_type)
            queries[...] = scaled(dot(normed_low, weights[0], 1, 0))
            queries_t[...] = scaled(dot(weights[0], normed_low, 0, 1))

        @pl.loop(0, PAIRS)
        def _(pair, number=number, block=block, rows=rows):
            for (when, which), actions in events.items():
                if when == number:

                    @pl.when(pair == which)
                    def _(actions=actions):
                        for action in actions:
                            action()

            attend_pair(block, rows, pair)

    for head in range(HEADS):
        total = sums[head, HEAD : HEAD + 1]
        context_t[HEAD * head : HEAD * head + HEAD, :] = sums[head, :HEAD] / total
        log_total[head : head + 1, :] = tops[head, 0:1] + jnp.log(total)
    rest_step(5)
    ring.finish()
    for copy in copies:
        copy.wait()


def open_layer(shards, own, gains, bucket_rows, bias_table, lengths):
    shards = [pltpu.with_memory_space_constraint(shard, pltpu.HBM) for shard in shards]
    own = pltpu.with_memory_space_constraint(own, pltpu.HBM)
    anywhere = pl.BlockSpec(memory_space=pl.ANY)
    in_place = pl.BlockSpec(memory_space=pltpu.VMEM)
    count, blocks = own.shape[0], bucket_rows.shape[0]
    row_length = 4 * count
    picked = blocks * bias_table.shape[0] + 16
    low = lambda *shape: jax.ShapeDtypeStruct(shape, low_type)
    whole_shapes = [(4, 2, 2, 2 * shard.shape[0], shard.shape[1]) for shard in shards]
    of_gathers = []
    for which, _, width, _ in GATHERS:
        half = (2 * shards[which].shape[0], width // 2)
        of_gathers += [
            pltpu.VMEM(half, f32),
            pltpu.VMEM(half, low_type),
            pltpu.SemaphoreType.DMA((2, 7)),
            pltpu.SemaphoreType.DMA((2,)),
        ]
    return pl.pallas_call(
        opening_kernel,
        out_shape=[low(*shape) for shape in whole_shapes]
        + [low(4, count, D)] * 2
        + [low(4, D, count), low(row_length, HEADS * 128), low(picked, row_length)]
        + [low(count, D), low(D, count)]
        + [jax.ShapeDtypeStruct((D, count), f32), jax.ShapeDtypeStruct((16, count), f32)]
        + [low(count, 128)],
        in_specs=[anywhere] * 5 + [in_place] * 3 + [pl.BlockSpec(memory_space=pltpu.SMEM)],
        out_specs=[anywhere] * 9 + [in_place] * 5,
        scratch_shapes=of_gathers
        + [
            pltpu.SemaphoreType.DMA((2, 8)),
            pltpu.SemaphoreType.DMA((1,)),
            pltpu.SemaphoreType.DMA((24,)),
            pltpu.VMEM((4, count, D), low_type),
            pltpu.VMEM(whole_shapes[0], low_type),
            pltpu.VMEM((4, count, D), low_type),
            pltpu.VMEM((4, count, D), low_type),
            pltpu.VMEM((4, D, count), low_type),
            pltpu.VMEM((row_length, HEADS * 128), low_type),
            pltpu.VMEM((picked, row_length), low_type),
            pltpu.VMEM((HEADS, HEAD + 16, count), f32),
            pltpu.VMEM((HEADS, 8, count), f32),
        ],
        compiler_params=pltpu.CompilerParams(
            collective_id=0, has_side_effects=True, vmem_limit_bytes=open_vmem
        ),
        name="open_layer",
    )(*shards, own, gains, bucket_rows, bias_table, lengths)


def plane_scratch(rows, width):
    half = width // 2
    return [
        pltpu.VMEM((4, 2, 2, rows, half), low_type),
        pltpu.VMEM((4, 2, 2, rows, half), low_type),
        pltpu.VMEM((4, 2, rows, half), low_type),
        pltpu.VMEM((4, rows, half), low_type),
        pltpu.SemaphoreType.DMA((2, 3)),
        pltpu.SemaphoreType.DMA((2,)),
    ]


def line_scratch(rows, width):
    half = width // 2
    return [
        pltpu.VMEM((rows, half), low_type),
        pltpu.VMEM((3, rows, half), low_type),
        pltpu.VMEM((rows, half), f32),
        pltpu.SemaphoreType.DMA((2, 4)),
        pltpu.SemaphoreType.DMA((2,)),
    ]


def take_plane(at, plan, term, kept, scratch):
    return ScatterPlane(at, plan, term, kept, scratch[0], scratch[1:4], scratch[4], scratch[5])


def by_chip(term):
    return term.reshape(4, 2, 2, term.shape[0] // 16, term.shape[1])


class AllSum:
    def __init__(self, at, own, plane, line, sems):
        self.at, self.own, self.plane, self.line = at, own, plane, line
        self.local = pltpu.make_async_copy(own, plane.at[at.dp], sems.at[0, 10])
        self.beside = [
            send(own, plane.at[at.dp], sems, k, partner) for k, partner in enumerate(at.plane)
        ]
        place = line.at[at.seq]
        self.over_z = [
            send(place, place, sems, 7 + k, partner) for k, partner in enumerate(at.others)
        ]

    def step(self, number):
        if number == 0:
            self.local.start()
            for copy in self.beside:
                copy.start()
        elif number == 1:
            self.local.wait()
            for copy in self.beside:
                copy.wait()
            total = self.plane[0]
            for k in range(1, 8):
                total = total + self.plane[k]
            self.line[self.at.seq] = total
            for copy in self.over_z:
                copy.start()
        else:
            for copy in self.over_z:
                copy.wait()

    def total(self):
        return (self.line[0] + self.line[1]) + (self.line[2] + self.line[3])


def sum_scratch(width):
    return [
        pltpu.VMEM((8, width), f32),
        pltpu.VMEM((8, 8, width), f32),
        pltpu.VMEM((4, 8, width), f32),
        pltpu.SemaphoreType.DMA((2, 11)),
    ]


EARLY_WIDTH, LATE_WIDTH = D + 512, D
CLOSE_PLANS = ((2, 0, D, True), (1, 0, D, False), (0, 0, D, True))


def split_low(values):
    terms = []
    for _ in range(TERMS):
        terms.append(values.astype(low_type))
        values = values - terms[-1].astype(f32)
    return terms


def close_kernel(scale, *refs):
    normed, key_grad_t, value_grad_t, query_grad, project, key_part_t = refs[:6]
    inputs, residual_grad, folded, picks, gains, gain_two, own_weight = refs[6:13]
    kept_rest, rows_before, refs = refs[13:18], refs[18:22], refs[22:]
    input_grad, shares, early_total, late_total = refs[0], refs[1:5], refs[5], refs[6]
    scratch = refs[7:]
    normed_in, key_in, value_in, weight_in, part_in, residual_in, load_sems = scratch[:7]
    early, late, scratch = scratch[7:11], scratch[11:15], scratch[15:]
    terms, kept, scratch = scratch[:3], scratch[3:6], scratch[6:]
    at = Place()
    loads = [
        pltpu.make_async_copy(source, target, load_sems.at[k])
        for k, (source, target) in enumerate(
            (
                (normed.at[3], normed_in.at[3]),
                (value_grad_t, value_in),
                (normed.at[pl.ds(0, 3)], normed_in.at[pl.ds(0, 3)]),
                (key_grad_t, key_in),
                (project.at[:, 0:D], weight_in),
                (key_part_t, part_in),
                (residual_grad, residual_in),
            )
        )
    ]
    for load in loads:
        load.start()
    at.greet(whole_plane=True)
    planes, lines = [], []
    for k, plan in enumerate(CLOSE_PLANS):
        planes.append(take_plane(at, plan, terms[k], kept[k], scratch[:6]))
        lines.append(ScatterLine(at, D * plan[0], kept[k], shares[0], *scratch[6:11]))
        scratch = scratch[11:]
    rest_lines = []
    for k, (which, start, _, _) in enumerate(BACK_PLANS):
        rest_lines.append(
            ScatterLine(at, start, kept_rest[k], shares[which + 1], *scratch[5 * k : 5 * k + 5])
        )
    first, second = AllSum(at, *early), AllSum(at, *late)

    for line in rest_lines:
        line.step(0)
    early_own, late_own = early[0], late[0]
    early_own[...] = jnp.zeros_like(early_own)
    late_own[...] = jnp.zeros_like(late_own)
    count = inputs.shape[0]
    query_low = (query_grad[...] * score_scale).astype(low_type)

    def put(term, values):
        term[...] = values.astype(low_type).reshape(term.shape)

    def of_row(parts):
        whole = normed_in[...].reshape(4 * count, D)
        return dot(parts[...], whole, 1, 0).astype(low_type).T

    loads[0].wait()
    put(terms[2], dot(normed_in[3], query_low, 0, 0))
    planes[2].step(0)
    loads[1].wait()
    loads[2].wait()
    put(terms[0], of_row(value_in))
    planes[0].step(0)
    planes[2].step(1)
    loads[3].wait()
    put(terms[1], of_row(key_in))
    planes[1].step(0)
    planes[2].step(2)
    planes[0].step(1)

    for load in loads[4:]:
        load.wait()
    scaled = (dot(query_low, weight_in[...], 1, 1) + part_in[...].T) * gains[0:1, :]
    planes[1].step(1)
    planes[0].step(2)
    planes[2].step(3)
    planes[2].step(4)
    lines[2].step(0)
    source = inputs[...].astype(f32)
    inverse = lax.rsqrt(jnp.mean(source * source, axis=1, keepdims=True) + norm_epsilon)
    along = jnp.mean(source * scaled, axis=1, keepdims=True)
    input_grad[...] = (
        residual_in[...] + inverse * scaled - source * (inverse * inverse * inverse * along)
    ).astype(low_type)
    planes[1].step(2)
    planes[0].step(3)
    planes[0].step(4)
    lines[0].step(0)

    blocks = query_blocks_of(picks.shape[0])
    buckets = (picks.shape[0] - 16) // blocks
    rows = folded.shape[0] * folded.shape[1]
    flat = split_low(folded[...].reshape(rows, folded.shape[2]))
    parted = dot(jnp.concatenate(flat, axis=0), picks[: blocks * buckets, :], 1, 1)
    parted = parted[:rows] + parted[rows : 2 * rows] + parted[2 * rows :]
    row = lax.broadcasted_iota(jnp.int32, parted.shape, 0) % folded.shape[1]
    lane = lax.broadcasted_iota(jnp.int32, parted.shape, 1)
    parted = jnp.where(row == lane // buckets, parted, 0.0)
    at_bucket = (
        lax.broadcasted_iota(jnp.int32, (blocks * buckets, buckets), 0) % buckets
        == lax.broadcasted_iota(jnp.int32, (blocks * buckets, buckets), 1)
    )
    at_bucket = at_bucket.astype(f32).astype(low_type)
    table = sum(dot(term, at_bucket, 1, 0) for term in split_low(parted))
    table = jnp.sum(table.reshape(HEADS, folded.shape[1], buckets), axis=1)
    early_own[:, D + 256 : D + 256 + buckets] = table[:8]
    early_own[0 : HEADS - 8, D + 384 : D + 384 + buckets] = table[8:]
    early_own[2:3, :D] = gain_two[...]

    planes[1].step(3)
    planes[1].step(4)
    lines[1].step(0)
    for line in rest_lines:
        line.step(1)

    def statistics(raw, previous):
        gradient = raw * scale
        squares = gradient * gradient + tiny_term
        means = jnp.sum(jnp.mean(squares, axis=1, keepdims=True), axis=0, keepdims=True)
        before = jnp.sum(previous.reshape(1, previous.shape[0]), axis=1, keepdims=True)
        row_sum = decay_rate * before + (1.0 - decay_rate) * means
        return jnp.sum(squares, axis=0, keepdims=True), jnp.broadcast_to(row_sum, (1, 128))

    lines[2].step(1)
    lines[0].step(1)
    for line in rest_lines:
        line.step(2)
    for position in (1, 2, 3):
        columns, row_sum = statistics(shares[position][...], rows_before[position][...])
        early_own[position : position + 1, D : D + 128] = row_sum
        if position == 2:
            for part in range(4):
                early_own[4 + part : 5 + part, :D] = columns[:, D * part : D * part + D]
        else:
            early_own[position // 2 : position // 2 + 1, :D] = columns
    first.step(0)
    lines[1].step(1)
    first.step(1)
    for line in lines:
        line.step(2)

    raw = shares[0][...]
    columns, row_sum = statistics(raw, rows_before[0][...])
    for part in range(3):
        late_own[part : part + 1, :] = columns[:, D * part : D * part + D]
    late_own[4:5, :128] = row_sum
    own_rows = raw.shape[0]
    lane = lax.broadcasted_iota(jnp.int32, (own_rows, D), 1)
    row = lax.broadcasted_iota(jnp.int32, (own_rows, D), 0)
    mine = lane == row + (at.seq * 8 + at.dp) * own_rows
    gain_one = jnp.sum(
        raw * own_weight[...].astype(low_type).astype(f32), axis=1, keepdims=True
    )
    spread = jnp.where(mine, jnp.broadcast_to(gain_one, (own_rows, D)), 0.0)
    late_own[3:4, :] = jnp.sum(spread, axis=0, keepdims=True) / gains[0:1, :]
    second.step(0)
    first.step(2)
    early_total[...] = first.total()
    second.step(1)
    second.step(2)
    late_total[...] = second.total()


def query_blocks_of(rows):
    return (rows - 16) // 32


def close(scale, large, small, kept_rest, rows_before, weight_shapes):
    in_place = pl.BlockSpec(memory_space=pltpu.VMEM)
    anywhere = pl.BlockSpec(memory_space=pl.ANY)
    count, row_length = small[0].shape[0], large[1].shape[1]
    scratch = [
        pltpu.VMEM((4, count, D), low_type),
        pltpu.VMEM((D, row_length), low_type),
        pltpu.VMEM((D, row_length), low_type),
        pltpu.VMEM((D, D), low_type),
        pltpu.VMEM((D, count), f32),
        pltpu.VMEM((count, D), f32),
        pltpu.SemaphoreType.DMA((7,)),
    ]
    scratch += sum_scratch(EARLY_WIDTH) + sum_scratch(LATE_WIDTH)
    scratch += [pltpu.VMEM((4, 2, 2, D // 16, D), low_type)] * 3
    scratch += [pltpu.VMEM((4, D // 16, D // 2), low_type)] * 3
    for _ in CLOSE_PLANS:
        scratch += plane_scratch(D // 16, D) + line_scratch(D // 16, D)
    for which, _, width, _ in BACK_PLANS:
        scratch += line_scratch(2 * weight_shapes[which + 1][0], width)
    return pl.pallas_call(
        functools.partial(close_kernel, scale),
        out_shape=[jax.ShapeDtypeStruct((count, D), low_type)]
        + [jax.ShapeDtypeStruct(shape, f32) for shape in weight_shapes]
        + [
            jax.ShapeDtypeStruct((8, EARLY_WIDTH), f32),
            jax.ShapeDtypeStruct((8, LATE_WIDTH), f32),
        ],
        in_specs=[anywhere] * 3
        + [in_place]
        + [anywhere] * 2
        + [in_place, anywhere]
        + [in_place] * 5
        + [anywhere] * 5
        + [in_place] * 4,
        out_specs=[in_place] * 7,
        scratch_shapes=scratch,
        compiler_params=pltpu.CompilerParams(
            collective_id=2, has_side_effects=True, vmem_limit_bytes=close_vmem
        ),
        name="close_layer",
    )(*large, *small, *kept_rest, *rows_before)


def apply_kernel(scale, *refs):
    shares, early, late, far, refs = refs[:4], refs[4], refs[5], refs[6:22], refs[22:]
    near, load_sems = refs[22:38], refs[38]
    loads = [
        pltpu.make_async_copy(source, target, load_sems.at[k])
        for k, (source, target) in enumerate(zip(far, near))
    ]
    for load in loads:
        load.start()
    for load in loads:
        load.wait()
    weights, rows_before, columns_before = near[:4], near[4:8], near[8:12]
    gains, gains_moment, table, table_moment = near[12:]
    gradients, updated, rows_after, columns_after = refs[:4], refs[4:8], refs[8:12], refs[12:16]
    gains_out, table_out = refs[16:19], refs[19:22]
    early_sums, late_sums = early[...], late[...]
    sums = [
        jnp.concatenate([late_sums[part : part + 1] for part in range(3)], axis=1),
        early_sums[0:1, :D],
        jnp.concatenate([early_sums[4 + part : 5 + part, :D] for part in range(4)], axis=1),
        early_sums[1:2, :D],
    ]
    row_sums = [late_sums[4:5, 0:1]] + [early_sums[k : k + 1, D : D + 1] for k in (1, 2, 3)]
    for position in range(4):
        rows, width = shares[position].shape
        full = rows * 32
        gradient = shares[position][...] * scale
        gradients[position][...] = gradient
        squares = gradient * gradient + tiny_term
        eye = lax.broadcasted_iota(jnp.int32, (rows, rows), 0) == lax.broadcasted_iota(
            jnp.int32, (rows, rows), 1
        )
        before = jnp.broadcast_to(rows_before[position][...].reshape(1, rows), (rows, rows))
        before = jnp.sum(jnp.where(eye, before, 0.0), axis=1, keepdims=True)
        rows_new = decay_rate * before + (1.0 - decay_rate) * jnp.mean(
            squares, axis=1, keepdims=True
        )
        rows_after[position][...] = jnp.sum(
            jnp.where(eye, jnp.broadcast_to(rows_new, (rows, rows)), 0.0), axis=0, keepdims=True
        ).reshape(rows)
        columns_new = decay_rate * columns_before[position][...].reshape(1, width) + (
            1.0 - decay_rate
        ) * (sums[position] / full)
        columns_after[position][...] = columns_new.reshape(width)
        denominator = rows_new * columns_new / (row_sums[position] / full)
        updated[position][...] = weights[position][...] - learn_rate * gradient * lax.rsqrt(
            denominator
        )

    def moments(gradient, old, moment, results):
        moment_new = decay_rate * moment[...] + (1.0 - decay_rate) * (
            gradient * gradient + tiny_term
        )
        results[0][...] = gradient
        results[1][...] = old[...] - learn_rate * gradient * lax.rsqrt(moment_new)
        results[2][...] = moment_new

    moments(
        jnp.concatenate([late_sums[3:4, :D], early_sums[2:3, :D]], axis=0) * scale,
        gains,
        gains_moment,
        gains_out,
    )
    buckets = table.shape[0]
    of_table = jnp.concatenate(
        [
            early_sums[:, D + 256 : D + 256 + buckets],
            early_sums[0 : HEADS - 8, D + 384 : D + 384 + buckets],
        ],
        axis=0,
    )
    moments(of_table.T * scale, table, table_moment, table_out)


def apply_updates(scale, shares, sums, weights, rows_before, columns_before, rest):
    in_place = pl.BlockSpec(memory_space=pltpu.VMEM)
    same = lambda arrays: [jax.ShapeDtypeStruct(array.shape, f32) for array in arrays]
    gains, table = rest[0], rest[2]
    far = [*weights, *rows_before, *columns_before, *rest]
    far = [pltpu.with_memory_space_constraint(array, pltpu.HBM) for array in far]
    return pl.pallas_call(
        functools.partial(apply_kernel, scale),
        out_shape=same(weights)
        + same(weights)
        + same(rows_before)
        + same(columns_before)
        + same([gains] * 3)
        + same([table] * 3),
        in_specs=[in_place] * 6 + [pl.BlockSpec(memory_space=pl.ANY)] * 16,
        out_specs=[in_place] * 22,
        scratch_shapes=[pltpu.VMEM(array.shape, f32) for array in far]
        + [pltpu.SemaphoreType.DMA((16,))],
        compiler_params=pltpu.CompilerParams(vmem_limit_bytes=apply_vmem),
        name="apply_updates",
    )(*shares, *sums, *far)


def middle_kernel(
    context_t,
    log_total,
    inputs,
    upstream,
    gains,
    output_weight,
    expand_weight,
    reduce_weight,
    layer_output,
    residual_grad,
    output_term,
    expand_term,
    reduce_term,
    context_grad,
    context_grad_t,
    row_columns,
    gain_two,
    residual,
    normed,
    normed_t,
    reduced,
    normed_grad,
):
    step = pl.program_id(0)
    gain = gains[1:2, :]

    def inverse():
        values = residual[...]
        return lax.rsqrt(jnp.mean(values * values, axis=1, keepdims=True) + norm_epsilon)

    @pl.when(step == 0)
    def _():
        residual[...] = inputs[...].astype(f32) + dot(
            context_t[...].astype(low_type), output_weight[...], 0, 0
        )
        normed_low = (residual[...] * inverse() * gain).astype(low_type)
        normed[...] = normed_low
        normed_t[...] = normed_low.T
        reduced[...] = jnp.zeros_like(reduced)
        normed_grad[...] = jnp.zeros_like(normed_grad)

    expanded = dot(normed[...], expand_weight[...], 1, 0)
    squared = expanded * expanded
    bent = jnp.tanh(0.7978845608028654 * expanded * (1.0 + 0.044715 * squared))
    above = 0.5 * (1.0 + bent)
    activated = (expanded * above).astype(low_type)
    slope = above + 0.5 * expanded * (1.0 - bent * bent) * (
        0.7978845608028654 * (1.0 + 3.0 * 0.044715 * squared)
    )
    expanded_low = (dot(upstream[...], reduce_weight[...], 1, 1) * slope).astype(low_type)
    reduced[...] += dot(activated, reduce_weight[...], 1, 0)
    reduce_term[...] = dot(activated, upstream[...], 0, 0).astype(low_type)
    normed_grad[...] += dot(expanded_low, expand_weight[...], 1, 1)
    expand_term[...] = dot(normed_t[...], expanded_low, 1, 0).astype(low_type)

    @pl.when(step == pl.num_programs(0) - 1)
    def _():
        values, scale = residual[...], inverse()
        layer_output[...] = (values + reduced[...]).astype(low_type)
        gain_two[...] = jnp.sum(normed_grad[...] * values * scale, axis=0, keepdims=True)
        scaled = normed_grad[...] * gain
        along = jnp.mean(values * scaled, axis=1, keepdims=True)
        gradient = (
            upstream[...].astype(f32)
            + scale * scaled
            - values * (scale * scale * scale * along)
        )
        residual_grad[...] = gradient
        low = gradient.astype(low_type)
        output_term[...] = dot(context_t[...].astype(low_type), low, 1, 0).astype(low_type)
        context_grad[...] = dot(low, output_weight[...], 1, 1).astype(low_type)
        turned = dot(output_weight[...], low, 1, 1).astype(low_type)
        context_grad_t[...] = turned
        count = low.shape[0]
        delta = jnp.sum(
            (turned.astype(f32) * context_t[...]).reshape(HEADS, HEAD, count), axis=1
        )
        rows = jnp.concatenate(
            [log_total[0:HEADS, :], delta, jnp.zeros((128 - 2 * HEADS, count), f32)], axis=0
        )
        row_columns[...] = rows.T


def middle(context_t, log_total, inputs, upstream, gains, output_weight, expand_weight, reduce_weight):
    count = inputs.shape[0]
    hidden = expand_weight.shape[1]
    still = lambda *shape: pl.BlockSpec(shape, lambda step: (0,) * len(shape))
    low = lambda *shape: jax.ShapeDtypeStruct(shape, low_type)
    across = pl.BlockSpec((D, D), lambda step: (0, step))
    down = pl.BlockSpec((D, D), lambda step: (step, 0))
    return pl.pallas_call(
        middle_kernel,
        grid=(hidden // D,),
        out_shape=[
            low(count, D),
            jax.ShapeDtypeStruct((count, D), f32),
            low(D, D),
            low(D, hidden),
            low(hidden, D),
            low(count, D),
            low(D, count),
            jax.ShapeDtypeStruct((count, 128), f32),
            jax.ShapeDtypeStruct((1, D), f32),
        ],
        in_specs=[
            still(D, count),
            still(*log_total.shape),
            still(count, D),
            still(count, D),
            still(2, D),
            still(D, D),
            across,
            down,
        ],
        out_specs=[
            still(count, D),
            still(count, D),
            still(D, D),
            across,
            down,
            still(count, D),
            still(D, count),
            still(count, 128),
            still(1, D),
        ],
        scratch_shapes=[
            pltpu.VMEM((count, D), f32),
            pltpu.VMEM((count, D), low_type),
            pltpu.VMEM((D, count), low_type),
            pltpu.VMEM((count, D), f32),
            pltpu.VMEM((count, D), f32),
        ],
        compiler_params=pltpu.CompilerParams(vmem_limit_bytes=middle_vmem),
        cost_estimate=pl.CostEstimate(
            flops=2 * count * D * (6 * hidden + 4 * D),
            bytes_accessed=8 * D * hidden + 20 * count * D,
            transcendentals=count * hidden,
        ),
        name="middle",
    )(context_t, log_total, inputs, upstream, gains, output_weight, expand_weight, reduce_weight)


BACK_PLANS = (
    (1, 0, 2 * D, False),
    (2, 0, 512, True),
    (1, 2 * D, 2 * D, False),
    (2, 512, 256, True),
    (0, 0, D, True),
)
EARLY, LATE = (0, 1), (2, 3, 4)
BACK_TIMES = (
    (0, None),
    (0, (EARLY, 0)),
    (1, (LATE, 0)),
    (2, (EARLY, 1)),
    (6, (EARLY, 2)),
    (6, (LATE, 1)),
    (9, (EARLY, 3)),
    (11, (LATE, 2)),
    (14, (LATE, 3)),
    (23, (EARLY, 4)),
    (23, (LATE, 4)),
)


class Relay:
    def __init__(self, at, kept, arrived, sems):
        self.kept, self.arrived = kept, arrived
        seq = at.seq
        self.is_end = (seq == 0) | (seq == 3)
        self.is_inner = (seq == 1) | (seq == 2)
        inwards = (1 + seq // 3, at.dp)
        outwards = ((3 * seq + 1) % 4, at.dp)
        across = ((7 - seq) % 4, at.dp)
        self.from_end = [send(kept.at[k], arrived.at[k], sems, k, inwards) for k in range(3)]
        self.to_peer = [
            send(kept.at[1], arrived.at[3], sems, 3, across),
            send(kept.at[0], arrived.at[4], sems, 4, across),
        ]
        self.to_end = send(kept.at[2], arrived.at[0], sems, 5, outwards)

    def turn(self, number, part, total):
        kept, arrived = self.kept, self.arrived
        low = lambda values: values.astype(low_type)
        wide = lambda ref, k: ref[k].astype(f32)
        if number < 3:

            @pl.when(self.is_end)
            def _():
                kept[number] = low(part)
                self.from_end[number].start()

        if number == 0:

            @pl.when(self.is_inner)
            def _():
                kept[0] = low(part)

        elif number == 1:

            @pl.when(self.is_inner)
            def _():
                self.from_end[0].wait_recv()
                kept[1] = low(part + wide(arrived, 0))
                self.to_peer[0].start()

        elif number == 2:

            @pl.when(self.is_inner)
            def _():
                self.from_end[1].wait_recv()
                kept[0] = low(wide(kept, 0) + wide(arrived, 1))
                self.to_peer[1].start()
                self.to_peer[0].wait_recv()
                kept[2] = low(part + wide(arrived, 3))
                self.to_end.start()

        else:

            @pl.when(self.is_end)
            def _():
                self.to_end.wait_recv()
                total[...] = part + wide(arrived, 0)
                for copy in self.from_end:
                    copy.wait_send()

            @pl.when(self.is_inner)
            def _():
                self.from_end[2].wait_recv()
                self.to_peer[1].wait_recv()
                total[...] = part + wide(arrived, 2) + wide(arrived, 4)
                for copy in self.to_peer:
                    copy.wait_send()
                self.to_end.wait_send()


def backward_kernel(
    queries,
    extra,
    row_columns,
    context_grad,
    queries_t,
    context_grad_t,
    keys,
    values_t,
    keys_extra,
    *refs,
):
    turn, pair = pl.program_id(0), pl.program_id(1)
    remote = len(refs) > 4
    if remote:
        weights, terms, refs = refs[0], refs[1:4], refs[4:]
        total, kept_rest, scratch = refs[4], refs[5:10], refs[10:]
        parts, kept, arrived, relay_sems = scratch[:4]
        at = Place()
        relay = Relay(at, kept, arrived, relay_sems)
        scatters = [
            take_plane(at, plan, terms[plan[0]], kept_rest[k], scratch[4 + 6 * k : 10 + 6 * k])
            for k, plan in enumerate(BACK_PLANS)
        ]
        now = turn * PAIRS + pair
        for when, doing in BACK_TIMES:

            @pl.when(now == when)
            def _(doing=doing):
                if doing is None:
                    at.greet()
                else:
                    for which in doing[0]:
                        scatters[which].step(doing[1])

    query_grad, key_grad_t, value_grad_t, folded = refs[:4]
    count = queries.shape[0]
    lane = lax.broadcasted_iota(jnp.int32, (count, PAIR), 1)
    query_pair, grad_pair = queries[...], context_grad[...]
    zeros = jnp.zeros_like(query_pair)
    lanes = pl.ds(pl.multiple_of(PAIR * pair, PAIR), PAIR)
    columns = pltpu.roll(row_columns[...], (128 - 2 * pair) % 128, 1)

    @pl.when(turn == 0)
    def _():
        query_grad[:, lanes] = jnp.zeros((count, PAIR), f32)

    query_grads = []
    for head in range(2):
        mine = (lane < HEAD) if head == 0 else (lane >= HEAD)
        rows = pl.ds(HEAD * head, HEAD)
        query_side = jnp.concatenate([jnp.where(mine, query_pair, zeros), extra[...]], axis=1)
        key_side = jnp.concatenate(
            [keys[...], keys_extra[:, 128 * head : 128 * head + 128]], axis=1
        )
        attention = jnp.exp(dot(query_side, key_side, 1, 1) - columns[:, head : head + 1])
        score_grad = attention * (
            dot(jnp.where(mine, grad_pair, zeros), values_t[0], 1, 0)
            - columns[:, HEADS + head : HEADS + head + 1]
        )
        attention_low = attention.astype(low_type)
        score_low = score_grad.astype(low_type)
        sums = [
            jnp.sum(score_grad[BLK * block : BLK * block + BLK], axis=0, keepdims=True)
            for block in range(count // BLK)
        ]
        spare = folded.shape[1] - len(sums)
        folded[head] = jnp.concatenate(sums + [jnp.zeros((spare, count), f32)] * (spare > 0), axis=0)
        query_grads.append(dot(score_low, keys[...], 1, 0))
        value_grad_t[rows, :] = dot(context_grad_t[rows, :], attention_low, 1, 0).astype(low_type)
        key_grad_t[rows, :] = dot(queries_t[rows, :], score_low, 1, 0).astype(low_type)
    query_grad[:, lanes] += jnp.where(lane < HEAD, query_grads[0], query_grads[1])

    if remote:
        parts[pl.ds(pl.multiple_of(PAIR * pair, PAIR), PAIR), :] = key_grad_t[...]
        parts[pl.ds(pl.multiple_of(D + PAIR * pair, PAIR), PAIR), :] = value_grad_t[...]
        for number in range(4):

            @pl.when(now == number * PAIRS + PAIRS - 1)
            def _(number=number):
                relay.turn(number, dot(weights[...], parts[...], 1, 0), total)


def attend_back(
    queries,
    extra,
    row_columns,
    context_grad,
    queries_t,
    context_grad_t,
    keys,
    values_t,
    keys_extra,
    weights,
    terms,
):
    count, row_length = queries.shape[0], keys.shape[0]
    fold_rows = -(-(count // BLK) // 8) * 8
    terms = [by_chip(term) for term in terms]
    anywhere = pl.BlockSpec(memory_space=pl.ANY)
    of_pair = pl.BlockSpec((count, PAIR), lambda turn, pair: (0, pair))
    of_pair_t = pl.BlockSpec((PAIR, count), lambda turn, pair: (pair, 0))
    key_t = pl.BlockSpec((PAIR, count), lambda turn, pair: (pair, turn))
    still = lambda *shape: pl.BlockSpec(shape, lambda turn, pair: (0,) * len(shape))
    remote, more_specs, more_shapes, more_out, scratch, more = {}, [], [], [], [], []
    if terms:
        remote = {"collective_id": 1, "has_side_effects": True}
        more = [weights, *terms]
        more_specs = [still(D, 2 * D)] + [anywhere] * 3
        more_shapes = [jax.ShapeDtypeStruct((D, count), f32)] + [
            jax.ShapeDtypeStruct((4, terms[which].shape[3], width // 2), low_type)
            for which, _, width, _ in BACK_PLANS
        ]
        more_out = [still(D, count)] + [anywhere] * len(BACK_PLANS)
        scratch = [
            pltpu.VMEM((2 * D, count), low_type),
            pltpu.VMEM((3, D, count), low_type),
            pltpu.VMEM((5, D, count), low_type),
            pltpu.SemaphoreType.DMA((2, 6)),
        ]
        for which, _, width, _ in BACK_PLANS:
            scratch += plane_scratch(terms[which].shape[3], width)
    return pl.pallas_call(
        backward_kernel,
        grid=(row_length // count, PAIRS),
        out_shape=[
            jax.ShapeDtypeStruct((count, D), f32),
            jax.ShapeDtypeStruct((D, row_length), low_type),
            jax.ShapeDtypeStruct((D, row_length), low_type),
            jax.ShapeDtypeStruct((HEADS, fold_rows, row_length), f32),
        ]
        + more_shapes,
        in_specs=[
            of_pair,
            still(count, 128),
            still(count, 128),
            of_pair,
            of_pair_t,
            of_pair_t,
            pl.BlockSpec((count, PAIR), lambda turn, pair: (turn, pair)),
            pl.BlockSpec((1, PAIR, count), lambda turn, pair: (turn, pair, 0)),
            pl.BlockSpec((count, 256), lambda turn, pair: (turn, pair)),
        ]
        + more_specs,
        out_specs=[
            still(count, D),
            key_t,
            key_t,
            pl.BlockSpec((2, fold_rows, count), lambda turn, pair: (pair, 0, turn)),
        ]
        + more_out,
        scratch_shapes=scratch,
        compiler_params=pltpu.CompilerParams(vmem_limit_bytes=back_vmem, **remote),
        cost_estimate=pl.CostEstimate(
            flops=10 * HEADS * count * row_length * 200,
            bytes_accessed=HEADS * row_length * 2048,
            transcendentals=HEADS * count * row_length,
        ),
        name="attention_backward",
    )(
        queries,
        extra,
        row_columns,
        context_grad,
        queries_t,
        context_grad_t,
        keys,
        values_t,
        keys_extra,
        *more,
    )


def body(
    hidden_states,
    output_cotangent,
    document_lengths,
    bucket_index,
    norm_gains,
    bias_table,
    project_weight,
    output_weight,
    expand_weight,
    reduce_weight,
    project_rows,
    project_columns,
    output_rows,
    output_columns,
    expand_rows,
    expand_columns,
    reduce_rows,
    reduce_columns,
    gains_moment,
    table_moment,
):
    every = ("seq", "dp")
    local_rows = hidden_states.shape[1]
    row_length = local_rows * lax.axis_size("seq")
    gradient_scale = 1.0 / math.sqrt(row_length * lax.axis_size("dp"))
    place = lax.axis_index("seq")
    blocks = local_rows // BLK

    shards = (project_weight, output_weight, expand_weight, reduce_weight)
    direct = (
        lax.axis_size("seq") == 4
        and lax.axis_size("dp") == 8
        and all(shard.shape[0] % 8 == 0 and shard.shape[1] % 256 == 0 for shard in shards)
    )
    inputs = hidden_states[0].astype(f32)
    if direct:
        opened = open_layer(
            shards, hidden_states[0], norm_gains, bucket_index[0], bias_table, document_lengths
        )
        project_full, output_full, expand_full, reduce_full = (
            whole.reshape(-1, whole.shape[4]) for whole in opened[:4]
        )
        normed_all, keys = (blocks_of.reshape(row_length, D) for blocks_of in opened[4:6])
        values_t, keys_extra, picks, queries, queries_t, context_t, log_total, extra = opened[6:]
        normed_low = normed_all[row_length - local_rows :]
    else:
        project_full, output_full, expand_full, reduce_full = (
            lax.all_gather(shard.astype(low_type), every, axis=0, tiled=True) for shard in shards
        )
        row_states = lax.all_gather(hidden_states[0], "seq", axis=0, tiled=True)
        normed_low = rms_norm(inputs, norm_gains[0]).astype(low_type)
        normed_all = rms_norm(row_states.astype(f32), norm_gains[0]).astype(low_type)
        doc_all = documents(document_lengths[0], row_length)
        doc_query = lax.dynamic_slice_in_dim(doc_all, place * local_rows, local_rows)
        picks = key_picks(bucket_index[0], doc_all, bias_table.shape[0])
        one_hot = picks[:, : blocks * bias_table.shape[0]]
        keys_extra = key_extra(picks, bias_table, blocks)
        extra = query_extra(doc_query, blocks)
        scaled = lambda values: (values.astype(low_type).astype(f32) * score_scale).astype(low_type)
        queries = scaled(dot(normed_low, project_full[:, :D], 1, 0))
        queries_t = scaled(dot(project_full[:, :D], normed_low, 0, 1))
        keys = dot(normed_all, project_full[:, D : 2 * D], 1, 0).astype(low_type)
        values_t = dot(project_full[:, 2 * D :], normed_all, 0, 1).astype(low_type)
        context_t, log_total = attend(queries, extra, keys, values_t, keys_extra)
        log_total = log_total.reshape(HEADS, 8, local_rows)[:, 0]
        values_t = jnp.transpose(values_t.reshape(D, -1, local_rows), (1, 0, 2))
    _, pullback_one = jax.vjp(rms_norm, inputs, norm_gains[0])
    query_weight, key_weight, value_weight = (
        project_full[:, :D],
        project_full[:, D : 2 * D],
        project_full[:, 2 * D :],
    )
    (
        layer_output,
        residual_grad,
        output_term,
        expand_term,
        reduce_term,
        context_grad,
        context_grad_t,
        row_columns,
        gain_two_grad,
    ) = middle(
        context_t,
        log_total,
        hidden_states[0],
        output_cotangent[0],
        norm_gains,
        output_full,
        expand_full,
        reduce_full,
    )
    layer_output = layer_output[None]
    query_grad, key_grad_t, value_grad_t, folded, *summed_back = attend_back(
        queries,
        extra,
        row_columns,
        context_grad,
        queries_t,
        context_grad_t,
        keys,
        values_t,
        keys_extra,
        project_full[:, D:],
        [output_term, expand_term, reduce_term] if direct else [],
    )
    if direct:
        rows_before = [project_rows, output_rows, expand_rows, reduce_rows]
        input_gradient, *results = close(
            gradient_scale,
            (
                normed_all.reshape(4, local_rows, D),
                key_grad_t,
                value_grad_t,
                query_grad,
                project_full,
                summed_back[0],
            ),
            (
                hidden_states[0],
                residual_grad,
                folded,
                picks,
                norm_gains,
                gain_two_grad,
                project_weight,
            ),
            summed_back[1:],
            rows_before,
            [shard.shape for shard in shards],
        )
        results = apply_updates(
            gradient_scale,
            results[:4],
            results[4:6],
            shards,
            rows_before,
            [project_columns, output_columns, expand_columns, reduce_columns],
            (norm_gains, gains_moment, bias_table, table_moment),
        )
        gradients, updated_weights, row_after, columns_after = (
            results[:4],
            results[4:8],
            results[8:12],
            results[12:16],
        )
        gains_gradient, gains_updated, gains_moment_new = results[16:19]
        table_gradient, table_updated, table_moment_new = results[19:]
        return (
            layer_output,
            input_gradient[None],
            gains_gradient,
            table_gradient,
            *gradients,
            gains_updated,
            table_updated,
            *updated_weights,
            row_after[0],
            columns_after[0],
            row_after[1],
            columns_after[1],
            row_after[2],
            columns_after[2],
            row_after[3],
            columns_after[3],
            gains_moment_new,
            table_moment_new,
        )

    buckets = bias_table.shape[0]
    picked = jnp.dot(
        folded[:, :blocks].reshape(HEADS * blocks, row_length),
        one_hot.astype(f32),
        precision=lax.Precision.HIGHEST,
    )
    table_grad = jnp.einsum("hkkb->bh", picked.reshape(HEADS, blocks, blocks, buckets))

    query_grad_low = (query_grad * score_scale).astype(low_type)
    project_terms = [
        dot(normed_low, query_grad_low, 0, 0),
        dot(normed_all, key_grad_t, 0, 1),
        dot(normed_all, value_grad_t, 0, 1),
    ]
    key_part = dot(key_grad_t, key_weight, 0, 1) + dot(value_grad_t, value_weight, 0, 1)
    key_part = lax.psum_scatter(
        key_part.astype(low_type), "seq", scatter_dimension=0, tiled=True
    ).astype(f32)
    input_part, gain_one_grad = pullback_one(dot(query_grad_low, query_weight, 1, 1) + key_part)
    input_gradient = (residual_grad + input_part).astype(low_type)[None]
    terms = [
        term.astype(low_type)
        for term in (jnp.concatenate(project_terms, axis=1), output_term, expand_term, reduce_term)
    ]
    shares = [
        lax.psum_scatter(term, every, scatter_dimension=0, tiled=True).astype(f32)
        for term in terms
    ]
    gradients = tuple((share * gradient_scale for share in shares))
    row_before = (project_rows, output_rows, expand_rows, reduce_rows)
    row_after = []
    column_parts = []
    row_sums = []
    for gradient, previous in zip(gradients, row_before):
        squares = gradient * gradient + tiny_term
        updated_rows = decay_rate * previous + (1.0 - decay_rate) * jnp.mean(squares, axis=1)
        row_after.append(updated_rows)
        column_parts.append(jnp.sum(squares, axis=0))
        row_sums.append(jnp.sum(updated_rows))
    summed = lax.psum(
        (
            column_parts[0],
            column_parts[1],
            column_parts[2],
            column_parts[3],
            jnp.stack(row_sums),
            jnp.stack([gain_one_grad, gain_two_grad[0]]),
            table_grad,
        ),
        every,
    )
    column_before = (project_columns, output_columns, expand_columns, reduce_columns)
    weights_before = (project_weight, output_weight, expand_weight, reduce_weight)
    full_rows = (
        project_full.shape[0],
        output_full.shape[0],
        expand_full.shape[0],
        reduce_full.shape[0],
    )
    updated_weights = []
    columns_after = []
    for position in range(4):
        columns_new = decay_rate * column_before[position] + (1.0 - decay_rate) * (
            summed[position] / full_rows[position]
        )
        row_mean = summed[4][position] / full_rows[position]
        denominator = row_after[position][:, None] * columns_new[None, :] / row_mean
        updated_weights.append(
            weights_before[position] - learn_rate * gradients[position] * lax.rsqrt(denominator)
        )
        columns_after.append(columns_new)
    gains_gradient = summed[5] * gradient_scale
    table_gradient = summed[6] * gradient_scale
    gains_moment_new = decay_rate * gains_moment + (1.0 - decay_rate) * (
        gains_gradient * gains_gradient + tiny_term
    )
    gains_updated = norm_gains - learn_rate * gains_gradient * lax.rsqrt(gains_moment_new)
    table_moment_new = decay_rate * table_moment + (1.0 - decay_rate) * (
        table_gradient * table_gradient + tiny_term
    )
    table_updated = bias_table - learn_rate * table_gradient * lax.rsqrt(table_moment_new)
    return (
        layer_output,
        input_gradient,
        gains_gradient,
        table_gradient,
        gradients[0],
        gradients[1],
        gradients[2],
        gradients[3],
        gains_updated,
        table_updated,
        updated_weights[0],
        updated_weights[1],
        updated_weights[2],
        updated_weights[3],
        row_after[0],
        columns_after[0],
        row_after[1],
        columns_after[1],
        row_after[2],
        columns_after[2],
        row_after[3],
        columns_after[3],
        gains_moment_new,
        table_moment_new,
    )


def solution(mesh):
    placed = (
        P("dp", "seq", None),
        P("dp", "seq", None),
        P("dp", None),
        P("dp", "seq", None),
        P(),
        P(),
        P(("seq", "dp"), None),
        P(("seq", "dp"), None),
        P(("seq", "dp"), None),
        P(("seq", "dp"), None),
        P(("seq", "dp")),
        P(),
        P(("seq", "dp")),
        P(),
        P(("seq", "dp")),
        P(),
        P(("seq", "dp")),
        P(),
        P(),
        P(),
    )
    return jax.shard_map(
        body,
        mesh=mesh,
        in_specs=placed,
        out_specs=(
            P("dp", "seq", None),
            P("dp", "seq", None),
            P(),
            P(),
            P(("seq", "dp"), None),
            P(("seq", "dp"), None),
            P(("seq", "dp"), None),
            P(("seq", "dp"), None),
            P(),
            P(),
            P(("seq", "dp"), None),
            P(("seq", "dp"), None),
            P(("seq", "dp"), None),
            P(("seq", "dp"), None),
            P(("seq", "dp")),
            P(),
            P(("seq", "dp")),
            P(),
            P(("seq", "dp")),
            P(),
            P(("seq", "dp")),
            P(),
            P(),
            P(),
        ),
        check_vma=False,
    )
```

```python
import functools
import math

import jax
import jax.numpy as jnp
from jax import lax
from jax.experimental import pallas as pl
from jax.experimental.pallas import tpu as pltpu
from jax.sharding import PartitionSpec as P

D = 768
HEADS = 12
HEAD = 64
BLK = 128
PAIR = 2 * HEAD
PAIRS = HEADS // 2
DOCS = 5
TERMS = 3

score_scale = 0.125
masked_score = -1e30
norm_epsilon = 1e-06
tiny_term = 1e-30
learn_rate = 0.3
decay_rate = 1.0 - 2.0 ** (-0.8)
vmem_bytes = 56 * 2**20
open_vmem = 48 * 2**20
back_vmem = 48 * 2**20
close_vmem = 48 * 2**20
apply_vmem = 16 * 2**20
middle_vmem = 52 * 2**20

low_type = jnp.bfloat16
f32 = jnp.float32


def dot(former, latter, former_axis, latter_axis):
    return lax.dot_general(
        former,
        latter,
        (((former_axis,), (latter_axis,)), ((), ())),
        preferred_element_type=f32,
    )


def in_hbm(*arrays):
    return [pltpu.with_memory_space_constraint(array, pltpu.HBM) for array in arrays]


def rms_norm(values, gain_vector):
    return (
        values
        * lax.rsqrt(jnp.mean(values * values, axis=-1, keepdims=True) + norm_epsilon)
        * gain_vector
    )


def documents(lengths, row_length):
    doc_ends = jnp.cumsum(lengths)
    position = jnp.arange(row_length, dtype=jnp.int32)
    return jnp.sum((position[:, None] >= doc_ends[None, :]).astype(jnp.int32), axis=1)


def split_terms(values):
    terms = []
    rest = values
    for _ in range(TERMS):
        term = lax.reduce_precision(rest, 8, 7)
        terms.append(term)
        rest = rest - term
    return terms


def extra_columns(blocks):
    return TERMS * blocks, TERMS * blocks + DOCS


def query_extra(doc_query, blocks):
    count = doc_query.shape[0]
    doc_start, one_start = extra_columns(blocks)
    lane = lax.broadcasted_iota(jnp.int32, (count, 128), 1)
    block = lax.broadcasted_iota(jnp.int32, (count, 128), 0) // BLK
    is_block = (lane < doc_start) & (lane % blocks == block)
    is_doc = (lane >= doc_start) & (lane < one_start) & (lane - doc_start == doc_query[:, None])
    return (is_block | is_doc).astype(low_type)


def key_picks(bucket_rows, doc_all, buckets):
    blocks, row_length = bucket_rows.shape
    one_hot = (
        bucket_rows.T[:, :, None] == jnp.arange(buckets, dtype=jnp.int32)[None, None, :]
    ).reshape(row_length, blocks * buckets)
    other_doc = doc_all[:, None] != jnp.arange(DOCS, dtype=jnp.int32)[None, :]
    ones = jnp.ones((row_length, 1), jnp.bool_)
    return jnp.concatenate([one_hot, other_doc, ones], axis=1).astype(low_type)


def key_extra(picks, bias_table, blocks):
    buckets = bias_table.shape[0]
    doc_start, one_start = extra_columns(blocks)
    terms = jnp.stack(split_terms(bias_table), axis=0)
    lane = jnp.arange(128, dtype=jnp.int32)
    place = jnp.clip(lane // blocks, 0, TERMS - 1)
    spread = jnp.transpose(terms[place], (1, 2, 0))
    at_block = (lane[None, :] % blocks == jnp.arange(blocks, dtype=jnp.int32)[:, None]) & (
        lane[None, :] < doc_start
    )
    bias_part = jnp.where(at_block[:, None, None, :], spread[None], 0.0).reshape(
        blocks * buckets, HEADS, 128
    )
    doc_part = jnp.where(
        lane[None, :] - doc_start == jnp.arange(DOCS, dtype=jnp.int32)[:, None], masked_score, 0.0
    )
    one_part = ((lane >= one_start) & (lane < one_start + TERMS)).astype(f32)[None]
    rest = jnp.concatenate([doc_part, one_part], axis=0)
    rest = jnp.broadcast_to(rest[:, None, :], (DOCS + 1, HEADS, 128))
    whole = jnp.concatenate([bias_part, rest], axis=0).reshape(-1, HEADS * 128).astype(low_type)
    return dot(picks, whole, 1, 0).astype(low_type)


def forward_kernel(queries, extra, keys, values_t, keys_extra, context_t, log_total):
    count = queries.shape[0]
    lane = lax.broadcasted_iota(jnp.int32, (count, PAIR), 1)
    query_pair = queries[...]
    for head in range(2):
        mine = (lane < HEAD) if head == 0 else (lane >= HEAD)
        query_side = jnp.concatenate(
            [jnp.where(mine, query_pair, jnp.zeros_like(query_pair)), extra[...]], axis=1
        )
        key_side = jnp.concatenate([keys[...], keys_extra[:, 128 * head : 128 * head + 128]], axis=1)
        scores = dot(key_side, query_side, 1, 1)
        top = jnp.max(scores, axis=0, keepdims=True)
        unscaled = jnp.exp(scores - top).astype(low_type)
        value_side = jnp.concatenate(
            [
                values_t[HEAD * head : HEAD * head + HEAD, :],
                jnp.ones((16, unscaled.shape[0]), low_type),
            ],
            axis=0,
        )
        weighted = dot(value_side, unscaled, 1, 0)
        total = weighted[HEAD : HEAD + 1]
        context_t[pl.ds(HEAD * head, HEAD), :] = weighted[:HEAD] / total
        log_total[pl.ds(8 * head, 8), :] = jnp.broadcast_to(top + jnp.log(total), (8, count))


def attend(queries, extra, keys, values_t, keys_extra):
    count, row_length = queries.shape[0], keys.shape[0]
    return pl.pallas_call(
        forward_kernel,
        grid=(PAIRS,),
        out_shape=[
            jax.ShapeDtypeStruct((D, count), f32),
            jax.ShapeDtypeStruct((HEADS * 8, count), f32),
        ],
        in_specs=[
            pl.BlockSpec((count, PAIR), lambda pair: (0, pair)),
            pl.BlockSpec((count, 128), lambda pair: (0, 0)),
            pl.BlockSpec((row_length, PAIR), lambda pair: (0, pair)),
            pl.BlockSpec((PAIR, row_length), lambda pair: (pair, 0)),
            pl.BlockSpec((row_length, 256), lambda pair: (0, pair)),
        ],
        out_specs=[
            pl.BlockSpec((PAIR, count), lambda pair: (pair, 0)),
            pl.BlockSpec((16, count), lambda pair: (pair, 0)),
        ],
        compiler_params=pltpu.CompilerParams(vmem_limit_bytes=vmem_bytes),
        cost_estimate=pl.CostEstimate(
            flops=4 * HEADS * count * row_length * 256,
            bytes_accessed=HEADS * row_length * 1024,
            transcendentals=HEADS * count * row_length,
        ),
        name="attention_forward",
    )(queries, extra, keys, values_t, keys_extra)


MESH = pl.DeviceIdType.MESH


class Place:
    def __init__(self):
        self.seq, self.dp = lax.axis_index("seq"), lax.axis_index("dp")
        self.core, self.x, self.y = self.dp % 2, self.dp // 2 % 2, self.dp // 4
        self.by_core = (self.seq, self.dp + 1 - 2 * self.core)
        self.by_x = (self.seq, self.dp + 2 - 4 * self.x)
        self.by_y = (self.seq, self.dp + 4 - 8 * self.y)
        self.plane = [(self.seq, (self.dp + step) % 8) for step in range(1, 8)]
        self.others = [((self.seq + step) % 4, self.dp) for step in (1, 2, 3)]

    def turn(self, block):
        flip = 3 - self.seq
        return 2 * ((block // 2 + flip // 2) % 2) + (block + flip) % 2

    def greet(self, whole_plane=False):
        barrier = pltpu.get_barrier_semaphore()
        beside = self.plane if whole_plane else [self.by_core, self.by_x, self.by_y]
        partners = beside + self.others
        for partner in partners:
            pl.semaphore_signal(barrier, inc=1, device_id=partner, device_id_type=MESH)
        pl.semaphore_wait(barrier, len(partners))


def send(source, target, sems, index, partner):
    return pltpu.make_async_remote_copy(
        src_ref=source,
        dst_ref=target,
        send_sem=sems.at[0, index],
        recv_sem=sems.at[1, index],
        device_id=partner,
        device_id_type=MESH,
    )


def half_of(start, width, which):
    return pl.ds(pl.multiple_of(start + which * (width // 2), 128), width // 2)


class Gather:
    steps = 6

    def __init__(self, at, plan, shard, whole, pair, low, sems, local_sems):
        _, start, width, x_first = plan
        self.at, self.shard, self.pair, self.low, self.whole = at, shard, pair, low, whole
        rows = shard.shape[0]
        mine, other = half_of(start, width, at.core), half_of(start, width, 1 - at.core)
        own_rows = pl.ds(pl.multiple_of(rows * at.core, 8), rows)
        place = whole.at[at.seq, at.y, at.x, :, mine]
        along_x, along_y = (whole.at[:, at.y, at.x, :, mine], whole.at[:, at.y, :, :, mine])
        if not x_first:
            along_x, along_y = (whole.at[:, :, at.x, :, mine], along_x)
        self.local = [
            pltpu.make_async_copy(shard.at[:, mine], pair.at[own_rows], local_sems.at[0]),
            pltpu.make_async_copy(low, place, local_sems.at[1]),
        ]
        self.first = send(shard.at[:, other], pair.at[own_rows], sems, 0, at.by_core)
        self.over_z = [send(low, place, sems, 1 + k, at.others[k]) for k in range(3)]
        self.over_x = send(along_x, along_x, sems, 4, at.by_x)
        self.over_y = send(along_y, along_y, sems, 5, at.by_y)
        self.order = [self.over_x, self.over_y] if x_first else [self.over_y, self.over_x]
        self.last = send(whole.at[:, :, :, :, mine], whole.at[:, :, :, :, mine], sems, 6, at.by_core)

    def step(self, number):
        if number == 0:
            self.local[0].start()
            self.first.start()
        elif number == 1:
            self.local[0].wait()
            self.first.wait()
            self.low[...] = self.pair[...].astype(low_type)
            self.local[1].start()
            for copy in self.over_z:
                copy.start()
        elif number == 2:
            self.local[1].wait()
            for copy in self.over_z:
                copy.wait()
            self.order[0].start()
        elif number == 3:
            self.order[0].wait()
            self.order[1].start()
        elif number == 4:
            self.order[1].wait()
            self.last.start()
        else:
            self.last.wait()


class ScatterPlane:
    steps = 5

    def __init__(self, at, plan, term, kept, held, arrived, sems, local_sems):
        _, start, width, self.x_first = plan
        self.at, self.held, self.arrived = at, held, arrived
        mine, other = half_of(start, width, at.core), half_of(start, width, 1 - at.core)
        self.local = [
            pltpu.make_async_copy(term.at[:, :, :, :, mine], held, local_sems.at[0]),
            pltpu.make_async_copy(held.at[:, at.y, at.x], kept, local_sems.at[1]),
        ]
        self.first = send(term.at[:, :, :, :, other], arrived[0], sems, 0, at.by_core)
        if self.x_first:
            self.second = send(held.at[:, :, 1 - at.x], arrived[1], sems, 1, at.by_x)
            self.third = send(held.at[:, 1 - at.y, at.x], arrived[2], sems, 2, at.by_y)
        else:
            self.second = send(held.at[:, 1 - at.y], arrived[1], sems, 1, at.by_y)
            self.third = send(held.at[:, at.y, 1 - at.x], arrived[2], sems, 2, at.by_x)

    def add(self, place, values):
        self.held[place] = self.held[place] + values

    def step(self, number):
        at = self.at
        if number == 0:
            self.local[0].start()
            self.first.start()
        elif number == 1:
            self.local[0].wait()
            self.first.wait()

            @pl.loop(0, 4)
            def _(row):
                for across in range(4):
                    place = (row, across // 2, across % 2)
                    self.add(place, self.arrived[0][place])

            self.second.start()
        elif number == 2:
            self.second.wait()

            @pl.loop(0, 4)
            def _(row):
                for across in range(2):
                    place = (row, across, at.x) if self.x_first else (row, at.y, across)
                    self.add(place, self.arrived[1][row, across])

            self.third.start()
        elif number == 3:
            self.third.wait()

            @pl.loop(0, 4)
            def _(row):
                self.add((row, at.y, at.x), self.arrived[2][row])

            self.local[1].start()
        else:
            self.local[1].wait()


class ScatterLine:
    def __init__(self, at, share_start, kept, share, own, arrived, total, sems, local_sems):
        self.at, self.own, self.arrived, self.total = at, own, arrived, total
        rows, half = total.shape[0] // 2, total.shape[1]
        of_core = lambda which: pl.ds(pl.multiple_of(rows * which, 8), rows)
        mine = half_of(share_start, 2 * half, at.core)
        self.local = [
            pltpu.make_async_copy(kept.at[at.seq], own, local_sems.at[0]),
            pltpu.make_async_copy(
                total.at[of_core(at.core)], share.at[:, mine], local_sems.at[1]
            ),
        ]
        self.over_z = [
            send(kept.at[at.others[k][0]], arrived.at[k], sems, k, at.others[k]) for k in range(3)
        ]
        self.last = send(total.at[of_core(1 - at.core)], share.at[:, mine], sems, 3, at.by_core)

    def step(self, number):
        if number == 0:
            self.local[0].start()
            for copy in self.over_z:
                copy.start()
        elif number == 1:
            self.local[0].wait()
            for copy in self.over_z:
                copy.wait()
            total = self.own[...].astype(f32)
            for k in range(3):
                total = total + self.arrived[k].astype(f32)
            self.total[...] = total
            self.local[1].start()
            self.last.start()
        else:
            self.local[1].wait()
            self.last.wait()


FIRST_ROWS = 256


class Ring:
    def __init__(self, at, own, blocks, sems, local_sem):
        self.at = at
        seq = at.seq
        self.local = pltpu.make_async_copy(own, blocks.at[seq], local_sem)
        right, left = ((seq + 1) % 4, at.dp), ((seq + 3) % 4, at.dp)
        half = own.shape[0] // 2
        self.hops = []
        for number, (hop, rows) in enumerate(
            (
                (0, pl.ds(0, FIRST_ROWS)),
                (0, pl.ds(FIRST_ROWS, 2 * half - FIRST_ROWS)),
                (1, pl.ds(0, 2 * half)),
                (2, pl.ds(0, half)),
                (2, pl.ds(half, half)),
            )
        ):
            back, ahead = blocks.at[(seq + 4 - hop) % 4, rows], blocks.at[(seq + hop) % 4, rows]
            self.hops.append(
                [
                    (
                        (seq >= hop) & (seq < 3),
                        send(own.at[rows] if hop == 0 else back, back, sems, number, right),
                        seq >= hop + 1,
                    ),
                    (
                        (seq + hop <= 3) & (seq > 0),
                        send(own.at[rows] if hop == 0 else ahead, ahead, sems, 5 + number, left),
                        seq + hop + 1 <= 3,
                    ),
                ]
            )

    def start(self, hop):
        if hop == 0:
            self.local.start()
        for sends, copy, _ in self.hops[hop]:
            pl.when(sends)(copy.start)

    def arrive(self, hop):
        for _, copy, receives in self.hops[hop]:
            pl.when(receives)(copy.wait_recv)

    def finish(self):
        for hop in self.hops:
            for sends, copy, _ in hop:
                pl.when(sends)(copy.wait_send)


GATHERS = (
    (0, 0, 1280, True),
    (0, 1280, 1024, False),
    (1, 0, D, False),
    (2, 0, 512, True),
    (2, 512, 2560, False),
    (3, 0, D, True),
)


def opening_kernel(*refs):
    shards, own = refs[:4], refs[4]
    small, lengths = refs[5:8], refs[8]
    wholes, outs = refs[9:13], refs[13:18]
    normed_out, keys_out, values_out, keys_extra_out, picks_out = outs
    queries, queries_t, context_t, log_total, extra = refs[18:23]
    scratch = refs[23:]
    many = len(GATHERS)
    of_gathers, scratch = scratch[: 4 * many], scratch[4 * many :]
    ring_sems, ring_local, out_sems, blocks, project, normed, keys, values_t = scratch[:8]
    keys_extra, picks, sums, tops = scratch[8:12]
    gains, bucket_rows, bias_table, small_sems = scratch[12:]
    loads = [
        pltpu.make_async_copy(source, target, small_sems.at[k])
        for k, (source, target) in enumerate(zip(small, (gains, bucket_rows, bias_table)))
    ]
    for load in loads:
        load.start()
    at = Place()
    at.greet()
    gathers = [
        Gather(
            at,
            plan,
            shards[plan[0]],
            project if plan[0] == 0 else wholes[plan[0]],
            *of_gathers[4 * k : 4 * k + 4],
        )
        for k, plan in enumerate(GATHERS)
    ]
    ring = Ring(at, own, blocks, ring_sems, ring_local.at[0])

    def first_step(number):
        for gather in gathers[:2]:
            gather.step(number)

    def rest_step(number):
        for gather in gathers[2:]:
            gather.step(number)

    ring.start(0)
    first_step(0)
    rest_step(0)
    first_step(1)
    ring.start(1)
    for load in loads:
        load.wait()

    count, buckets = own.shape[0], bias_table.shape[1]
    row_length = keys_extra.shape[0]
    query_blocks = count // BLK
    doc_start, one_start = extra_columns(query_blocks)
    picked = query_blocks * buckets
    ends = []
    for doc in range(DOCS):
        ends.append(lengths[0, doc] + (ends[-1] if ends else 0))

    def documents_at(position):
        return sum((position >= end).astype(jnp.int32) for end in ends)

    bucket_at = lax.broadcasted_iota(jnp.int32, (buckets, row_length), 0)
    for block in range(query_blocks):
        picks[buckets * block : buckets * block + buckets, :] = (
            (bucket_rows[block] == bucket_at).astype(f32).astype(low_type)
        )
    last = picks.shape[0] - picked
    row = lax.broadcasted_iota(jnp.int32, (last, row_length), 0)
    key_doc = documents_at(lax.broadcasted_iota(jnp.int32, (last, row_length), 1))
    picks[picked:, :] = (
        jnp.where(row < DOCS, (key_doc != row).astype(f32), (row == DOCS).astype(f32))
    ).astype(low_type)

    same = lax.broadcasted_iota(jnp.int32, (buckets, buckets), 0) == lax.broadcasted_iota(
        jnp.int32, (buckets, buckets), 1
    )
    lane = lax.broadcasted_iota(jnp.int32, (picked, 128), 1)
    lane_block = lax.broadcasted_iota(jnp.int32, (picked, 128), 0) // buckets
    lane_last = lax.broadcasted_iota(jnp.int32, (last, 128), 1)
    row_last = lax.broadcasted_iota(jnp.int32, (last, 128), 0)
    below = jnp.where(
        (row_last < DOCS) & (lane_last - doc_start == row_last),
        masked_score,
        jnp.where(
            (row_last == DOCS) & (lane_last >= one_start) & (lane_last < one_start + TERMS), 1.0, 0.0
        ),
    ).astype(low_type)

    first_step(2)
    rest_step(1)

    def make_extra(pair):
        sides = []
        for head in range(2):
            of_head = jnp.broadcast_to(bias_table[pl.ds(2 * pair + head, 1), :], same.shape)
            of_head = jnp.sum(jnp.where(same, of_head, 0.0), axis=1, keepdims=True)
            rest_of = jnp.concatenate([of_head] * query_blocks, axis=0)
            side = jnp.zeros((picked, 128), f32)
            for term in range(TERMS):
                part = rest_of.astype(low_type).astype(f32)
                rest_of = rest_of - part
                side = jnp.where(lane == term * query_blocks + lane_block, part, side)
            sides.append(jnp.concatenate([side.astype(low_type), below], axis=0))
        keys_extra[:, pl.ds(pl.multiple_of(256 * pair, 256), 256)] = dot(
            picks[...], jnp.concatenate(sides, axis=1), 0, 0
        ).astype(low_type)

    pl.loop(0, PAIRS // 2)(make_extra)
    first_step(3)
    pl.loop(PAIRS // 2, PAIRS)(make_extra)
    first_step(4)
    extra_lane = lax.broadcasted_iota(jnp.int32, (count, 128), 1)
    extra_row = lax.broadcasted_iota(jnp.int32, (count, 128), 0)
    query_doc = documents_at(extra_row + at.seq * count)
    extra[...] = (
        (
            ((extra_lane < doc_start) & (extra_lane % query_blocks == extra_row // BLK))
            | ((extra_lane < one_start) & (extra_lane - doc_start == query_doc))
        )
        .astype(f32)
        .astype(low_type)
    )
    sums[...] = jnp.zeros_like(sums)
    tops[...] = jnp.full_like(tops, masked_score)
    ring.local.wait()
    first_step(5)

    copies = [pltpu.make_async_copy(project, wholes[0], out_sems.at[0])]
    for block in range(4):
        columns = pl.ds(count * block, count)
        into = pl.ds(pl.multiple_of(count * at.turn(block), count), count)
        copies += [
            pltpu.make_async_copy(
                keys_extra.at[columns], keys_extra_out.at[into], out_sems.at[1 + block]
            ),
            pltpu.make_async_copy(
                picks.at[:, columns], picks_out.at[:, into], out_sems.at[5 + block]
            ),
        ]
    for copy in copies:
        copy.start()
    weights = [project[:, :, :, :, D * part : D * part + D].reshape(D, D) for part in range(3)]
    pair_lane = lax.broadcasted_iota(jnp.int32, (count, PAIR), 1)

    def attend_pair(block, rows, pair):
        lanes = pl.ds(pl.multiple_of(pair * PAIR, PAIR), PAIR)
        start = block * count + rows.start
        key_rows = pl.ds(pl.multiple_of(start, rows.size), rows.size)
        query_pair, key_pair = queries[:, lanes], keys[block, rows, lanes]
        for head in range(2):
            which = 2 * pair + head
            mine = (pair_lane < HEAD) if head == 0 else (pair_lane >= HEAD)
            query_side = jnp.concatenate(
                [jnp.where(mine, query_pair, jnp.zeros_like(query_pair)), extra[...]], axis=1
            )
            more = keys_extra[key_rows, pl.ds(pl.multiple_of(128 * which, 128), 128)]
            scores = dot(jnp.concatenate([key_pair, more], axis=1), query_side, 1, 1)
            top_before = tops[which, 0:1]
            top = jnp.maximum(top_before, jnp.max(scores, axis=0, keepdims=True))
            unscaled = jnp.exp(scores - top).astype(low_type)
            value_side = jnp.concatenate(
                [
                    values_t[block, pl.ds(pl.multiple_of(HEAD * which, HEAD), HEAD), rows],
                    jnp.ones((16, rows.size), low_type),
                ],
                axis=0,
            )
            sums[which] = sums[which] * jnp.exp(top_before - top) + dot(value_side, unscaled, 1, 0)
            tops[which] = jnp.broadcast_to(top, (8, count))

    side = at.seq // 2
    order = [at.seq, 1 - at.seq + 4 * side, 2 - side, 3 - 3 * side]
    whole_block, halves = pl.ds(0, count), [pl.ds(0, count // 2), pl.ds(count // 2, count // 2)]
    passes = [(block, whole_block) for block in order[:3]] + [(order[3], rows) for rows in halves]
    events = {
        (0, 0): [lambda: (ring.arrive(0), ring.arrive(1), ring.start(2))],
        (0, 5): [lambda: rest_step(2)],
        (1, 4): [lambda: rest_step(3)],
        (1, 5): [lambda: (ring.arrive(2), ring.start(3), ring.start(4))],
        (2, 5): [lambda: ring.arrive(3)],
        (3, 3): [lambda: rest_step(4)],
        (3, 5): [lambda: ring.arrive(4)],
    }
    for number, (block, rows) in enumerate(passes):
        values = blocks[block, rows].astype(f32)
        normed_low = (
            values
            * lax.rsqrt(jnp.mean(values * values, axis=1, keepdims=True) + norm_epsilon)
            * gains[0:1, :]
        ).astype(low_type)
        normed[block, rows] = normed_low
        keys[block, rows] = dot(normed_low, weights[1], 1, 0).astype(low_type)
        values_t[block, :, rows] = dot(weights[2], normed_low, 0, 1).astype(low_type)
        turn = at.turn(block)
        for place, (source, target, index) in enumerate(
            (
                (normed, normed_out, (rows,)),
                (keys, keys_out, (rows,)),
                (values_t, values_out, (slice(None), rows)),
            )
        ):
            copy = pltpu.make_async_copy(
                source.at[(block, *index)],
                target.at[(turn, *index)],
                out_sems.at[9 + 3 * number + place],
            )
            copy.start()
            copies.append(copy)
        if number == 0:
            scaled = lambda values: (values.astype(low_type).astype(f32) * score_scale).astype(low_type)
            queries[...] = scaled(dot(normed_low, weights[0], 1, 0))
            queries_t[...] = scaled(dot(weights[0], normed_low, 0, 1))

        @pl.loop(0, PAIRS)
        def _(pair, number=number, block=block, rows=rows):
            for (when, which), actions in events.items():
                if when == number:

                    @pl.when(pair == which)
                    def _(actions=actions):
                        for action in actions:
                            action()

            attend_pair(block, rows, pair)

    for head in range(HEADS):
        total = sums[head, HEAD : HEAD + 1]
        context_t[HEAD * head : HEAD * head + HEAD, :] = sums[head, :HEAD] / total
        log_total[head : head + 1, :] = tops[head, 0:1] + jnp.log(total)
    rest_step(5)
    ring.finish()
    for copy in copies:
        copy.wait()


def open_layer(shards, own, gains, bucket_rows, bias_table, lengths):
    shards = [pltpu.with_memory_space_constraint(shard, pltpu.HBM) for shard in shards]
    own, gains, bucket_rows, bias_table, lengths = (
        pltpu.with_memory_space_constraint(array, pltpu.HBM)
        for array in (own, gains, jnp.transpose(bucket_rows, (1, 0, 2)), bias_table.T, lengths)
    )
    anywhere = pl.BlockSpec(memory_space=pl.ANY)
    in_place = pl.BlockSpec(memory_space=pltpu.VMEM)
    count, blocks = own.shape[0], bucket_rows.shape[0]
    row_length = 4 * count
    picked = blocks * bias_table.shape[1] + 16
    low = lambda *shape: pltpu.HBM(shape, low_type)
    whole_shapes = [(4, 2, 2, 2 * shard.shape[0], shard.shape[1]) for shard in shards]
    of_gathers = []
    for which, _, width, _ in GATHERS:
        half = (2 * shards[which].shape[0], width // 2)
        of_gathers += [
            pltpu.VMEM(half, f32),
            pltpu.VMEM(half, low_type),
            pltpu.SemaphoreType.DMA((2, 7)),
            pltpu.SemaphoreType.DMA((2,)),
        ]
    return pl.pallas_call(
        opening_kernel,
        out_shape=[low(*shape) for shape in whole_shapes]
        + [low(4, count, D)] * 2
        + [low(4, D, count), low(row_length, HEADS * 128), low(picked, row_length)]
        + [low(count, D), low(D, count)]
        + [jax.ShapeDtypeStruct((D, count), f32), jax.ShapeDtypeStruct((16, count), f32)]
        + [low(count, 128)],
        in_specs=[anywhere] * 8 + [pl.BlockSpec(memory_space=pltpu.SMEM)],
        out_specs=[anywhere] * 9 + [in_place] * 5,
        scratch_shapes=of_gathers
        + [
            pltpu.SemaphoreType.DMA((2, 10)),
            pltpu.SemaphoreType.DMA((1,)),
            pltpu.SemaphoreType.DMA((24,)),
            pltpu.VMEM((4, count, D), low_type),
            pltpu.VMEM(whole_shapes[0], low_type),
            pltpu.VMEM((4, count, D), low_type),
            pltpu.VMEM((4, count, D), low_type),
            pltpu.VMEM((4, D, count), low_type),
            pltpu.VMEM((row_length, HEADS * 128), low_type),
            pltpu.VMEM((picked, row_length), low_type),
            pltpu.VMEM((HEADS, HEAD + 16, count), f32),
            pltpu.VMEM((HEADS, 8, count), f32),
            pltpu.VMEM(gains.shape, f32),
            pltpu.VMEM(bucket_rows.shape, jnp.int32),
            pltpu.VMEM(bias_table.shape, f32),
            pltpu.SemaphoreType.DMA((3,)),
        ],
        compiler_params=pltpu.CompilerParams(
            collective_id=0, has_side_effects=True, vmem_limit_bytes=open_vmem
        ),
        name="open_layer",
    )(*shards, own, gains, bucket_rows, bias_table, lengths)


def plane_scratch(rows, width):
    half = width // 2
    return [
        pltpu.VMEM((4, 2, 2, rows, half), low_type),
        pltpu.VMEM((4, 2, 2, rows, half), low_type),
        pltpu.VMEM((4, 2, rows, half), low_type),
        pltpu.VMEM((4, rows, half), low_type),
        pltpu.SemaphoreType.DMA((2, 3)),
        pltpu.SemaphoreType.DMA((2,)),
    ]


def line_scratch(rows, width):
    half = width // 2
    return [
        pltpu.VMEM((rows, half), low_type),
        pltpu.VMEM((3, rows, half), low_type),
        pltpu.VMEM((rows, half), f32),
        pltpu.SemaphoreType.DMA((2, 4)),
        pltpu.SemaphoreType.DMA((2,)),
    ]


def take_plane(at, plan, term, kept, scratch):
    return ScatterPlane(at, plan, term, kept, scratch[0], scratch[1:4], scratch[4], scratch[5])


def by_chip(term):
    return term.reshape(4, 2, 2, term.shape[0] // 16, term.shape[1])


class AllSum:
    def __init__(self, at, own, plane, line, sems):
        self.at, self.own, self.plane, self.line = at, own, plane, line
        self.local = pltpu.make_async_copy(own, plane.at[at.dp], sems.at[0, 10])
        self.beside = [
            send(own, plane.at[at.dp], sems, k, partner) for k, partner in enumerate(at.plane)
        ]
        place = line.at[at.seq]
        self.over_z = [
            send(place, place, sems, 7 + k, partner) for k, partner in enumerate(at.others)
        ]

    def step(self, number):
        if number == 0:
            self.local.start()
            for copy in self.beside:
                copy.start()
        elif number == 1:
            self.local.wait()
            for copy in self.beside:
                copy.wait()
            total = self.plane[0]
            for k in range(1, 8):
                total = total + self.plane[k]
            self.line[self.at.seq] = total
            for copy in self.over_z:
                copy.start()
        else:
            for copy in self.over_z:
                copy.wait()

    def total(self):
        return (self.line[0] + self.line[1]) + (self.line[2] + self.line[3])


def sum_scratch(width):
    return [
        pltpu.VMEM((8, width), f32),
        pltpu.VMEM((8, 8, width), f32),
        pltpu.VMEM((4, 8, width), f32),
        pltpu.SemaphoreType.DMA((2, 11)),
    ]


EARLY_WIDTH, LATE_WIDTH = D + 512, D
CLOSE_PLANS = ((2, 0, D, True), (1, 0, D, False), (0, 0, D, True))


def split_low(values):
    terms = []
    for _ in range(TERMS):
        terms.append(values.astype(low_type))
        values = values - terms[-1].astype(f32)
    return terms


def close_kernel(scale, *refs):
    normed, key_grad_t, value_grad_t, query_grad, project, key_part_t = refs[:6]
    inputs, residual_grad, folded, picks, gains, gain_two, own_weight = refs[6:13]
    kept_rest, rows_before, refs = refs[13:18], refs[18:22], refs[22:]
    input_grad, shares, early_total, late_total = refs[0], refs[1:5], refs[5], refs[6]
    scratch = refs[7:]
    normed_in, key_in, value_in, weight_in, part_in, residual_in, load_sems = scratch[:7]
    early, late, scratch = scratch[7:11], scratch[11:15], scratch[15:]
    terms, kept, scratch = scratch[:3], scratch[3:6], scratch[6:]
    at = Place()
    loads = [
        pltpu.make_async_copy(source, target, load_sems.at[k])
        for k, (source, target) in enumerate(
            (
                (normed.at[3], normed_in.at[3]),
                (value_grad_t, value_in),
                (normed.at[pl.ds(0, 3)], normed_in.at[pl.ds(0, 3)]),
                (key_grad_t, key_in),
                (project.at[:, 0:D], weight_in),
                (key_part_t, part_in),
                (residual_grad, residual_in),
            )
        )
    ]
    for load in loads:
        load.start()
    at.greet(whole_plane=True)
    planes, lines = [], []
    for k, plan in enumerate(CLOSE_PLANS):
        planes.append(take_plane(at, plan, terms[k], kept[k], scratch[:6]))
        lines.append(ScatterLine(at, D * plan[0], kept[k], shares[0], *scratch[6:11]))
        scratch = scratch[11:]
    rest_lines = []
    for k, (which, start, _, _) in enumerate(BACK_PLANS):
        rest_lines.append(
            ScatterLine(at, start, kept_rest[k], shares[which + 1], *scratch[5 * k : 5 * k + 5])
        )
    first, second = AllSum(at, *early), AllSum(at, *late)

    for line in rest_lines:
        line.step(0)
    early_own, late_own = early[0], late[0]
    early_own[...] = jnp.zeros_like(early_own)
    late_own[...] = jnp.zeros_like(late_own)
    count = inputs.shape[0]
    query_low = (query_grad[...] * score_scale).astype(low_type)

    def put(term, values):
        term[...] = values.astype(low_type).reshape(term.shape)

    def of_row(parts):
        whole = normed_in[...].reshape(4 * count, D)
        return dot(parts[...], whole, 1, 0).astype(low_type).T

    loads[0].wait()
    put(terms[2], dot(normed_in[3], query_low, 0, 0))
    planes[2].step(0)
    loads[1].wait()
    loads[2].wait()
    put(terms[0], of_row(value_in))
    planes[0].step(0)
    planes[2].step(1)
    loads[3].wait()
    put(terms[1], of_row(key_in))
    planes[1].step(0)
    planes[2].step(2)
    planes[0].step(1)

    for load in loads[4:]:
        load.wait()
    scaled = (dot(query_low, weight_in[...], 1, 1) + part_in[...].T) * gains[0:1, :]
    planes[1].step(1)
    planes[0].step(2)
    planes[2].step(3)
    planes[2].step(4)
    lines[2].step(0)
    source = inputs[...].astype(f32)
    inverse = lax.rsqrt(jnp.mean(source * source, axis=1, keepdims=True) + norm_epsilon)
    along = jnp.mean(source * scaled, axis=1, keepdims=True)
    input_grad[...] = (
        residual_in[...] + inverse * scaled - source * (inverse * inverse * inverse * along)
    ).astype(low_type)
    planes[1].step(2)
    planes[0].step(3)
    planes[0].step(4)
    lines[0].step(0)

    blocks = query_blocks_of(picks.shape[0])
    buckets = (picks.shape[0] - 16) // blocks
    rows = folded.shape[0] * folded.shape[1]
    flat = split_low(folded[...].reshape(rows, folded.shape[2]))
    parted = dot(jnp.concatenate(flat, axis=0), picks[: blocks * buckets, :], 1, 1)
    parted = parted[:rows] + parted[rows : 2 * rows] + parted[2 * rows :]
    row = lax.broadcasted_iota(jnp.int32, parted.shape, 0) % folded.shape[1]
    lane = lax.broadcasted_iota(jnp.int32, parted.shape, 1)
    parted = jnp.where(row == lane // buckets, parted, 0.0)
    at_bucket = (
        lax.broadcasted_iota(jnp.int32, (blocks * buckets, buckets), 0) % buckets
        == lax.broadcasted_iota(jnp.int32, (blocks * buckets, buckets), 1)
    )
    at_bucket = at_bucket.astype(f32).astype(low_type)
    table = sum(dot(term, at_bucket, 1, 0) for term in split_low(parted))
    table = jnp.sum(table.reshape(HEADS, folded.shape[1], buckets), axis=1)
    early_own[:, D + 256 : D + 256 + buckets] = table[:8]
    early_own[0 : HEADS - 8, D + 384 : D + 384 + buckets] = table[8:]
    early_own[2:3, :D] = gain_two[...]

    planes[1].step(3)
    planes[1].step(4)
    lines[1].step(0)
    for line in rest_lines:
        line.step(1)

    def statistics(raw, previous):
        gradient = raw * scale
        squares = gradient * gradient + tiny_term
        means = jnp.sum(jnp.mean(squares, axis=1, keepdims=True), axis=0, keepdims=True)
        before = jnp.sum(previous.reshape(1, previous.shape[0]), axis=1, keepdims=True)
        row_sum = decay_rate * before + (1.0 - decay_rate) * means
        return jnp.sum(squares, axis=0, keepdims=True), jnp.broadcast_to(row_sum, (1, 128))

    lines[2].step(1)
    lines[0].step(1)
    for line in rest_lines:
        line.step(2)
    for position in (1, 2, 3):
        columns, row_sum = statistics(shares[position][...], rows_before[position][...])
        early_own[position : position + 1, D : D + 128] = row_sum
        if position == 2:
            for part in range(4):
                early_own[4 + part : 5 + part, :D] = columns[:, D * part : D * part + D]
        else:
            early_own[position // 2 : position // 2 + 1, :D] = columns
    first.step(0)
    lines[1].step(1)
    first.step(1)
    for line in lines:
        line.step(2)

    raw = shares[0][...]
    columns, row_sum = statistics(raw, rows_before[0][...])
    for part in range(3):
        late_own[part : part + 1, :] = columns[:, D * part : D * part + D]
    late_own[4:5, :128] = row_sum
    own_rows = raw.shape[0]
    lane = lax.broadcasted_iota(jnp.int32, (own_rows, D), 1)
    row = lax.broadcasted_iota(jnp.int32, (own_rows, D), 0)
    mine = lane == row + (at.seq * 8 + at.dp) * own_rows
    gain_one = jnp.sum(
        raw * own_weight[...].astype(low_type).astype(f32), axis=1, keepdims=True
    )
    spread = jnp.where(mine, jnp.broadcast_to(gain_one, (own_rows, D)), 0.0)
    late_own[3:4, :] = jnp.sum(spread, axis=0, keepdims=True) / gains[0:1, :]
    second.step(0)
    first.step(2)
    early_total[...] = first.total()
    second.step(1)
    second.step(2)
    late_total[...] = second.total()


def query_blocks_of(rows):
    return (rows - 16) // 32


def close(scale, large, small, kept_rest, rows_before, weight_shapes):
    in_place = pl.BlockSpec(memory_space=pltpu.VMEM)
    anywhere = pl.BlockSpec(memory_space=pl.ANY)
    count, row_length = small[0].shape[0], large[1].shape[1]
    scratch = [
        pltpu.VMEM((4, count, D), low_type),
        pltpu.VMEM((D, row_length), low_type),
        pltpu.VMEM((D, row_length), low_type),
        pltpu.VMEM((D, D), low_type),
        pltpu.VMEM((D, count), f32),
        pltpu.VMEM((count, D), f32),
        pltpu.SemaphoreType.DMA((7,)),
    ]
    scratch += sum_scratch(EARLY_WIDTH) + sum_scratch(LATE_WIDTH)
    scratch += [pltpu.VMEM((4, 2, 2, D // 16, D), low_type)] * 3
    scratch += [pltpu.VMEM((4, D // 16, D // 2), low_type)] * 3
    for _ in CLOSE_PLANS:
        scratch += plane_scratch(D // 16, D) + line_scratch(D // 16, D)
    for which, _, width, _ in BACK_PLANS:
        scratch += line_scratch(2 * weight_shapes[which + 1][0], width)
    return pl.pallas_call(
        functools.partial(close_kernel, scale),
        out_shape=[jax.ShapeDtypeStruct((count, D), low_type)]
        + [jax.ShapeDtypeStruct(shape, f32) for shape in weight_shapes]
        + [
            jax.ShapeDtypeStruct((8, EARLY_WIDTH), f32),
            jax.ShapeDtypeStruct((8, LATE_WIDTH), f32),
        ],
        in_specs=[anywhere] * 3
        + [in_place]
        + [anywhere] * 2
        + [in_place, anywhere]
        + [in_place] * 5
        + [anywhere] * 5
        + [in_place] * 4,
        out_specs=[in_place] * 7,
        scratch_shapes=scratch,
        compiler_params=pltpu.CompilerParams(
            collective_id=2, has_side_effects=True, vmem_limit_bytes=close_vmem
        ),
        name="close_layer",
    )(*large, *small, *kept_rest, *rows_before)


def apply_kernel(scale, *refs):
    shares, early, late, far, refs = refs[:4], refs[4], refs[5], refs[6:22], refs[22:]
    near, load_sems = refs[22:38], refs[38]
    loads = [
        pltpu.make_async_copy(source, target, load_sems.at[k])
        for k, (source, target) in enumerate(zip(far, near))
    ]
    for load in loads:
        load.start()
    for load in loads:
        load.wait()
    weights, rows_before, columns_before = near[:4], near[4:8], near[8:12]
    gains, gains_moment, table, table_moment = near[12:]
    gradients, updated, rows_after, columns_after = refs[:4], refs[4:8], refs[8:12], refs[12:16]
    gains_out, table_out = refs[16:19], refs[19:22]
    early_sums, late_sums = early[...], late[...]
    sums = [
        jnp.concatenate([late_sums[part : part + 1] for part in range(3)], axis=1),
        early_sums[0:1, :D],
        jnp.concatenate([early_sums[4 + part : 5 + part, :D] for part in range(4)], axis=1),
        early_sums[1:2, :D],
    ]
    row_sums = [late_sums[4:5, 0:1]] + [early_sums[k : k + 1, D : D + 1] for k in (1, 2, 3)]
    for position in range(4):
        rows, width = shares[position].shape
        full = rows * 32
        gradient = shares[position][...] * scale
        gradients[position][...] = gradient
        squares = gradient * gradient + tiny_term
        eye = lax.broadcasted_iota(jnp.int32, (rows, rows), 0) == lax.broadcasted_iota(
            jnp.int32, (rows, rows), 1
        )
        before = jnp.broadcast_to(rows_before[position][...].reshape(1, rows), (rows, rows))
        before = jnp.sum(jnp.where(eye, before, 0.0), axis=1, keepdims=True)
        rows_new = decay_rate * before + (1.0 - decay_rate) * jnp.mean(
            squares, axis=1, keepdims=True
        )
        rows_after[position][...] = jnp.sum(
            jnp.where(eye, jnp.broadcast_to(rows_new, (rows, rows)), 0.0), axis=0, keepdims=True
        ).reshape(rows)
        columns_new = decay_rate * columns_before[position][...].reshape(1, width) + (
            1.0 - decay_rate
        ) * (sums[position] / full)
        columns_after[position][...] = columns_new.reshape(width)
        denominator = rows_new * columns_new / (row_sums[position] / full)
        updated[position][...] = weights[position][...] - learn_rate * gradient * lax.rsqrt(
            denominator
        )

    def moments(gradient, old, moment, results):
        moment_new = decay_rate * moment[...] + (1.0 - decay_rate) * (
            gradient * gradient + tiny_term
        )
        results[0][...] = gradient
        results[1][...] = old[...] - learn_rate * gradient * lax.rsqrt(moment_new)
        results[2][...] = moment_new

    moments(
        jnp.concatenate([late_sums[3:4, :D], early_sums[2:3, :D]], axis=0) * scale,
        gains,
        gains_moment,
        gains_out,
    )
    buckets = table.shape[1]
    of_table = jnp.concatenate(
        [
            early_sums[:, D + 256 : D + 256 + buckets],
            early_sums[0 : HEADS - 8, D + 384 : D + 384 + buckets],
        ],
        axis=0,
    )
    moments(of_table * scale, table, table_moment, table_out)


def apply_updates(scale, shares, sums, weights, rows_before, columns_before, rest):
    in_place = pl.BlockSpec(memory_space=pltpu.VMEM)
    same = lambda arrays: [jax.ShapeDtypeStruct(array.shape, f32) for array in arrays]
    gains, table = rest[0], rest[2]
    far = [*weights, *rows_before, *columns_before, *rest]
    far = [pltpu.with_memory_space_constraint(array, pltpu.HBM) for array in far]
    return pl.pallas_call(
        functools.partial(apply_kernel, scale),
        out_shape=same(weights)
        + same(weights)
        + same(rows_before)
        + same(columns_before)
        + same([gains] * 3)
        + same([table] * 3),
        in_specs=[in_place] * 6 + [pl.BlockSpec(memory_space=pl.ANY)] * 16,
        out_specs=[in_place] * 22,
        scratch_shapes=[pltpu.VMEM(array.shape, f32) for array in far]
        + [pltpu.SemaphoreType.DMA((16,))],
        compiler_params=pltpu.CompilerParams(vmem_limit_bytes=apply_vmem),
        name="apply_updates",
    )(*shares, *sums, *far)


def middle_kernel(
    context_t,
    log_total,
    inputs,
    upstream,
    gains,
    output_weight,
    expand_weight,
    reduce_weight,
    layer_output,
    residual_grad,
    output_term,
    expand_term,
    reduce_term,
    context_grad,
    context_grad_t,
    row_columns,
    gain_two,
    residual,
    normed,
    normed_t,
    reduced,
    normed_grad,
):
    step = pl.program_id(0)
    gain = gains[1:2, :]

    def inverse():
        values = residual[...]
        return lax.rsqrt(jnp.mean(values * values, axis=1, keepdims=True) + norm_epsilon)

    @pl.when(step == 0)
    def _():
        residual[...] = inputs[...].astype(f32) + dot(
            context_t[...].astype(low_type), output_weight[...], 0, 0
        )
        normed_low = (residual[...] * inverse() * gain).astype(low_type)
        normed[...] = normed_low
        normed_t[...] = normed_low.T
        reduced[...] = jnp.zeros_like(reduced)
        normed_grad[...] = jnp.zeros_like(normed_grad)

    expanded = dot(normed[...], expand_weight[...], 1, 0)
    squared = expanded * expanded
    bent = jnp.tanh(0.7978845608028654 * expanded * (1.0 + 0.044715 * squared))
    above = 0.5 * (1.0 + bent)
    activated = (expanded * above).astype(low_type)
    slope = above + 0.5 * expanded * (1.0 - bent * bent) * (
        0.7978845608028654 * (1.0 + 3.0 * 0.044715 * squared)
    )
    expanded_low = (dot(upstream[...], reduce_weight[...], 1, 1) * slope).astype(low_type)
    reduced[...] += dot(activated, reduce_weight[...], 1, 0)
    reduce_term[...] = dot(activated, upstream[...], 0, 0).astype(low_type)
    normed_grad[...] += dot(expanded_low, expand_weight[...], 1, 1)
    expand_term[...] = dot(normed_t[...], expanded_low, 1, 0).astype(low_type)

    @pl.when(step == pl.num_programs(0) - 1)
    def _():
        values, scale = residual[...], inverse()
        layer_output[...] = (values + reduced[...]).astype(low_type)
        gain_two[...] = jnp.sum(normed_grad[...] * values * scale, axis=0, keepdims=True)
        scaled = normed_grad[...] * gain
        along = jnp.mean(values * scaled, axis=1, keepdims=True)
        gradient = (
            upstream[...].astype(f32)
            + scale * scaled
            - values * (scale * scale * scale * along)
        )
        residual_grad[...] = gradient
        low = gradient.astype(low_type)
        output_term[...] = dot(context_t[...].astype(low_type), low, 1, 0).astype(low_type)
        context_grad[...] = dot(low, output_weight[...], 1, 1).astype(low_type)
        turned = dot(output_weight[...], low, 1, 1).astype(low_type)
        context_grad_t[...] = turned
        count = low.shape[0]
        delta = jnp.sum(
            (turned.astype(f32) * context_t[...]).reshape(HEADS, HEAD, count), axis=1
        )
        rows = jnp.concatenate(
            [log_total[0:HEADS, :], delta, jnp.zeros((128 - 2 * HEADS, count), f32)], axis=0
        )
        row_columns[...] = rows.T


def middle(context_t, log_total, inputs, upstream, gains, output_weight, expand_weight, reduce_weight):
    count = inputs.shape[0]
    hidden = expand_weight.shape[1]
    still = lambda *shape: pl.BlockSpec(shape, lambda step: (0,) * len(shape))
    low = lambda *shape: pltpu.HBM(shape, low_type)
    across = pl.BlockSpec((D, D), lambda step: (0, step))
    down = pl.BlockSpec((D, D), lambda step: (step, 0))
    return pl.pallas_call(
        middle_kernel,
        grid=(hidden // D,),
        out_shape=[
            low(count, D),
            pltpu.HBM((count, D), f32),
            low(D, D),
            low(D, hidden),
            low(hidden, D),
            low(count, D),
            low(D, count),
            jax.ShapeDtypeStruct((count, 128), f32),
            jax.ShapeDtypeStruct((1, D), f32),
        ],
        in_specs=[
            still(D, count),
            still(*log_total.shape),
            still(count, D),
            still(count, D),
            still(2, D),
            still(D, D),
            across,
            down,
        ],
        out_specs=[
            still(count, D),
            still(count, D),
            still(D, D),
            across,
            down,
            still(count, D),
            still(D, count),
            still(count, 128),
            still(1, D),
        ],
        scratch_shapes=[
            pltpu.VMEM((count, D), f32),
            pltpu.VMEM((count, D), low_type),
            pltpu.VMEM((D, count), low_type),
            pltpu.VMEM((count, D), f32),
            pltpu.VMEM((count, D), f32),
        ],
        compiler_params=pltpu.CompilerParams(vmem_limit_bytes=middle_vmem),
        cost_estimate=pl.CostEstimate(
            flops=2 * count * D * (6 * hidden + 4 * D),
            bytes_accessed=8 * D * hidden + 20 * count * D,
            transcendentals=count * hidden,
        ),
        name="middle",
    )(
        context_t,
        log_total,
        *in_hbm(inputs, upstream, gains, output_weight, expand_weight, reduce_weight),
    )


BACK_PLANS = (
    (1, 0, 2 * D, False),
    (2, 0, 512, True),
    (1, 2 * D, 2 * D, False),
    (2, 512, 256, True),
    (0, 0, D, True),
)
EARLY, LATE = (0, 1), (2, 3, 4)
BACK_TIMES = (
    (0, None),
    (0, (EARLY, 0)),
    (1, (LATE, 0)),
    (2, (EARLY, 1)),
    (7, (EARLY, 2)),
    (7, (LATE, 1)),
    (11, (EARLY, 3)),
    (13, (LATE, 2)),
    (17, (LATE, 3)),
    (23, (EARLY, 4)),
    (23, (LATE, 4)),
)


class Relay:
    def __init__(self, at, kept, arrived, sems):
        self.kept, self.arrived = kept, arrived
        seq = at.seq
        self.is_end = (seq == 0) | (seq == 3)
        self.is_inner = (seq == 1) | (seq == 2)
        inwards = (1 + seq // 3, at.dp)
        outwards = ((3 * seq + 1) % 4, at.dp)
        across = ((7 - seq) % 4, at.dp)
        half = kept.shape[2] // 2
        self.halves = [pl.ds(0, half), pl.ds(half, half)]

        def by_half(source, target, index, partner):
            return [
                send(kept.at[source, :, rows], arrived.at[target, :, rows], sems, 2 * index + k, partner)
                for k, rows in enumerate(self.halves)
            ]

        self.from_end = [by_half(k, k, k, inwards) for k in range(3)]
        self.to_peer = [by_half(1, 3, 3, across), by_half(0, 4, 4, across)]
        self.to_end = by_half(2, 0, 5, outwards)

    def turn(self, number, part, total):
        kept, arrived = self.kept, self.arrived
        low = lambda values: values.astype(low_type)
        wide = lambda ref, k, rows: ref[k, :, rows].astype(f32)
        of = lambda rows: part[:, rows.start : rows.start + rows.size]
        halves = list(enumerate(self.halves))
        if number < 3:

            @pl.when(self.is_end)
            def _():
                for k, rows in halves:
                    kept[number, :, rows] = low(of(rows))
                    self.from_end[number][k].start()

        if number == 0:

            @pl.when(self.is_inner)
            def _():
                kept[0] = low(part)

        elif number == 1:

            @pl.when(self.is_inner)
            def _():
                for k, rows in halves:
                    self.from_end[0][k].wait_recv()
                    kept[1, :, rows] = low(of(rows) + wide(arrived, 0, rows))
                    self.to_peer[0][k].start()

        elif number == 2:

            @pl.when(self.is_inner)
            def _():
                for k, rows in halves:
                    self.to_peer[0][k].wait_recv()
                    kept[2, :, rows] = low(of(rows) + wide(arrived, 3, rows))
                    self.to_end[k].start()
                    self.from_end[1][k].wait_recv()
                    kept[0, :, rows] = low(wide(kept, 0, rows) + wide(arrived, 1, rows))
                    self.to_peer[1][k].start()

        else:

            @pl.when(self.is_end)
            def _():
                for k, rows in halves:
                    self.to_end[k].wait_recv()
                    total[:, rows] = of(rows) + wide(arrived, 0, rows)
                    for copies in self.from_end:
                        copies[k].wait_send()

            @pl.when(self.is_inner)
            def _():
                for k, rows in halves:
                    self.to_peer[1][k].wait_recv()
                    self.from_end[2][k].wait_recv()
                    total[:, rows] = of(rows) + wide(arrived, 2, rows) + wide(arrived, 4, rows)
                    for copies in self.to_peer + [self.to_end]:
                        copies[k].wait_send()


def backward_kernel(
    queries,
    extra,
    row_columns,
    context_grad,
    queries_t,
    context_grad_t,
    keys,
    values_t,
    keys_extra,
    *refs,
):
    turn, pair = pl.program_id(0), pl.program_id(1)
    remote = len(refs) > 4
    if remote:
        key_weight, value_weight, terms, refs = refs[0], refs[1], refs[2:5], refs[5:]
        total, kept_rest, scratch = refs[4], refs[5:10], refs[10:]
        parts, kept, arrived, relay_sems = scratch[:4]
        at = Place()
        relay = Relay(at, kept, arrived, relay_sems)
        scatters = [
            take_plane(at, plan, terms[plan[0]], kept_rest[k], scratch[4 + 6 * k : 10 + 6 * k])
            for k, plan in enumerate(BACK_PLANS)
        ]
        now = turn * PAIRS + pair
        for when, doing in BACK_TIMES:

            @pl.when(now == when)
            def _(doing=doing):
                if doing is None:
                    at.greet()
                else:
                    for which in doing[0]:
                        scatters[which].step(doing[1])

    query_grad, key_grad_t, value_grad_t, folded = refs[:4]
    count = queries.shape[0]
    lane = lax.broadcasted_iota(jnp.int32, (count, PAIR), 1)
    query_pair, grad_pair = queries[...], context_grad[...]
    zeros = jnp.zeros_like(query_pair)
    lanes = pl.ds(pl.multiple_of(PAIR * pair, PAIR), PAIR)
    columns = pltpu.roll(row_columns[...], (128 - 2 * pair) % 128, 1)

    @pl.when(turn == 0)
    def _():
        query_grad[:, lanes] = jnp.zeros((count, PAIR), f32)

    query_grads = []
    for head in range(2):
        mine = (lane < HEAD) if head == 0 else (lane >= HEAD)
        rows = pl.ds(HEAD * head, HEAD)
        query_side = jnp.concatenate([jnp.where(mine, query_pair, zeros), extra[...]], axis=1)
        key_side = jnp.concatenate(
            [keys[...], keys_extra[:, 128 * head : 128 * head + 128]], axis=1
        )
        attention = jnp.exp(dot(query_side, key_side, 1, 1) - columns[:, head : head + 1])
        score_grad = attention * (
            dot(jnp.where(mine, grad_pair, zeros), values_t[0], 1, 0)
            - columns[:, HEADS + head : HEADS + head + 1]
        )
        attention_low = attention.astype(low_type)
        score_low = score_grad.astype(low_type)
        sums = [
            jnp.sum(score_grad[BLK * block : BLK * block + BLK], axis=0, keepdims=True)
            for block in range(count // BLK)
        ]
        spare = folded.shape[1] - len(sums)
        folded[head] = jnp.concatenate(sums + [jnp.zeros((spare, count), f32)] * (spare > 0), axis=0)
        query_grads.append(dot(score_low, keys[...], 1, 0))
        value_grad_t[rows, :] = dot(context_grad_t[rows, :], attention_low, 1, 0).astype(low_type)
        key_grad_t[rows, :] = dot(queries_t[rows, :], score_low, 1, 0).astype(low_type)
    query_grad[:, lanes] += jnp.where(lane < HEAD, query_grads[0], query_grads[1])

    if remote:
        parts[pl.ds(pl.multiple_of(PAIR * pair, PAIR), PAIR), :] = key_grad_t[...]
        parts[pl.ds(pl.multiple_of(D + PAIR * pair, PAIR), PAIR), :] = value_grad_t[...]
        for number in range(4):

            @pl.when(now == number * PAIRS + PAIRS - 1)
            def _(number=number):
                part = dot(key_weight[...], parts[:D], 1, 0) + dot(value_weight[...], parts[D:], 1, 0)
                relay.turn(number, part, total)


def attend_back(
    queries,
    extra,
    row_columns,
    context_grad,
    queries_t,
    context_grad_t,
    keys,
    values_t,
    keys_extra,
    weights,
    terms,
):
    count, row_length = queries.shape[0], keys.shape[0]
    fold_rows = -(-(count // BLK) // 8) * 8
    terms = [by_chip(term) for term in terms]
    anywhere = pl.BlockSpec(memory_space=pl.ANY)
    of_pair = pl.BlockSpec((count, PAIR), lambda turn, pair: (0, pair))
    of_pair_t = pl.BlockSpec((PAIR, count), lambda turn, pair: (pair, 0))
    key_t = pl.BlockSpec((PAIR, count), lambda turn, pair: (pair, turn))
    still = lambda *shape: pl.BlockSpec(shape, lambda turn, pair: (0,) * len(shape))
    remote, more_specs, more_shapes, more_out, scratch, more = {}, [], [], [], [], []
    if terms:
        remote = {"collective_id": 1, "has_side_effects": True}
        more = [weights, weights, *terms]
        columns = [pl.BlockSpec((D, D), lambda turn, pair, k=k: (0, k)) for k in (1, 2)]
        more_specs = columns + [anywhere] * 3
        more_shapes = [jax.ShapeDtypeStruct((D, count), f32)] + [
            jax.ShapeDtypeStruct((4, terms[which].shape[3], width // 2), low_type)
            for which, _, width, _ in BACK_PLANS
        ]
        more_out = [still(D, count)] + [anywhere] * len(BACK_PLANS)
        scratch = [
            pltpu.VMEM((2 * D, count), low_type),
            pltpu.VMEM((3, D, count), low_type),
            pltpu.VMEM((5, D, count), low_type),
            pltpu.SemaphoreType.DMA((2, 12)),
        ]
        for which, _, width, _ in BACK_PLANS:
            scratch += plane_scratch(terms[which].shape[3], width)
    return pl.pallas_call(
        backward_kernel,
        grid=(row_length // count, PAIRS),
        out_shape=[
            jax.ShapeDtypeStruct((count, D), f32),
            jax.ShapeDtypeStruct((D, row_length), low_type),
            jax.ShapeDtypeStruct((D, row_length), low_type),
            jax.ShapeDtypeStruct((HEADS, fold_rows, row_length), f32),
        ]
        + more_shapes,
        in_specs=[
            of_pair,
            still(count, 128),
            still(count, 128),
            of_pair,
            of_pair_t,
            of_pair_t,
            pl.BlockSpec((count, PAIR), lambda turn, pair: (turn, pair)),
            pl.BlockSpec((1, PAIR, count), lambda turn, pair: (turn, pair, 0)),
            pl.BlockSpec((count, 256), lambda turn, pair: (turn, pair)),
        ]
        + more_specs,
        out_specs=[
            still(count, D),
            key_t,
            key_t,
            pl.BlockSpec((2, fold_rows, count), lambda turn, pair: (pair, 0, turn)),
        ]
        + more_out,
        scratch_shapes=scratch,
        compiler_params=pltpu.CompilerParams(vmem_limit_bytes=back_vmem, **remote),
        cost_estimate=pl.CostEstimate(
            flops=10 * HEADS * count * row_length * 200,
            bytes_accessed=HEADS * row_length * 2048,
            transcendentals=HEADS * count * row_length,
        ),
        name="attention_backward",
    )(
        *in_hbm(
            queries,
            extra,
            row_columns,
            context_grad,
            queries_t,
            context_grad_t,
            keys,
            values_t,
            keys_extra,
            *more,
        )
    )


def body(
    hidden_states,
    output_cotangent,
    document_lengths,
    bucket_index,
    norm_gains,
    bias_table,
    project_weight,
    output_weight,
    expand_weight,
    reduce_weight,
    project_rows,
    project_columns,
    output_rows,
    output_columns,
    expand_rows,
    expand_columns,
    reduce_rows,
    reduce_columns,
    gains_moment,
    table_moment,
):
    every = ("seq", "dp")
    local_rows = hidden_states.shape[1]
    row_length = local_rows * lax.axis_size("seq")
    gradient_scale = 1.0 / math.sqrt(row_length * lax.axis_size("dp"))
    place = lax.axis_index("seq")
    blocks = local_rows // BLK

    shards = (project_weight, output_weight, expand_weight, reduce_weight)
    direct = (
        lax.axis_size("seq") == 4
        and lax.axis_size("dp") == 8
        and all(shard.shape[0] % 8 == 0 and shard.shape[1] % 256 == 0 for shard in shards)
    )
    inputs = hidden_states[0].astype(f32)
    if direct:
        opened = open_layer(
            shards, hidden_states[0], norm_gains, bucket_index, bias_table, document_lengths
        )
        project_full, output_full, expand_full, reduce_full = (
            whole.reshape(-1, whole.shape[4]) for whole in opened[:4]
        )
        normed_all, keys = (blocks_of.reshape(row_length, D) for blocks_of in opened[4:6])
        values_t, keys_extra, picks, queries, queries_t, context_t, log_total, extra = opened[6:]
        normed_low = normed_all[row_length - local_rows :]
    else:
        project_full, output_full, expand_full, reduce_full = (
            lax.all_gather(shard.astype(low_type), every, axis=0, tiled=True) for shard in shards
        )
        row_states = lax.all_gather(hidden_states[0], "seq", axis=0, tiled=True)
        normed_low = rms_norm(inputs, norm_gains[0]).astype(low_type)
        normed_all = rms_norm(row_states.astype(f32), norm_gains[0]).astype(low_type)
        doc_all = documents(document_lengths[0], row_length)
        doc_query = lax.dynamic_slice_in_dim(doc_all, place * local_rows, local_rows)
        picks = key_picks(bucket_index[0], doc_all, bias_table.shape[0])
        one_hot = picks[:, : blocks * bias_table.shape[0]]
        keys_extra = key_extra(picks, bias_table, blocks)
        extra = query_extra(doc_query, blocks)
        scaled = lambda values: (values.astype(low_type).astype(f32) * score_scale).astype(low_type)
        queries = scaled(dot(normed_low, project_full[:, :D], 1, 0))
        queries_t = scaled(dot(project_full[:, :D], normed_low, 0, 1))
        keys = dot(normed_all, project_full[:, D : 2 * D], 1, 0).astype(low_type)
        values_t = dot(project_full[:, 2 * D :], normed_all, 0, 1).astype(low_type)
        context_t, log_total = attend(queries, extra, keys, values_t, keys_extra)
        log_total = log_total.reshape(HEADS, 8, local_rows)[:, 0]
        values_t = jnp.transpose(values_t.reshape(D, -1, local_rows), (1, 0, 2))
    _, pullback_one = jax.vjp(rms_norm, inputs, norm_gains[0])
    query_weight, key_weight, value_weight = (
        project_full[:, :D],
        project_full[:, D : 2 * D],
        project_full[:, 2 * D :],
    )
    (
        layer_output,
        residual_grad,
        output_term,
        expand_term,
        reduce_term,
        context_grad,
        context_grad_t,
        row_columns,
        gain_two_grad,
    ) = middle(
        context_t,
        log_total,
        hidden_states[0],
        output_cotangent[0],
        norm_gains,
        output_full,
        expand_full,
        reduce_full,
    )
    layer_output = layer_output[None]
    query_grad, key_grad_t, value_grad_t, folded, *summed_back = attend_back(
        queries,
        extra,
        row_columns,
        context_grad,
        queries_t,
        context_grad_t,
        keys,
        values_t,
        keys_extra,
        project_full,
        [output_term, expand_term, reduce_term] if direct else [],
    )
    if direct:
        rows_before = [project_rows, output_rows, expand_rows, reduce_rows]
        input_gradient, *results = close(
            gradient_scale,
            (
                normed_all.reshape(4, local_rows, D),
                key_grad_t,
                value_grad_t,
                query_grad,
                project_full,
                summed_back[0],
            ),
            (
                hidden_states[0],
                residual_grad,
                folded,
                picks,
                norm_gains,
                gain_two_grad,
                project_weight,
            ),
            summed_back[1:],
            rows_before,
            [shard.shape for shard in shards],
        )
        results = apply_updates(
            gradient_scale,
            results[:4],
            results[4:6],
            shards,
            rows_before,
            [project_columns, output_columns, expand_columns, reduce_columns],
            (norm_gains, gains_moment, bias_table.T, table_moment.T),
        )
        gradients, updated_weights, row_after, columns_after = (
            results[:4],
            results[4:8],
            results[8:12],
            results[12:16],
        )
        gains_gradient, gains_updated, gains_moment_new = results[16:19]
        table_gradient, table_updated, table_moment_new = (table.T for table in results[19:])
        return (
            layer_output,
            input_gradient[None],
            gains_gradient,
            table_gradient,
            *gradients,
            gains_updated,
            table_updated,
            *updated_weights,
            row_after[0],
            columns_after[0],
            row_after[1],
            columns_after[1],
            row_after[2],
            columns_after[2],
            row_after[3],
            columns_after[3],
            gains_moment_new,
            table_moment_new,
        )

    buckets = bias_table.shape[0]
    picked = jnp.dot(
        folded[:, :blocks].reshape(HEADS * blocks, row_length),
        one_hot.astype(f32),
        precision=lax.Precision.HIGHEST,
    )
    table_grad = jnp.einsum("hkkb->bh", picked.reshape(HEADS, blocks, blocks, buckets))

    query_grad_low = (query_grad * score_scale).astype(low_type)
    project_terms = [
        dot(normed_low, query_grad_low, 0, 0),
        dot(normed_all, key_grad_t, 0, 1),
        dot(normed_all, value_grad_t, 0, 1),
    ]
    key_part = dot(key_grad_t, key_weight, 0, 1) + dot(value_grad_t, value_weight, 0, 1)
    key_part = lax.psum_scatter(
        key_part.astype(low_type), "seq", scatter_dimension=0, tiled=True
    ).astype(f32)
    input_part, gain_one_grad = pullback_one(dot(query_grad_low, query_weight, 1, 1) + key_part)
    input_gradient = (residual_grad + input_part).astype(low_type)[None]
    terms = [
        term.astype(low_type)
        for term in (jnp.concatenate(project_terms, axis=1), output_term, expand_term, reduce_term)
    ]
    shares = [
        lax.psum_scatter(term, every, scatter_dimension=0, tiled=True).astype(f32)
        for term in terms
    ]
    gradients = tuple((share * gradient_scale for share in shares))
    row_before = (project_rows, output_rows, expand_rows, reduce_rows)
    row_after = []
    column_parts = []
    row_sums = []
    for gradient, previous in zip(gradients, row_before):
        squares = gradient * gradient + tiny_term
        updated_rows = decay_rate * previous + (1.0 - decay_rate) * jnp.mean(squares, axis=1)
        row_after.append(updated_rows)
        column_parts.append(jnp.sum(squares, axis=0))
        row_sums.append(jnp.sum(updated_rows))
    summed = lax.psum(
        (
            column_parts[0],
            column_parts[1],
            column_parts[2],
            column_parts[3],
            jnp.stack(row_sums),
            jnp.stack([gain_one_grad, gain_two_grad[0]]),
            table_grad,
        ),
        every,
    )
    column_before = (project_columns, output_columns, expand_columns, reduce_columns)
    weights_before = (project_weight, output_weight, expand_weight, reduce_weight)
    full_rows = (
        project_full.shape[0],
        output_full.shape[0],
        expand_full.shape[0],
        reduce_full.shape[0],
    )
    updated_weights = []
    columns_after = []
    for position in range(4):
        columns_new = decay_rate * column_before[position] + (1.0 - decay_rate) * (
            summed[position] / full_rows[position]
        )
        row_mean = summed[4][position] / full_rows[position]
        denominator = row_after[position][:, None] * columns_new[None, :] / row_mean
        updated_weights.append(
            weights_before[position] - learn_rate * gradients[position] * lax.rsqrt(denominator)
        )
        columns_after.append(columns_new)
    gains_gradient = summed[5] * gradient_scale
    table_gradient = summed[6] * gradient_scale
    gains_moment_new = decay_rate * gains_moment + (1.0 - decay_rate) * (
        gains_gradient * gains_gradient + tiny_term
    )
    gains_updated = norm_gains - learn_rate * gains_gradient * lax.rsqrt(gains_moment_new)
    table_moment_new = decay_rate * table_moment + (1.0 - decay_rate) * (
        table_gradient * table_gradient + tiny_term
    )
    table_updated = bias_table - learn_rate * table_gradient * lax.rsqrt(table_moment_new)
    return (
        layer_output,
        input_gradient,
        gains_gradient,
        table_gradient,
        gradients[0],
        gradients[1],
        gradients[2],
        gradients[3],
        gains_updated,
        table_updated,
        updated_weights[0],
        updated_weights[1],
        updated_weights[2],
        updated_weights[3],
        row_after[0],
        columns_after[0],
        row_after[1],
        columns_after[1],
        row_after[2],
        columns_after[2],
        row_after[3],
        columns_after[3],
        gains_moment_new,
        table_moment_new,
    )


def solution(mesh):
    placed = (
        P("dp", "seq", None),
        P("dp", "seq", None),
        P("dp", None),
        P("dp", "seq", None),
        P(),
        P(),
        P(("seq", "dp"), None),
        P(("seq", "dp"), None),
        P(("seq", "dp"), None),
        P(("seq", "dp"), None),
        P(("seq", "dp")),
        P(),
        P(("seq", "dp")),
        P(),
        P(("seq", "dp")),
        P(),
        P(("seq", "dp")),
        P(),
        P(),
        P(),
    )
    return jax.shard_map(
        body,
        mesh=mesh,
        in_specs=placed,
        out_specs=(
            P("dp", "seq", None),
            P("dp", "seq", None),
            P(),
            P(),
            P(("seq", "dp"), None),
            P(("seq", "dp"), None),
            P(("seq", "dp"), None),
            P(("seq", "dp"), None),
            P(),
            P(),
            P(("seq", "dp"), None),
            P(("seq", "dp"), None),
            P(("seq", "dp"), None),
            P(("seq", "dp"), None),
            P(("seq", "dp")),
            P(),
            P(("seq", "dp")),
            P(),
            P(("seq", "dp")),
            P(),
            P(("seq", "dp")),
            P(),
            P(),
            P(),
        ),
        check_vma=False,
    )
```

```python
import functools
import math

import jax
import jax.numpy as jnp
from jax import lax
from jax.experimental import pallas as pl
from jax.experimental.pallas import tpu as pltpu
from jax.sharding import PartitionSpec as P

D = 768
HEADS = 12
HEAD = 64
BLK = 128
PAIR = 2 * HEAD
PAIRS = HEADS // 2
DOCS = 5
TERMS = 3

score_scale = 0.125
masked_score = -1e30
norm_epsilon = 1e-06
tiny_term = 1e-30
learn_rate = 0.3
decay_rate = 1.0 - 2.0 ** (-0.8)
vmem_bytes = 56 * 2**20
open_vmem = 48 * 2**20
back_vmem = 48 * 2**20
close_vmem = 48 * 2**20
apply_vmem = 16 * 2**20
middle_vmem = 52 * 2**20

low_type = jnp.bfloat16
f32 = jnp.float32


def dot(former, latter, former_axis, latter_axis):
    return lax.dot_general(
        former,
        latter,
        (((former_axis,), (latter_axis,)), ((), ())),
        preferred_element_type=f32,
    )


def in_hbm(*arrays):
    return [pltpu.with_memory_space_constraint(array, pltpu.HBM) for array in arrays]


def rms_norm(values, gain_vector):
    return (
        values
        * lax.rsqrt(jnp.mean(values * values, axis=-1, keepdims=True) + norm_epsilon)
        * gain_vector
    )


def documents(lengths, row_length):
    doc_ends = jnp.cumsum(lengths)
    position = jnp.arange(row_length, dtype=jnp.int32)
    return jnp.sum((position[:, None] >= doc_ends[None, :]).astype(jnp.int32), axis=1)


def split_terms(values):
    terms = []
    rest = values
    for _ in range(TERMS):
        term = lax.reduce_precision(rest, 8, 7)
        terms.append(term)
        rest = rest - term
    return terms


def extra_columns(blocks):
    return TERMS * blocks, TERMS * blocks + DOCS


def query_extra(doc_query, blocks):
    count = doc_query.shape[0]
    doc_start, one_start = extra_columns(blocks)
    lane = lax.broadcasted_iota(jnp.int32, (count, 128), 1)
    block = lax.broadcasted_iota(jnp.int32, (count, 128), 0) // BLK
    is_block = (lane < doc_start) & (lane % blocks == block)
    is_doc = (lane >= doc_start) & (lane < one_start) & (lane - doc_start == doc_query[:, None])
    return (is_block | is_doc).astype(low_type)


def key_picks(bucket_rows, doc_all, buckets):
    blocks, row_length = bucket_rows.shape
    one_hot = (
        bucket_rows.T[:, :, None] == jnp.arange(buckets, dtype=jnp.int32)[None, None, :]
    ).reshape(row_length, blocks * buckets)
    other_doc = doc_all[:, None] != jnp.arange(DOCS, dtype=jnp.int32)[None, :]
    ones = jnp.ones((row_length, 1), jnp.bool_)
    return jnp.concatenate([one_hot, other_doc, ones], axis=1).astype(low_type)


def key_extra(picks, bias_table, blocks):
    buckets = bias_table.shape[0]
    doc_start, one_start = extra_columns(blocks)
    terms = jnp.stack(split_terms(bias_table), axis=0)
    lane = jnp.arange(128, dtype=jnp.int32)
    place = jnp.clip(lane // blocks, 0, TERMS - 1)
    spread = jnp.transpose(terms[place], (1, 2, 0))
    at_block = (lane[None, :] % blocks == jnp.arange(blocks, dtype=jnp.int32)[:, None]) & (
        lane[None, :] < doc_start
    )
    bias_part = jnp.where(at_block[:, None, None, :], spread[None], 0.0).reshape(
        blocks * buckets, HEADS, 128
    )
    doc_part = jnp.where(
        lane[None, :] - doc_start == jnp.arange(DOCS, dtype=jnp.int32)[:, None], masked_score, 0.0
    )
    one_part = ((lane >= one_start) & (lane < one_start + TERMS)).astype(f32)[None]
    rest = jnp.concatenate([doc_part, one_part], axis=0)
    rest = jnp.broadcast_to(rest[:, None, :], (DOCS + 1, HEADS, 128))
    whole = jnp.concatenate([bias_part, rest], axis=0).reshape(-1, HEADS * 128).astype(low_type)
    return dot(picks, whole, 1, 0).astype(low_type)


def forward_kernel(queries, extra, keys, values_t, keys_extra, context_t, log_total):
    count = queries.shape[0]
    lane = lax.broadcasted_iota(jnp.int32, (count, PAIR), 1)
    query_pair = queries[...]
    for head in range(2):
        mine = (lane < HEAD) if head == 0 else (lane >= HEAD)
        query_side = jnp.concatenate(
            [jnp.where(mine, query_pair, jnp.zeros_like(query_pair)), extra[...]], axis=1
        )
        key_side = jnp.concatenate([keys[...], keys_extra[:, 128 * head : 128 * head + 128]], axis=1)
        scores = dot(key_side, query_side, 1, 1)
        top = jnp.max(scores, axis=0, keepdims=True)
        unscaled = jnp.exp(scores - top).astype(low_type)
        value_side = jnp.concatenate(
            [
                values_t[HEAD * head : HEAD * head + HEAD, :],
                jnp.ones((16, unscaled.shape[0]), low_type),
            ],
            axis=0,
        )
        weighted = dot(value_side, unscaled, 1, 0)
        total = weighted[HEAD : HEAD + 1]
        context_t[pl.ds(HEAD * head, HEAD), :] = weighted[:HEAD] / total
        log_total[pl.ds(8 * head, 8), :] = jnp.broadcast_to(top + jnp.log(total), (8, count))


def attend(queries, extra, keys, values_t, keys_extra):
    count, row_length = queries.shape[0], keys.shape[0]
    return pl.pallas_call(
        forward_kernel,
        grid=(PAIRS,),
        out_shape=[
            jax.ShapeDtypeStruct((D, count), f32),
            jax.ShapeDtypeStruct((HEADS * 8, count), f32),
        ],
        in_specs=[
            pl.BlockSpec((count, PAIR), lambda pair: (0, pair)),
            pl.BlockSpec((count, 128), lambda pair: (0, 0)),
            pl.BlockSpec((row_length, PAIR), lambda pair: (0, pair)),
            pl.BlockSpec((PAIR, row_length), lambda pair: (pair, 0)),
            pl.BlockSpec((row_length, 256), lambda pair: (0, pair)),
        ],
        out_specs=[
            pl.BlockSpec((PAIR, count), lambda pair: (pair, 0)),
            pl.BlockSpec((16, count), lambda pair: (pair, 0)),
        ],
        compiler_params=pltpu.CompilerParams(vmem_limit_bytes=vmem_bytes),
        cost_estimate=pl.CostEstimate(
            flops=4 * HEADS * count * row_length * 256,
            bytes_accessed=HEADS * row_length * 1024,
            transcendentals=HEADS * count * row_length,
        ),
        name="attention_forward",
    )(queries, extra, keys, values_t, keys_extra)


MESH = pl.DeviceIdType.MESH


class Place:
    def __init__(self):
        self.seq, self.dp = lax.axis_index("seq"), lax.axis_index("dp")
        self.core, self.x, self.y = self.dp % 2, self.dp // 2 % 2, self.dp // 4
        self.by_core = (self.seq, self.dp + 1 - 2 * self.core)
        self.by_x = (self.seq, self.dp + 2 - 4 * self.x)
        self.by_y = (self.seq, self.dp + 4 - 8 * self.y)
        self.plane = [(self.seq, (self.dp + step) % 8) for step in range(1, 8)]
        self.others = [((self.seq + step) % 4, self.dp) for step in (1, 2, 3)]

    def turn(self, block):
        flip = 3 - self.seq
        return 2 * ((block // 2 + flip // 2) % 2) + (block + flip) % 2

    def greet(self, whole_plane=False):
        barrier = pltpu.get_barrier_semaphore()
        beside = self.plane if whole_plane else [self.by_core, self.by_x, self.by_y]
        partners = beside + self.others
        for partner in partners:
            pl.semaphore_signal(barrier, inc=1, device_id=partner, device_id_type=MESH)
        pl.semaphore_wait(barrier, len(partners))


def send(source, target, sems, index, partner):
    return pltpu.make_async_remote_copy(
        src_ref=source,
        dst_ref=target,
        send_sem=sems.at[0, index],
        recv_sem=sems.at[1, index],
        device_id=partner,
        device_id_type=MESH,
    )


def half_of(start, width, which):
    return pl.ds(pl.multiple_of(start + which * (width // 2), 128), width // 2)


class Gather:
    steps = 6

    def __init__(self, at, plan, shard, whole, pair, low, sems, local_sems):
        _, start, width, x_first = plan
        self.at, self.shard, self.pair, self.low, self.whole = at, shard, pair, low, whole
        rows = shard.shape[0]
        mine, other = half_of(start, width, at.core), half_of(start, width, 1 - at.core)
        own_rows = pl.ds(pl.multiple_of(rows * at.core, 8), rows)
        place = whole.at[at.seq, at.y, at.x, :, mine]
        along_x, along_y = (whole.at[:, at.y, at.x, :, mine], whole.at[:, at.y, :, :, mine])
        if not x_first:
            along_x, along_y = (whole.at[:, :, at.x, :, mine], along_x)
        self.local = [
            pltpu.make_async_copy(shard.at[:, mine], pair.at[own_rows], local_sems.at[0]),
            pltpu.make_async_copy(low, place, local_sems.at[1]),
        ]
        self.first = send(shard.at[:, other], pair.at[own_rows], sems, 0, at.by_core)
        self.over_z = [send(low, place, sems, 1 + k, at.others[k]) for k in range(3)]
        self.over_x = send(along_x, along_x, sems, 4, at.by_x)
        self.over_y = send(along_y, along_y, sems, 5, at.by_y)
        self.order = [self.over_x, self.over_y] if x_first else [self.over_y, self.over_x]
        self.last = send(whole.at[:, :, :, :, mine], whole.at[:, :, :, :, mine], sems, 6, at.by_core)

    def step(self, number):
        if number == 0:
            self.local[0].start()
            self.first.start()
        elif number == 1:
            self.local[0].wait()
            self.first.wait()
            self.low[...] = self.pair[...].astype(low_type)
            self.local[1].start()
            for copy in self.over_z:
                copy.start()
        elif number == 2:
            self.local[1].wait()
            for copy in self.over_z:
                copy.wait()
            self.order[0].start()
        elif number == 3:
            self.order[0].wait()
            self.order[1].start()
        elif number == 4:
            self.order[1].wait()
            self.last.start()
        else:
            self.last.wait()


class ScatterPlane:
    steps = 5

    def __init__(self, at, plan, term, kept, held, arrived, sems, local_sems):
        _, start, width, self.x_first = plan
        self.at, self.held, self.arrived = at, held, arrived
        mine, other = half_of(start, width, at.core), half_of(start, width, 1 - at.core)
        self.local = [
            pltpu.make_async_copy(term.at[:, :, :, :, mine], held, local_sems.at[0]),
            pltpu.make_async_copy(held.at[:, at.y, at.x], kept, local_sems.at[1]),
        ]
        self.first = send(term.at[:, :, :, :, other], arrived[0], sems, 0, at.by_core)
        if self.x_first:
            self.second = send(held.at[:, :, 1 - at.x], arrived[1], sems, 1, at.by_x)
            self.third = send(held.at[:, 1 - at.y, at.x], arrived[2], sems, 2, at.by_y)
        else:
            self.second = send(held.at[:, 1 - at.y], arrived[1], sems, 1, at.by_y)
            self.third = send(held.at[:, at.y, 1 - at.x], arrived[2], sems, 2, at.by_x)

    def add(self, place, values):
        self.held[place] = self.held[place] + values

    def step(self, number):
        at = self.at
        if number == 0:
            self.local[0].start()
            self.first.start()
        elif number == 1:
            self.local[0].wait()
            self.first.wait()

            @pl.loop(0, 4)
            def _(row):
                for across in range(4):
                    place = (row, across // 2, across % 2)
                    self.add(place, self.arrived[0][place])

            self.second.start()
        elif number == 2:
            self.second.wait()

            @pl.loop(0, 4)
            def _(row):
                for across in range(2):
                    place = (row, across, at.x) if self.x_first else (row, at.y, across)
                    self.add(place, self.arrived[1][row, across])

            self.third.start()
        elif number == 3:
            self.third.wait()

            @pl.loop(0, 4)
            def _(row):
                self.add((row, at.y, at.x), self.arrived[2][row])

            self.local[1].start()
        else:
            self.local[1].wait()


class ScatterLine:
    def __init__(self, at, share_start, kept, share, own, arrived, total, sems, local_sems):
        self.at, self.own, self.arrived, self.total = at, own, arrived, total
        rows, half = total.shape[0] // 2, total.shape[1]
        of_core = lambda which: pl.ds(pl.multiple_of(rows * which, 8), rows)
        mine = half_of(share_start, 2 * half, at.core)
        self.local = [
            pltpu.make_async_copy(kept.at[at.seq], own, local_sems.at[0]),
            pltpu.make_async_copy(
                total.at[of_core(at.core)], share.at[:, mine], local_sems.at[1]
            ),
        ]
        self.over_z = [
            send(kept.at[at.others[k][0]], arrived.at[k], sems, k, at.others[k]) for k in range(3)
        ]
        self.last = send(total.at[of_core(1 - at.core)], share.at[:, mine], sems, 3, at.by_core)

    def step(self, number):
        if number == 0:
            self.local[0].start()
            for copy in self.over_z:
                copy.start()
        elif number == 1:
            self.local[0].wait()
            for copy in self.over_z:
                copy.wait()
            total = self.own[...].astype(f32)
            for k in range(3):
                total = total + self.arrived[k].astype(f32)
            self.total[...] = total
            self.local[1].start()
            self.last.start()
        else:
            self.local[1].wait()
            self.last.wait()


def ring_pieces(rows):
    sixth = rows // 6
    half = pl.ds(0, 3 * sixth)
    return [
        (0, pl.ds(0, 2 * sixth)),
        (0, pl.ds(2 * sixth, 4 * sixth)),
        (1, half),
        (1, pl.ds(3 * sixth, 3 * sixth)),
        (2, half),
        (2, pl.ds(3 * sixth, 2 * sixth)),
        (2, pl.ds(5 * sixth, sixth)),
    ]


class Ring:
    def __init__(self, at, own, blocks, sems, local_sem):
        self.at = at
        seq = at.seq
        self.local = pltpu.make_async_copy(own, blocks.at[seq], local_sem)
        right, left = ((seq + 1) % 4, at.dp), ((seq + 3) % 4, at.dp)
        pieces = ring_pieces(own.shape[0])
        self.hops = []
        for number, (hop, rows) in enumerate(pieces):
            back, ahead = blocks.at[(seq + 4 - hop) % 4, rows], blocks.at[(seq + hop) % 4, rows]
            self.hops.append(
                [
                    (
                        (seq >= hop) & (seq < 3),
                        send(own.at[rows] if hop == 0 else back, back, sems, number, right),
                        seq >= hop + 1,
                    ),
                    (
                        (seq + hop <= 3) & (seq > 0),
                        send(
                            own.at[rows] if hop == 0 else ahead,
                            ahead,
                            sems,
                            len(pieces) + number,
                            left,
                        ),
                        seq + hop + 1 <= 3,
                    ),
                ]
            )

    def start(self, hop):
        if hop == 0:
            self.local.start()
        for sends, copy, _ in self.hops[hop]:
            pl.when(sends)(copy.start)

    def arrive(self, hop):
        for _, copy, receives in self.hops[hop]:
            pl.when(receives)(copy.wait_recv)

    def finish(self):
        for hop in self.hops:
            for sends, copy, _ in hop:
                pl.when(sends)(copy.wait_send)


GATHERS = (
    (0, 0, 1280, True),
    (0, 1280, 1024, False),
    (1, 0, D, False),
    (2, 0, 512, True),
    (2, 512, 2560, False),
    (3, 0, D, True),
)


def opening_kernel(*refs):
    shards, own = refs[:4], refs[4]
    small, lengths = refs[5:8], refs[8]
    wholes, outs = refs[9:13], refs[13:18]
    normed_out, keys_out, values_out, keys_extra_out, picks_out = outs
    queries, queries_t, context_t, log_total, extra = refs[18:23]
    scratch = refs[23:]
    many = len(GATHERS)
    of_gathers, scratch = scratch[: 4 * many], scratch[4 * many :]
    ring_sems, ring_local, out_sems, blocks, project, normed, keys, values_t = scratch[:8]
    keys_extra, picks, sums, tops = scratch[8:12]
    gains, bucket_rows, bias_table, small_sems = scratch[12:]
    loads = [
        pltpu.make_async_copy(source, target, small_sems.at[k])
        for k, (source, target) in enumerate(zip(small, (gains, bucket_rows, bias_table)))
    ]
    for load in loads:
        load.start()
    at = Place()
    at.greet()
    gathers = [
        Gather(
            at,
            plan,
            shards[plan[0]],
            project if plan[0] == 0 else wholes[plan[0]],
            *of_gathers[4 * k : 4 * k + 4],
        )
        for k, plan in enumerate(GATHERS)
    ]
    ring = Ring(at, own, blocks, ring_sems, ring_local.at[0])

    def first_step(number):
        for gather in gathers[:2]:
            gather.step(number)

    def rest_step(number):
        for gather in gathers[2:]:
            gather.step(number)

    ring.start(0)
    first_step(0)
    rest_step(0)
    first_step(1)
    ring.start(1)
    for load in loads:
        load.wait()

    count, buckets = own.shape[0], bias_table.shape[1]
    row_length = keys_extra.shape[0]
    query_blocks = count // BLK
    doc_start, one_start = extra_columns(query_blocks)
    picked = query_blocks * buckets
    ends = []
    for doc in range(DOCS):
        ends.append(lengths[0, doc] + (ends[-1] if ends else 0))

    def documents_at(position):
        return sum((position >= end).astype(jnp.int32) for end in ends)

    bucket_at = lax.broadcasted_iota(jnp.int32, (buckets, row_length), 0)
    for block in range(query_blocks):
        picks[buckets * block : buckets * block + buckets, :] = (
            (bucket_rows[block] == bucket_at).astype(f32).astype(low_type)
        )
    last = picks.shape[0] - picked
    row = lax.broadcasted_iota(jnp.int32, (last, row_length), 0)
    key_doc = documents_at(lax.broadcasted_iota(jnp.int32, (last, row_length), 1))
    picks[picked:, :] = (
        jnp.where(row < DOCS, (key_doc != row).astype(f32), (row == DOCS).astype(f32))
    ).astype(low_type)

    same = lax.broadcasted_iota(jnp.int32, (buckets, buckets), 0) == lax.broadcasted_iota(
        jnp.int32, (buckets, buckets), 1
    )
    lane = lax.broadcasted_iota(jnp.int32, (picked, 128), 1)
    lane_block = lax.broadcasted_iota(jnp.int32, (picked, 128), 0) // buckets
    lane_last = lax.broadcasted_iota(jnp.int32, (last, 128), 1)
    row_last = lax.broadcasted_iota(jnp.int32, (last, 128), 0)
    below = jnp.where(
        (row_last < DOCS) & (lane_last - doc_start == row_last),
        masked_score,
        jnp.where(
            (row_last == DOCS) & (lane_last >= one_start) & (lane_last < one_start + TERMS), 1.0, 0.0
        ),
    ).astype(low_type)

    first_step(2)
    rest_step(1)

    def make_extra(pair):
        sides = []
        for head in range(2):
            of_head = jnp.broadcast_to(bias_table[pl.ds(2 * pair + head, 1), :], same.shape)
            of_head = jnp.sum(jnp.where(same, of_head, 0.0), axis=1, keepdims=True)
            rest_of = jnp.concatenate([of_head] * query_blocks, axis=0)
            side = jnp.zeros((picked, 128), f32)
            for term in range(TERMS):
                part = rest_of.astype(low_type).astype(f32)
                rest_of = rest_of - part
                side = jnp.where(lane == term * query_blocks + lane_block, part, side)
            sides.append(jnp.concatenate([side.astype(low_type), below], axis=0))
        keys_extra[:, pl.ds(pl.multiple_of(256 * pair, 256), 256)] = dot(
            picks[...], jnp.concatenate(sides, axis=1), 0, 0
        ).astype(low_type)

    pl.loop(0, PAIRS // 2)(make_extra)
    first_step(3)
    pl.loop(PAIRS // 2, PAIRS)(make_extra)
    first_step(4)
    extra_lane = lax.broadcasted_iota(jnp.int32, (count, 128), 1)
    extra_row = lax.broadcasted_iota(jnp.int32, (count, 128), 0)
    query_doc = documents_at(extra_row + at.seq * count)
    extra[...] = (
        (
            ((extra_lane < doc_start) & (extra_lane % query_blocks == extra_row // BLK))
            | ((extra_lane < one_start) & (extra_lane - doc_start == query_doc))
        )
        .astype(f32)
        .astype(low_type)
    )
    sums[...] = jnp.zeros_like(sums)
    tops[...] = jnp.full_like(tops, masked_score)
    ring.local.wait()
    first_step(5)

    copies = [pltpu.make_async_copy(project, wholes[0], out_sems.at[0])]
    for block in range(4):
        columns = pl.ds(count * block, count)
        into = pl.ds(pl.multiple_of(count * at.turn(block), count), count)
        copies += [
            pltpu.make_async_copy(
                keys_extra.at[columns], keys_extra_out.at[into], out_sems.at[1 + block]
            ),
            pltpu.make_async_copy(
                picks.at[:, columns], picks_out.at[:, into], out_sems.at[5 + block]
            ),
        ]
    for copy in copies:
        copy.start()
    weights = [project[:, :, :, :, D * part : D * part + D].reshape(D, D) for part in range(3)]
    pair_lane = lax.broadcasted_iota(jnp.int32, (count, PAIR), 1)

    def attend_pair(block, rows, pair):
        lanes = pl.ds(pl.multiple_of(pair * PAIR, PAIR), PAIR)
        start = block * count + rows.start
        key_rows = pl.ds(pl.multiple_of(start, BLK), rows.size)
        query_pair, key_pair = queries[:, lanes], keys[block, rows, lanes]
        for head in range(2):
            which = 2 * pair + head
            mine = (pair_lane < HEAD) if head == 0 else (pair_lane >= HEAD)
            query_side = jnp.concatenate(
                [jnp.where(mine, query_pair, jnp.zeros_like(query_pair)), extra[...]], axis=1
            )
            more = keys_extra[key_rows, pl.ds(pl.multiple_of(128 * which, 128), 128)]
            scores = dot(jnp.concatenate([key_pair, more], axis=1), query_side, 1, 1)
            top_before = tops[which, 0:1]
            top = jnp.maximum(top_before, jnp.max(scores, axis=0, keepdims=True))
            unscaled = jnp.exp(scores - top).astype(low_type)
            value_side = jnp.concatenate(
                [
                    values_t[block, pl.ds(pl.multiple_of(HEAD * which, HEAD), HEAD), rows],
                    jnp.ones((16, rows.size), low_type),
                ],
                axis=0,
            )
            sums[which] = sums[which] * jnp.exp(top_before - top) + dot(value_side, unscaled, 1, 0)
            tops[which] = jnp.broadcast_to(top, (8, count))

    side = at.seq // 2
    order = [at.seq, 1 - at.seq + 4 * side, 2 - side, 3 - 3 * side]
    whole_block = pl.ds(0, count)
    passes = [(block, whole_block) for block in order[:2]]
    passes += [(order[hop + 1], rows) for hop, rows in ring_pieces(count)[2:]]
    events = {
        (0, 0): [lambda: (ring.arrive(0), ring.arrive(1), ring.start(2), ring.start(3))],
        (1, 0): [lambda: rest_step(2)],
        (1, 5): [lambda: (rest_step(3), ring.arrive(2), ring.start(4))],
        (2, 5): [lambda: (ring.arrive(3), ring.start(5), ring.start(6))],
        (3, 5): [lambda: ring.arrive(4)],
        (4, 5): [lambda: (ring.arrive(5), rest_step(4))],
        (5, 5): [lambda: ring.arrive(6)],
    }
    for number, (block, rows) in enumerate(passes):
        values = blocks[block, rows].astype(f32)
        normed_low = (
            values
            * lax.rsqrt(jnp.mean(values * values, axis=1, keepdims=True) + norm_epsilon)
            * gains[0:1, :]
        ).astype(low_type)
        normed[block, rows] = normed_low
        keys[block, rows] = dot(normed_low, weights[1], 1, 0).astype(low_type)
        values_t[block, :, rows] = dot(weights[2], normed_low, 0, 1).astype(low_type)
        turn = at.turn(block)
        for place, (source, target, index) in enumerate(
            (
                (normed, normed_out, (rows,)),
                (keys, keys_out, (rows,)),
                (values_t, values_out, (slice(None), rows)),
            )
        ):
            copy = pltpu.make_async_copy(
                source.at[(block, *index)],
                target.at[(turn, *index)],
                out_sems.at[9 + 3 * number + place],
            )
            copy.start()
            copies.append(copy)
        if number == 0:
            scaled = lambda values: (values.astype(low_type).astype(f32) * score_scale).astype(low_type)
            queries[...] = scaled(dot(normed_low, weights[0], 1, 0))
            queries_t[...] = scaled(dot(weights[0], normed_low, 0, 1))

        @pl.loop(0, PAIRS)
        def _(pair, number=number, block=block, rows=rows):
            for (when, which), actions in events.items():
                if when == number:

                    @pl.when(pair == which)
                    def _(actions=actions):
                        for action in actions:
                            action()

            attend_pair(block, rows, pair)

    for head in range(HEADS):
        total = sums[head, HEAD : HEAD + 1]
        context_t[HEAD * head : HEAD * head + HEAD, :] = sums[head, :HEAD] * (1.0 / total)
        log_total[head : head + 1, :] = tops[head, 0:1] + jnp.log(total)
    rest_step(5)
    ring.finish()
    for copy in copies:
        copy.wait()


def open_layer(shards, own, gains, bucket_rows, bias_table, lengths):
    shards = [pltpu.with_memory_space_constraint(shard, pltpu.HBM) for shard in shards]
    own, gains, bucket_rows, bias_table, lengths = (
        pltpu.with_memory_space_constraint(array, pltpu.HBM)
        for array in (own, gains, jnp.transpose(bucket_rows, (1, 0, 2)), bias_table.T, lengths)
    )
    anywhere = pl.BlockSpec(memory_space=pl.ANY)
    in_place = pl.BlockSpec(memory_space=pltpu.VMEM)
    count, blocks = own.shape[0], bucket_rows.shape[0]
    row_length = 4 * count
    picked = blocks * bias_table.shape[1] + 16
    low = lambda *shape: pltpu.HBM(shape, low_type)
    whole_shapes = [(4, 2, 2, 2 * shard.shape[0], shard.shape[1]) for shard in shards]
    of_gathers = []
    for which, _, width, _ in GATHERS:
        half = (2 * shards[which].shape[0], width // 2)
        of_gathers += [
            pltpu.VMEM(half, f32),
            pltpu.VMEM(half, low_type),
            pltpu.SemaphoreType.DMA((2, 7)),
            pltpu.SemaphoreType.DMA((2,)),
        ]
    return pl.pallas_call(
        opening_kernel,
        out_shape=[low(*shape) for shape in whole_shapes]
        + [low(4, count, D)] * 2
        + [low(4, D, count), low(row_length, HEADS * 128), low(picked, row_length)]
        + [low(count, D), low(D, count)]
        + [jax.ShapeDtypeStruct((D, count), f32), jax.ShapeDtypeStruct((16, count), f32)]
        + [low(count, 128)],
        in_specs=[anywhere] * 8 + [pl.BlockSpec(memory_space=pltpu.SMEM)],
        out_specs=[anywhere] * 9 + [in_place] * 5,
        scratch_shapes=of_gathers
        + [
            pltpu.SemaphoreType.DMA((2, 14)),
            pltpu.SemaphoreType.DMA((1,)),
            pltpu.SemaphoreType.DMA((30,)),
            pltpu.VMEM((4, count, D), low_type),
            pltpu.VMEM(whole_shapes[0], low_type),
            pltpu.VMEM((4, count, D), low_type),
            pltpu.VMEM((4, count, D), low_type),
            pltpu.VMEM((4, D, count), low_type),
            pltpu.VMEM((row_length, HEADS * 128), low_type),
            pltpu.VMEM((picked, row_length), low_type),
            pltpu.VMEM((HEADS, HEAD + 16, count), f32),
            pltpu.VMEM((HEADS, 8, count), f32),
            pltpu.VMEM(gains.shape, f32),
            pltpu.VMEM(bucket_rows.shape, jnp.int32),
            pltpu.VMEM(bias_table.shape, f32),
            pltpu.SemaphoreType.DMA((3,)),
        ],
        compiler_params=pltpu.CompilerParams(
            collective_id=0, has_side_effects=True, vmem_limit_bytes=open_vmem
        ),
        name="open_layer",
    )(*shards, own, gains, bucket_rows, bias_table, lengths)


def plane_scratch(rows, width):
    half = width // 2
    return [
        pltpu.VMEM((4, 2, 2, rows, half), low_type),
        pltpu.VMEM((4, 2, 2, rows, half), low_type),
        pltpu.VMEM((4, 2, rows, half), low_type),
        pltpu.VMEM((4, rows, half), low_type),
        pltpu.SemaphoreType.DMA((2, 3)),
        pltpu.SemaphoreType.DMA((2,)),
    ]


def line_scratch(rows, width):
    half = width // 2
    return [
        pltpu.VMEM((rows, half), low_type),
        pltpu.VMEM((3, rows, half), low_type),
        pltpu.VMEM((rows, half), f32),
        pltpu.SemaphoreType.DMA((2, 4)),
        pltpu.SemaphoreType.DMA((2,)),
    ]


def take_plane(at, plan, term, kept, scratch):
    return ScatterPlane(at, plan, term, kept, scratch[0], scratch[1:4], scratch[4], scratch[5])


def by_chip(term):
    return term.reshape(4, 2, 2, term.shape[0] // 16, term.shape[1])


class AllSum:
    def __init__(self, at, own, plane, line, sems):
        self.at, self.own, self.plane, self.line = at, own, plane, line
        self.local = pltpu.make_async_copy(own, plane.at[at.dp], sems.at[0, 10])
        self.beside = [
            send(own, plane.at[at.dp], sems, k, partner) for k, partner in enumerate(at.plane)
        ]
        place = line.at[at.seq]
        self.over_z = [
            send(place, place, sems, 7 + k, partner) for k, partner in enumerate(at.others)
        ]

    def step(self, number):
        if number == 0:
            self.local.start()
            for copy in self.beside:
                copy.start()
        elif number == 1:
            self.local.wait()
            for copy in self.beside:
                copy.wait()
            total = self.plane[0]
            for k in range(1, 8):
                total = total + self.plane[k]
            self.line[self.at.seq] = total
            for copy in self.over_z:
                copy.start()
        else:
            for copy in self.over_z:
                copy.wait()

    def total(self):
        return (self.line[0] + self.line[1]) + (self.line[2] + self.line[3])


def sum_scratch(width):
    return [
        pltpu.VMEM((8, width), f32),
        pltpu.VMEM((8, 8, width), f32),
        pltpu.VMEM((4, 8, width), f32),
        pltpu.SemaphoreType.DMA((2, 11)),
    ]


EARLY_WIDTH, LATE_WIDTH = D + 512, D
CLOSE_PLANS = ((2, 0, D, True), (1, 0, D, False), (0, 0, D, True))


def split_low(values):
    terms = []
    for _ in range(TERMS):
        terms.append(values.astype(low_type))
        values = values - terms[-1].astype(f32)
    return terms


def close_kernel(scale, *refs):
    normed, key_grad_t, value_grad_t, query_grad, project, key_part_t = refs[:6]
    inputs, residual_grad, folded, picks, gains, gain_two = refs[6:12]
    kept_rest, rows_before, refs = refs[12:17], refs[17:21], refs[21:]
    input_grad, shares, early_total, late_total = refs[0], refs[1:5], refs[5], refs[6]
    scratch = refs[7:]
    normed_in, key_in, value_in, weight_in, part_in, residual_in, near, load_sems = scratch[:8]
    early, late, scratch = scratch[8:12], scratch[12:16], scratch[16:]
    terms, kept, scratch = scratch[:3], scratch[3:6], scratch[6:]
    at = Place()
    chip_rows, half = near.shape[1], near.shape[2]
    chip_start = (at.seq * 4 + at.dp // 2) * chip_rows
    loads = [
        pltpu.make_async_copy(source, target, load_sems.at[k])
        for k, (source, target) in enumerate(
            (
                (normed.at[3], normed_in.at[3]),
                (value_grad_t, value_in),
                (normed.at[pl.ds(0, 3)], normed_in.at[pl.ds(0, 3)]),
                (key_grad_t, key_in),
                (project.at[:, 0:D], weight_in),
                (key_part_t, part_in),
                (residual_grad, residual_in),
                *(
                    (
                        project.at[
                            pl.ds(pl.multiple_of(chip_start, 16), chip_rows),
                            half_of(D * plan[0], D, at.core),
                        ],
                        near.at[k],
                    )
                    for k, plan in enumerate(CLOSE_PLANS)
                ),
            )
        )
    ]
    for load in loads:
        load.start()
    at.greet(whole_plane=True)
    planes, lines = [], []
    for k, plan in enumerate(CLOSE_PLANS):
        planes.append(take_plane(at, plan, terms[k], kept[k], scratch[:6]))
        lines.append(ScatterLine(at, D * plan[0], kept[k], shares[0], *scratch[6:11]))
        scratch = scratch[11:]
    rest_lines = []
    for k, (which, start, _, _) in enumerate(BACK_PLANS):
        rest_lines.append(
            ScatterLine(at, start, kept_rest[k], shares[which + 1], *scratch[5 * k : 5 * k + 5])
        )
    first, second = AllSum(at, *early), AllSum(at, *late)

    for line in rest_lines:
        line.step(0)
    early_own, late_own = early[0], late[0]
    early_own[...] = jnp.zeros_like(early_own)
    late_own[...] = jnp.zeros_like(late_own)
    count = inputs.shape[0]
    query_low = (query_grad[...] * score_scale).astype(low_type)

    def put(term, values):
        term[...] = values.astype(low_type).reshape(term.shape)

    def of_row(parts):
        whole = normed_in[...].reshape(4 * count, D)
        return dot(parts[...], whole, 1, 0).astype(low_type).T

    loads[0].wait()
    put(terms[2], dot(normed_in[3], query_low, 0, 0))
    planes[2].step(0)
    loads[1].wait()
    loads[2].wait()
    put(terms[0], of_row(value_in))
    planes[0].step(0)
    planes[2].step(1)
    loads[3].wait()
    put(terms[1], of_row(key_in))
    planes[1].step(0)
    planes[2].step(2)
    planes[0].step(1)

    for load in loads[4:]:
        load.wait()
    scaled = (dot(query_low, weight_in[...], 1, 1) + part_in[...].T) * gains[0:1, :]
    planes[1].step(1)
    planes[0].step(2)
    planes[2].step(3)
    planes[2].step(4)
    lines[2].step(0)
    source = inputs[...].astype(f32)
    inverse = lax.rsqrt(jnp.mean(source * source, axis=1, keepdims=True) + norm_epsilon)
    along = jnp.mean(source * scaled, axis=1, keepdims=True)
    input_grad[...] = (
        residual_in[...] + inverse * scaled - source * (inverse * inverse * inverse * along)
    ).astype(low_type)
    planes[1].step(2)
    planes[0].step(3)
    planes[0].step(4)
    lines[0].step(0)

    blocks = query_blocks_of(picks.shape[0])
    buckets = (picks.shape[0] - 16) // blocks
    rows = folded.shape[0] * folded.shape[1]
    flat = split_low(folded[...].reshape(rows, folded.shape[2]))
    parted = dot(jnp.concatenate(flat, axis=0), picks[: blocks * buckets, :], 1, 1)
    parted = parted[:rows] + parted[rows : 2 * rows] + parted[2 * rows :]
    row = lax.broadcasted_iota(jnp.int32, parted.shape, 0) % folded.shape[1]
    lane = lax.broadcasted_iota(jnp.int32, parted.shape, 1)
    parted = jnp.where(row == lane // buckets, parted, 0.0)
    at_bucket = (
        lax.broadcasted_iota(jnp.int32, (blocks * buckets, buckets), 0) % buckets
        == lax.broadcasted_iota(jnp.int32, (blocks * buckets, buckets), 1)
    )
    at_bucket = at_bucket.astype(f32).astype(low_type)
    table = sum(dot(term, at_bucket, 1, 0) for term in split_low(parted))
    table = jnp.sum(table.reshape(HEADS, folded.shape[1], buckets), axis=1)
    early_own[:, D + 256 : D + 256 + buckets] = table[:8]
    early_own[0 : HEADS - 8, D + 384 : D + 384 + buckets] = table[8:]
    early_own[2:3, :D] = gain_two[...]

    planes[1].step(3)
    planes[1].step(4)
    lines[1].step(0)
    for line in rest_lines:
        line.step(1)

    def statistics(raw, previous):
        gradient = raw * scale
        squares = gradient * gradient + tiny_term
        means = jnp.sum(jnp.mean(squares, axis=1, keepdims=True), axis=0, keepdims=True)
        before = jnp.sum(previous.reshape(1, previous.shape[0]), axis=1, keepdims=True)
        row_sum = decay_rate * before + (1.0 - decay_rate) * means
        return jnp.sum(squares, axis=0, keepdims=True), jnp.broadcast_to(row_sum, (1, 128))

    lines[2].step(1)
    lines[0].step(1)
    for line in rest_lines:
        line.step(2)
    for position in (1, 2, 3):
        columns, row_sum = statistics(shares[position][...], rows_before[position][...])
        early_own[position : position + 1, D : D + 128] = row_sum
        if position == 2:
            for part in range(4):
                early_own[4 + part : 5 + part, :D] = columns[:, D * part : D * part + D]
        else:
            early_own[position // 2 : position // 2 + 1, :D] = columns
    first.step(0)
    lines[1].step(1)

    lane = lax.broadcasted_iota(jnp.int32, (chip_rows, D), 1)
    row = lax.broadcasted_iota(jnp.int32, (chip_rows, D), 0)
    before = jnp.sum(rows_before[0][...].reshape(1, rows_before[0].shape[0]), axis=1, keepdims=True)
    row_sum = decay_rate * before
    gain_one = jnp.zeros((chip_rows, 1), f32)
    for k, (part, _, _, _) in enumerate(CLOSE_PLANS):
        raw = lines[k].total[...]
        gradient = raw * scale
        columns = jnp.sum(gradient * gradient + tiny_term, axis=0, keepdims=True)
        late_own[part : part + 1, half_of(0, D, at.core)] = columns
        row_sum = row_sum + (1.0 - decay_rate) * (
            jnp.sum(columns, axis=1, keepdims=True) / (3 * D)
        )
        gain_one = gain_one + jnp.sum(raw * near[k].astype(f32), axis=1, keepdims=True)
    late_own[4:5, :128] = jnp.broadcast_to(row_sum, (1, 128))
    spread = jnp.where(
        lane == row + chip_start, jnp.broadcast_to(gain_one, (chip_rows, D)), 0.0
    )
    late_own[3:4, :] = jnp.sum(spread, axis=0, keepdims=True) / gains[0:1, :]
    second.step(0)
    first.step(1)
    for line in lines:
        line.step(2)
    first.step(2)
    early_total[...] = first.total()
    second.step(1)
    second.step(2)
    late_total[...] = second.total()


def query_blocks_of(rows):
    return (rows - 16) // 32


def close(scale, large, small, kept_rest, rows_before, weight_shapes):
    in_place = pl.BlockSpec(memory_space=pltpu.VMEM)
    anywhere = pl.BlockSpec(memory_space=pl.ANY)
    count, row_length = small[0].shape[0], large[1].shape[1]
    scratch = [
        pltpu.VMEM((4, count, D), low_type),
        pltpu.VMEM((D, row_length), low_type),
        pltpu.VMEM((D, row_length), low_type),
        pltpu.VMEM((D, D), low_type),
        pltpu.VMEM((D, count), f32),
        pltpu.VMEM((count, D), f32),
        pltpu.VMEM((3, D // 16, D // 2), low_type),
        pltpu.SemaphoreType.DMA((10,)),
    ]
    scratch += sum_scratch(EARLY_WIDTH) + sum_scratch(LATE_WIDTH)
    scratch += [pltpu.VMEM((4, 2, 2, D // 16, D), low_type)] * 3
    scratch += [pltpu.VMEM((4, D // 16, D // 2), low_type)] * 3
    for _ in CLOSE_PLANS:
        scratch += plane_scratch(D // 16, D) + line_scratch(D // 16, D)
    for which, _, width, _ in BACK_PLANS:
        scratch += line_scratch(2 * weight_shapes[which + 1][0], width)
    return pl.pallas_call(
        functools.partial(close_kernel, scale),
        out_shape=[jax.ShapeDtypeStruct((count, D), low_type)]
        + [jax.ShapeDtypeStruct(shape, f32) for shape in weight_shapes]
        + [
            jax.ShapeDtypeStruct((8, EARLY_WIDTH), f32),
            jax.ShapeDtypeStruct((8, LATE_WIDTH), f32),
        ],
        in_specs=[anywhere] * 3
        + [in_place]
        + [anywhere] * 2
        + [in_place, anywhere]
        + [in_place] * 4
        + [anywhere] * 5
        + [in_place] * 4,
        out_specs=[in_place] * 7,
        scratch_shapes=scratch,
        compiler_params=pltpu.CompilerParams(
            collective_id=2, has_side_effects=True, vmem_limit_bytes=close_vmem
        ),
        name="close_layer",
    )(*large, *small, *kept_rest, *rows_before)


def apply_kernel(scale, *refs):
    shares, early, late, far, refs = refs[:4], refs[4], refs[5], refs[6:22], refs[22:]
    near, load_sems = refs[22:38], refs[38]
    loads = [
        pltpu.make_async_copy(source, target, load_sems.at[k])
        for k, (source, target) in enumerate(zip(far, near))
    ]
    for load in loads:
        load.start()
    for load in loads:
        load.wait()
    weights, rows_before, columns_before = near[:4], near[4:8], near[8:12]
    gains, gains_moment, table, table_moment = near[12:]
    gradients, updated, rows_after, columns_after = refs[:4], refs[4:8], refs[8:12], refs[12:16]
    gains_out, table_out = refs[16:19], refs[19:22]
    early_sums, late_sums = early[...], late[...]
    sums = [
        jnp.concatenate([late_sums[part : part + 1] for part in range(3)], axis=1),
        early_sums[0:1, :D],
        jnp.concatenate([early_sums[4 + part : 5 + part, :D] for part in range(4)], axis=1),
        early_sums[1:2, :D],
    ]
    row_sums = [late_sums[4:5, 0:1]] + [early_sums[k : k + 1, D : D + 1] for k in (1, 2, 3)]
    for position in range(4):
        rows, width = shares[position].shape
        full = rows * 32
        gradient = shares[position][...] * scale
        gradients[position][...] = gradient
        squares = gradient * gradient + tiny_term
        eye = lax.broadcasted_iota(jnp.int32, (rows, rows), 0) == lax.broadcasted_iota(
            jnp.int32, (rows, rows), 1
        )
        before = jnp.broadcast_to(rows_before[position][...].reshape(1, rows), (rows, rows))
        before = jnp.sum(jnp.where(eye, before, 0.0), axis=1, keepdims=True)
        rows_new = decay_rate * before + (1.0 - decay_rate) * jnp.mean(
            squares, axis=1, keepdims=True
        )
        rows_after[position][...] = jnp.sum(
            jnp.where(eye, jnp.broadcast_to(rows_new, (rows, rows)), 0.0), axis=0, keepdims=True
        ).reshape(rows)
        columns_new = decay_rate * columns_before[position][...].reshape(1, width) + (
            1.0 - decay_rate
        ) * (sums[position] / full)
        columns_after[position][...] = columns_new.reshape(width)
        denominator = rows_new * columns_new / (row_sums[position] / full)
        updated[position][...] = weights[position][...] - learn_rate * gradient * lax.rsqrt(
            denominator
        )

    def moments(gradient, old, moment, results):
        moment_new = decay_rate * moment[...] + (1.0 - decay_rate) * (
            gradient * gradient + tiny_term
        )
        results[0][...] = gradient
        results[1][...] = old[...] - learn_rate * gradient * lax.rsqrt(moment_new)
        results[2][...] = moment_new

    moments(
        jnp.concatenate([late_sums[3:4, :D], early_sums[2:3, :D]], axis=0) * scale,
        gains,
        gains_moment,
        gains_out,
    )
    buckets = table.shape[1]
    of_table = jnp.concatenate(
        [
            early_sums[:, D + 256 : D + 256 + buckets],
            early_sums[0 : HEADS - 8, D + 384 : D + 384 + buckets],
        ],
        axis=0,
    )
    moments(of_table * scale, table, table_moment, table_out)


def apply_updates(scale, shares, sums, weights, rows_before, columns_before, rest):
    in_place = pl.BlockSpec(memory_space=pltpu.VMEM)
    same = lambda arrays: [jax.ShapeDtypeStruct(array.shape, f32) for array in arrays]
    gains, table = rest[0], rest[2]
    far = [*weights, *rows_before, *columns_before, *rest]
    far = [pltpu.with_memory_space_constraint(array, pltpu.HBM) for array in far]
    return pl.pallas_call(
        functools.partial(apply_kernel, scale),
        out_shape=same(weights)
        + same(weights)
        + same(rows_before)
        + same(columns_before)
        + same([gains] * 3)
        + same([table] * 3),
        in_specs=[in_place] * 6 + [pl.BlockSpec(memory_space=pl.ANY)] * 16,
        out_specs=[in_place] * 22,
        scratch_shapes=[pltpu.VMEM(array.shape, f32) for array in far]
        + [pltpu.SemaphoreType.DMA((16,))],
        compiler_params=pltpu.CompilerParams(vmem_limit_bytes=apply_vmem),
        name="apply_updates",
    )(*shares, *sums, *far)


def middle_kernel(
    context_t,
    log_total,
    inputs,
    upstream,
    gains,
    output_weight,
    expand_weight,
    reduce_weight,
    layer_output,
    residual_grad,
    output_term,
    expand_term,
    reduce_term,
    context_grad,
    context_grad_t,
    row_columns,
    gain_two,
    residual,
    normed,
    normed_t,
    reduced,
    normed_grad,
):
    step = pl.program_id(0)
    gain = gains[1:2, :]

    def inverse():
        values = residual[...]
        return lax.rsqrt(jnp.mean(values * values, axis=1, keepdims=True) + norm_epsilon)

    @pl.when(step == 0)
    def _():
        residual[...] = inputs[...].astype(f32) + dot(
            context_t[...].astype(low_type), output_weight[...], 0, 0
        )
        normed_low = (residual[...] * inverse() * gain).astype(low_type)
        normed[...] = normed_low
        normed_t[...] = normed_low.T
        reduced[...] = jnp.zeros_like(reduced)
        normed_grad[...] = jnp.zeros_like(normed_grad)

    expanded = dot(normed[...], expand_weight[...], 1, 0)
    squared = expanded * expanded
    bent = jnp.tanh(0.7978845608028654 * expanded * (1.0 + 0.044715 * squared))
    above = 0.5 * (1.0 + bent)
    activated = (expanded * above).astype(low_type)
    slope = above + 0.5 * expanded * (1.0 - bent * bent) * (
        0.7978845608028654 * (1.0 + 3.0 * 0.044715 * squared)
    )
    expanded_low = (dot(upstream[...], reduce_weight[...], 1, 1) * slope).astype(low_type)
    reduced[...] += dot(activated, reduce_weight[...], 1, 0)
    reduce_term[...] = dot(activated, upstream[...], 0, 0).astype(low_type)
    normed_grad[...] += dot(expanded_low, expand_weight[...], 1, 1)
    expand_term[...] = dot(normed_t[...], expanded_low, 1, 0).astype(low_type)

    @pl.when(step == pl.num_programs(0) - 1)
    def _():
        values, scale = residual[...], inverse()
        layer_output[...] = (values + reduced[...]).astype(low_type)
        gain_two[...] = jnp.sum(normed_grad[...] * values * scale, axis=0, keepdims=True)
        scaled = normed_grad[...] * gain
        along = jnp.mean(values * scaled, axis=1, keepdims=True)
        gradient = (
            upstream[...].astype(f32)
            + scale * scaled
            - values * (scale * scale * scale * along)
        )
        residual_grad[...] = gradient
        low = gradient.astype(low_type)
        output_term[...] = dot(context_t[...].astype(low_type), low, 1, 0).astype(low_type)
        context_grad[...] = dot(low, output_weight[...], 1, 1).astype(low_type)
        turned = dot(output_weight[...], low, 1, 1).astype(low_type)
        context_grad_t[...] = turned
        count = low.shape[0]
        delta = jnp.sum(
            (turned.astype(f32) * context_t[...]).reshape(HEADS, HEAD, count), axis=1
        )
        rows = jnp.concatenate(
            [log_total[0:HEADS, :], delta, jnp.zeros((128 - 2 * HEADS, count), f32)], axis=0
        )
        row_columns[...] = rows.T


def middle(context_t, log_total, inputs, upstream, gains, output_weight, expand_weight, reduce_weight):
    count = inputs.shape[0]
    hidden = expand_weight.shape[1]
    still = lambda *shape: pl.BlockSpec(shape, lambda step: (0,) * len(shape))
    low = lambda *shape: pltpu.HBM(shape, low_type)
    across = pl.BlockSpec((D, D), lambda step: (0, step))
    down = pl.BlockSpec((D, D), lambda step: (step, 0))
    return pl.pallas_call(
        middle_kernel,
        grid=(hidden // D,),
        out_shape=[
            low(count, D),
            pltpu.HBM((count, D), f32),
            low(D, D),
            low(D, hidden),
            low(hidden, D),
            low(count, D),
            low(D, count),
            jax.ShapeDtypeStruct((count, 128), f32),
            jax.ShapeDtypeStruct((1, D), f32),
        ],
        in_specs=[
            still(D, count),
            still(*log_total.shape),
            still(count, D),
            still(count, D),
            still(2, D),
            still(D, D),
            across,
            down,
        ],
        out_specs=[
            still(count, D),
            still(count, D),
            still(D, D),
            across,
            down,
            still(count, D),
            still(D, count),
            still(count, 128),
            still(1, D),
        ],
        scratch_shapes=[
            pltpu.VMEM((count, D), f32),
            pltpu.VMEM((count, D), low_type),
            pltpu.VMEM((D, count), low_type),
            pltpu.VMEM((count, D), f32),
            pltpu.VMEM((count, D), f32),
        ],
        compiler_params=pltpu.CompilerParams(vmem_limit_bytes=middle_vmem),
        cost_estimate=pl.CostEstimate(
            flops=2 * count * D * (6 * hidden + 4 * D),
            bytes_accessed=8 * D * hidden + 20 * count * D,
            transcendentals=count * hidden,
        ),
        name="middle",
    )(
        context_t,
        log_total,
        *in_hbm(inputs, upstream, gains, output_weight, expand_weight, reduce_weight),
    )


BACK_PLANS = (
    (1, 0, 2 * D, False),
    (2, 0, 512, True),
    (1, 2 * D, 2 * D, False),
    (2, 512, 256, True),
    (0, 0, D, True),
)
EARLY, LATE = (0, 1), (2, 3, 4)
BACK_TIMES = (
    (0, None),
    (0, (EARLY, 0)),
    (1, (LATE, 0)),
    (2, (EARLY, 1)),
    (7, (EARLY, 2)),
    (7, (LATE, 1)),
    (11, (EARLY, 3)),
    (13, (LATE, 2)),
    (17, (LATE, 3)),
    (23, (EARLY, 4)),
    (23, (LATE, 4)),
)


class Relay:
    def __init__(self, at, kept, arrived, sems):
        self.kept, self.arrived = kept, arrived
        seq = at.seq
        self.is_end = (seq == 0) | (seq == 3)
        self.is_inner = (seq == 1) | (seq == 2)
        inwards = (1 + seq // 3, at.dp)
        outwards = ((3 * seq + 1) % 4, at.dp)
        across = ((7 - seq) % 4, at.dp)
        half = kept.shape[2] // 2
        self.halves = [pl.ds(0, half), pl.ds(half, half)]

        def by_half(source, target, index, partner):
            return [
                send(kept.at[source, :, rows], arrived.at[target, :, rows], sems, 2 * index + k, partner)
                for k, rows in enumerate(self.halves)
            ]

        self.from_end = [by_half(k, k, k, inwards) for k in range(3)]
        self.to_peer = [by_half(1, 3, 3, across), by_half(0, 4, 4, across)]
        self.to_end = by_half(2, 0, 5, outwards)

    def turn(self, number, part, total):
        kept, arrived = self.kept, self.arrived
        low = lambda values: values.astype(low_type)
        wide = lambda ref, k, rows: ref[k, :, rows].astype(f32)
        of = lambda rows: part[:, rows.start : rows.start + rows.size]
        halves = list(enumerate(self.halves))
        if number < 3:

            @pl.when(self.is_end)
            def _():
                for k, rows in halves:
                    kept[number, :, rows] = low(of(rows))
                    self.from_end[number][k].start()

        if number == 0:

            @pl.when(self.is_inner)
            def _():
                kept[0] = low(part)

        elif number == 1:

            @pl.when(self.is_inner)
            def _():
                for k, rows in halves:
                    self.from_end[0][k].wait_recv()
                    kept[1, :, rows] = low(of(rows) + wide(arrived, 0, rows))
                    self.to_peer[0][k].start()

        elif number == 2:

            @pl.when(self.is_inner)
            def _():
                for k, rows in halves:
                    self.to_peer[0][k].wait_recv()
                    kept[2, :, rows] = low(of(rows) + wide(arrived, 3, rows))
                    self.to_end[k].start()
                    self.from_end[1][k].wait_recv()
                    kept[0, :, rows] = low(wide(kept, 0, rows) + wide(arrived, 1, rows))
                    self.to_peer[1][k].start()

        else:

            @pl.when(self.is_end)
            def _():
                for k, rows in halves:
                    self.to_end[k].wait_recv()
                    total[:, rows] = of(rows) + wide(arrived, 0, rows)
                    for copies in self.from_end:
                        copies[k].wait_send()

            @pl.when(self.is_inner)
            def _():
                for k, rows in halves:
                    self.to_peer[1][k].wait_recv()
                    self.from_end[2][k].wait_recv()
                    total[:, rows] = of(rows) + wide(arrived, 2, rows) + wide(arrived, 4, rows)
                    for copies in self.to_peer + [self.to_end]:
                        copies[k].wait_send()


def backward_kernel(
    queries,
    extra,
    row_columns,
    context_grad,
    queries_t,
    context_grad_t,
    keys,
    values_t,
    keys_extra,
    *refs,
):
    turn, pair = pl.program_id(0), pl.program_id(1)
    remote = len(refs) > 4
    if remote:
        key_weight, value_weight, terms, refs = refs[0], refs[1], refs[2:5], refs[5:]
        total, kept_rest, scratch = refs[4], refs[5:10], refs[10:]
        parts, kept, arrived, relay_sems = scratch[:4]
        at = Place()
        relay = Relay(at, kept, arrived, relay_sems)
        scatters = [
            take_plane(at, plan, terms[plan[0]], kept_rest[k], scratch[4 + 6 * k : 10 + 6 * k])
            for k, plan in enumerate(BACK_PLANS)
        ]
        now = turn * PAIRS + pair
        for when, doing in BACK_TIMES:

            @pl.when(now == when)
            def _(doing=doing):
                if doing is None:
                    at.greet()
                else:
                    for which in doing[0]:
                        scatters[which].step(doing[1])

    query_grad, key_grad_t, value_grad_t, folded = refs[:4]
    count = queries.shape[0]
    lane = lax.broadcasted_iota(jnp.int32, (count, PAIR), 1)
    query_pair, grad_pair = queries[...], context_grad[...]
    zeros = jnp.zeros_like(query_pair)
    lanes = pl.ds(pl.multiple_of(PAIR * pair, PAIR), PAIR)
    columns = pltpu.roll(row_columns[...], (128 - 2 * pair) % 128, 1)

    @pl.when(turn == 0)
    def _():
        query_grad[:, lanes] = jnp.zeros((count, PAIR), f32)

    query_grads = []
    for head in range(2):
        mine = (lane < HEAD) if head == 0 else (lane >= HEAD)
        rows = pl.ds(HEAD * head, HEAD)
        query_side = jnp.concatenate([jnp.where(mine, query_pair, zeros), extra[...]], axis=1)
        key_side = jnp.concatenate(
            [keys[...], keys_extra[:, 128 * head : 128 * head + 128]], axis=1
        )
        attention = jnp.exp(dot(query_side, key_side, 1, 1) - columns[:, head : head + 1])
        score_grad = attention * (
            dot(jnp.where(mine, grad_pair, zeros), values_t[0], 1, 0)
            - columns[:, HEADS + head : HEADS + head + 1]
        )
        attention_low = attention.astype(low_type)
        score_low = score_grad.astype(low_type)
        sums = [
            jnp.sum(score_grad[BLK * block : BLK * block + BLK], axis=0, keepdims=True)
            for block in range(count // BLK)
        ]
        spare = folded.shape[1] - len(sums)
        folded[head] = jnp.concatenate(sums + [jnp.zeros((spare, count), f32)] * (spare > 0), axis=0)
        query_grads.append(dot(score_low, keys[...], 1, 0))
        value_grad_t[rows, :] = dot(context_grad_t[rows, :], attention_low, 1, 0).astype(low_type)
        key_grad_t[rows, :] = dot(queries_t[rows, :], score_low, 1, 0).astype(low_type)
    query_grad[:, lanes] += jnp.where(lane < HEAD, query_grads[0], query_grads[1])

    if remote:
        parts[pl.ds(pl.multiple_of(PAIR * pair, PAIR), PAIR), :] = key_grad_t[...]
        parts[pl.ds(pl.multiple_of(D + PAIR * pair, PAIR), PAIR), :] = value_grad_t[...]
        for number in range(4):

            @pl.when(now == number * PAIRS + PAIRS - 1)
            def _(number=number):
                part = dot(key_weight[...], parts[:D], 1, 0) + dot(value_weight[...], parts[D:], 1, 0)
                relay.turn(number, part, total)


def attend_back(
    queries,
    extra,
    row_columns,
    context_grad,
    queries_t,
    context_grad_t,
    keys,
    values_t,
    keys_extra,
    weights,
    terms,
):
    count, row_length = queries.shape[0], keys.shape[0]
    fold_rows = -(-(count // BLK) // 8) * 8
    terms = [by_chip(term) for term in terms]
    anywhere = pl.BlockSpec(memory_space=pl.ANY)
    of_pair = pl.BlockSpec((count, PAIR), lambda turn, pair: (0, pair))
    of_pair_t = pl.BlockSpec((PAIR, count), lambda turn, pair: (pair, 0))
    key_t = pl.BlockSpec((PAIR, count), lambda turn, pair: (pair, turn))
    still = lambda *shape: pl.BlockSpec(shape, lambda turn, pair: (0,) * len(shape))
    remote, more_specs, more_shapes, more_out, scratch, more = {}, [], [], [], [], []
    if terms:
        remote = {"collective_id": 1, "has_side_effects": True}
        more = [weights, weights, *terms]
        columns = [pl.BlockSpec((D, D), lambda turn, pair, k=k: (0, k)) for k in (1, 2)]
        more_specs = columns + [anywhere] * 3
        more_shapes = [jax.ShapeDtypeStruct((D, count), f32)] + [
            jax.ShapeDtypeStruct((4, terms[which].shape[3], width // 2), low_type)
            for which, _, width, _ in BACK_PLANS
        ]
        more_out = [still(D, count)] + [anywhere] * len(BACK_PLANS)
        scratch = [
            pltpu.VMEM((2 * D, count), low_type),
            pltpu.VMEM((3, D, count), low_type),
            pltpu.VMEM((5, D, count), low_type),
            pltpu.SemaphoreType.DMA((2, 12)),
        ]
        for which, _, width, _ in BACK_PLANS:
            scratch += plane_scratch(terms[which].shape[3], width)
    return pl.pallas_call(
        backward_kernel,
        grid=(row_length // count, PAIRS),
        out_shape=[
            jax.ShapeDtypeStruct((count, D), f32),
            jax.ShapeDtypeStruct((D, row_length), low_type),
            jax.ShapeDtypeStruct((D, row_length), low_type),
            jax.ShapeDtypeStruct((HEADS, fold_rows, row_length), f32),
        ]
        + more_shapes,
        in_specs=[
            of_pair,
            still(count, 128),
            still(count, 128),
            of_pair,
            of_pair_t,
            of_pair_t,
            pl.BlockSpec((count, PAIR), lambda turn, pair: (turn, pair)),
            pl.BlockSpec((1, PAIR, count), lambda turn, pair: (turn, pair, 0)),
            pl.BlockSpec((count, 256), lambda turn, pair: (turn, pair)),
        ]
        + more_specs,
        out_specs=[
            still(count, D),
            key_t,
            key_t,
            pl.BlockSpec((2, fold_rows, count), lambda turn, pair: (pair, 0, turn)),
        ]
        + more_out,
        scratch_shapes=scratch,
        compiler_params=pltpu.CompilerParams(vmem_limit_bytes=back_vmem, **remote),
        cost_estimate=pl.CostEstimate(
            flops=10 * HEADS * count * row_length * 200,
            bytes_accessed=HEADS * row_length * 2048,
            transcendentals=HEADS * count * row_length,
        ),
        name="attention_backward",
    )(
        *in_hbm(
            queries,
            extra,
            row_columns,
            context_grad,
            queries_t,
            context_grad_t,
            keys,
            values_t,
            keys_extra,
            *more,
        )
    )


def body(
    hidden_states,
    output_cotangent,
    document_lengths,
    bucket_index,
    norm_gains,
    bias_table,
    project_weight,
    output_weight,
    expand_weight,
    reduce_weight,
    project_rows,
    project_columns,
    output_rows,
    output_columns,
    expand_rows,
    expand_columns,
    reduce_rows,
    reduce_columns,
    gains_moment,
    table_moment,
):
    every = ("seq", "dp")
    local_rows = hidden_states.shape[1]
    row_length = local_rows * lax.axis_size("seq")
    gradient_scale = 1.0 / math.sqrt(row_length * lax.axis_size("dp"))
    place = lax.axis_index("seq")
    blocks = local_rows // BLK

    shards = (project_weight, output_weight, expand_weight, reduce_weight)
    direct = (
        lax.axis_size("seq") == 4
        and lax.axis_size("dp") == 8
        and all(shard.shape[0] % 8 == 0 and shard.shape[1] % 256 == 0 for shard in shards)
    )
    inputs = hidden_states[0].astype(f32)
    if direct:
        opened = open_layer(
            shards, hidden_states[0], norm_gains, bucket_index, bias_table, document_lengths
        )
        project_full, output_full, expand_full, reduce_full = (
            whole.reshape(-1, whole.shape[4]) for whole in opened[:4]
        )
        normed_all, keys = (blocks_of.reshape(row_length, D) for blocks_of in opened[4:6])
        values_t, keys_extra, picks, queries, queries_t, context_t, log_total, extra = opened[6:]
        normed_low = normed_all[row_length - local_rows :]
    else:
        project_full, output_full, expand_full, reduce_full = (
            lax.all_gather(shard.astype(low_type), every, axis=0, tiled=True) for shard in shards
        )
        row_states = lax.all_gather(hidden_states[0], "seq", axis=0, tiled=True)
        normed_low = rms_norm(inputs, norm_gains[0]).astype(low_type)
        normed_all = rms_norm(row_states.astype(f32), norm_gains[0]).astype(low_type)
        doc_all = documents(document_lengths[0], row_length)
        doc_query = lax.dynamic_slice_in_dim(doc_all, place * local_rows, local_rows)
        picks = key_picks(bucket_index[0], doc_all, bias_table.shape[0])
        one_hot = picks[:, : blocks * bias_table.shape[0]]
        keys_extra = key_extra(picks, bias_table, blocks)
        extra = query_extra(doc_query, blocks)
        scaled = lambda values: (values.astype(low_type).astype(f32) * score_scale).astype(low_type)
        queries = scaled(dot(normed_low, project_full[:, :D], 1, 0))
        queries_t = scaled(dot(project_full[:, :D], normed_low, 0, 1))
        keys = dot(normed_all, project_full[:, D : 2 * D], 1, 0).astype(low_type)
        values_t = dot(project_full[:, 2 * D :], normed_all, 0, 1).astype(low_type)
        context_t, log_total = attend(queries, extra, keys, values_t, keys_extra)
        log_total = log_total.reshape(HEADS, 8, local_rows)[:, 0]
        values_t = jnp.transpose(values_t.reshape(D, -1, local_rows), (1, 0, 2))
    _, pullback_one = jax.vjp(rms_norm, inputs, norm_gains[0])
    query_weight, key_weight, value_weight = (
        project_full[:, :D],
        project_full[:, D : 2 * D],
        project_full[:, 2 * D :],
    )
    (
        layer_output,
        residual_grad,
        output_term,
        expand_term,
        reduce_term,
        context_grad,
        context_grad_t,
        row_columns,
        gain_two_grad,
    ) = middle(
        context_t,
        log_total,
        hidden_states[0],
        output_cotangent[0],
        norm_gains,
        output_full,
        expand_full,
        reduce_full,
    )
    layer_output = layer_output[None]
    query_grad, key_grad_t, value_grad_t, folded, *summed_back = attend_back(
        queries,
        extra,
        row_columns,
        context_grad,
        queries_t,
        context_grad_t,
        keys,
        values_t,
        keys_extra,
        project_full,
        [output_term, expand_term, reduce_term] if direct else [],
    )
    if direct:
        rows_before = [project_rows, output_rows, expand_rows, reduce_rows]
        input_gradient, *results = close(
            gradient_scale,
            (
                normed_all.reshape(4, local_rows, D),
                key_grad_t,
                value_grad_t,
                query_grad,
                project_full,
                summed_back[0],
            ),
            (
                hidden_states[0],
                residual_grad,
                folded,
                picks,
                norm_gains,
                gain_two_grad,
            ),
            summed_back[1:],
            rows_before,
            [shard.shape for shard in shards],
        )
        results = apply_updates(
            gradient_scale,
            results[:4],
            results[4:6],
            shards,
            rows_before,
            [project_columns, output_columns, expand_columns, reduce_columns],
            (norm_gains, gains_moment, bias_table.T, table_moment.T),
        )
        gradients, updated_weights, row_after, columns_after = (
            results[:4],
            results[4:8],
            results[8:12],
            results[12:16],
        )
        gains_gradient, gains_updated, gains_moment_new = results[16:19]
        table_gradient, table_updated, table_moment_new = (table.T for table in results[19:])
        return (
            layer_output,
            input_gradient[None],
            gains_gradient,
            table_gradient,
            *gradients,
            gains_updated,
            table_updated,
            *updated_weights,
            row_after[0],
            columns_after[0],
            row_after[1],
            columns_after[1],
            row_after[2],
            columns_after[2],
            row_after[3],
            columns_after[3],
            gains_moment_new,
            table_moment_new,
        )

    buckets = bias_table.shape[0]
    picked = jnp.dot(
        folded[:, :blocks].reshape(HEADS * blocks, row_length),
        one_hot.astype(f32),
        precision=lax.Precision.HIGHEST,
    )
    table_grad = jnp.einsum("hkkb->bh", picked.reshape(HEADS, blocks, blocks, buckets))

    query_grad_low = (query_grad * score_scale).astype(low_type)
    project_terms = [
        dot(normed_low, query_grad_low, 0, 0),
        dot(normed_all, key_grad_t, 0, 1),
        dot(normed_all, value_grad_t, 0, 1),
    ]
    key_part = dot(key_grad_t, key_weight, 0, 1) + dot(value_grad_t, value_weight, 0, 1)
    key_part = lax.psum_scatter(
        key_part.astype(low_type), "seq", scatter_dimension=0, tiled=True
    ).astype(f32)
    input_part, gain_one_grad = pullback_one(dot(query_grad_low, query_weight, 1, 1) + key_part)
    input_gradient = (residual_grad + input_part).astype(low_type)[None]
    terms = [
        term.astype(low_type)
        for term in (jnp.concatenate(project_terms, axis=1), output_term, expand_term, reduce_term)
    ]
    shares = [
        lax.psum_scatter(term, every, scatter_dimension=0, tiled=True).astype(f32)
        for term in terms
    ]
    gradients = tuple((share * gradient_scale for share in shares))
    row_before = (project_rows, output_rows, expand_rows, reduce_rows)
    row_after = []
    column_parts = []
    row_sums = []
    for gradient, previous in zip(gradients, row_before):
        squares = gradient * gradient + tiny_term
        updated_rows = decay_rate * previous + (1.0 - decay_rate) * jnp.mean(squares, axis=1)
        row_after.append(updated_rows)
        column_parts.append(jnp.sum(squares, axis=0))
        row_sums.append(jnp.sum(updated_rows))
    summed = lax.psum(
        (
            column_parts[0],
            column_parts[1],
            column_parts[2],
            column_parts[3],
            jnp.stack(row_sums),
            jnp.stack([gain_one_grad, gain_two_grad[0]]),
            table_grad,
        ),
        every,
    )
    column_before = (project_columns, output_columns, expand_columns, reduce_columns)
    weights_before = (project_weight, output_weight, expand_weight, reduce_weight)
    full_rows = (
        project_full.shape[0],
        output_full.shape[0],
        expand_full.shape[0],
        reduce_full.shape[0],
    )
    updated_weights = []
    columns_after = []
    for position in range(4):
        columns_new = decay_rate * column_before[position] + (1.0 - decay_rate) * (
            summed[position] / full_rows[position]
        )
        row_mean = summed[4][position] / full_rows[position]
        denominator = row_after[position][:, None] * columns_new[None, :] / row_mean
        updated_weights.append(
            weights_before[position] - learn_rate * gradients[position] * lax.rsqrt(denominator)
        )
        columns_after.append(columns_new)
    gains_gradient = summed[5] * gradient_scale
    table_gradient = summed[6] * gradient_scale
    gains_moment_new = decay_rate * gains_moment + (1.0 - decay_rate) * (
        gains_gradient * gains_gradient + tiny_term
    )
    gains_updated = norm_gains - learn_rate * gains_gradient * lax.rsqrt(gains_moment_new)
    table_moment_new = decay_rate * table_moment + (1.0 - decay_rate) * (
        table_gradient * table_gradient + tiny_term
    )
    table_updated = bias_table - learn_rate * table_gradient * lax.rsqrt(table_moment_new)
    return (
        layer_output,
        input_gradient,
        gains_gradient,
        table_gradient,
        gradients[0],
        gradients[1],
        gradients[2],
        gradients[3],
        gains_updated,
        table_updated,
        updated_weights[0],
        updated_weights[1],
        updated_weights[2],
        updated_weights[3],
        row_after[0],
        columns_after[0],
        row_after[1],
        columns_after[1],
        row_after[2],
        columns_after[2],
        row_after[3],
        columns_after[3],
        gains_moment_new,
        table_moment_new,
    )


def solution(mesh):
    placed = (
        P("dp", "seq", None),
        P("dp", "seq", None),
        P("dp", None),
        P("dp", "seq", None),
        P(),
        P(),
        P(("seq", "dp"), None),
        P(("seq", "dp"), None),
        P(("seq", "dp"), None),
        P(("seq", "dp"), None),
        P(("seq", "dp")),
        P(),
        P(("seq", "dp")),
        P(),
        P(("seq", "dp")),
        P(),
        P(("seq", "dp")),
        P(),
        P(),
        P(),
    )
    return jax.shard_map(
        body,
        mesh=mesh,
        in_specs=placed,
        out_specs=(
            P("dp", "seq", None),
            P("dp", "seq", None),
            P(),
            P(),
            P(("seq", "dp"), None),
            P(("seq", "dp"), None),
            P(("seq", "dp"), None),
            P(("seq", "dp"), None),
            P(),
            P(),
            P(("seq", "dp"), None),
            P(("seq", "dp"), None),
            P(("seq", "dp"), None),
            P(("seq", "dp"), None),
            P(("seq", "dp")),
            P(),
            P(("seq", "dp")),
            P(),
            P(("seq", "dp")),
            P(),
            P(("seq", "dp")),
            P(),
            P(),
            P(),
        ),
        check_vma=False,
    )
```
